32 devices in a mesh: clip: 4 (over x, core), tm: 8 (over z, y).
Axes of the slice: x: 2, y: 2, z: 4, core: 2. Of those that a mesh axis runs over, the one named last changes fastest.
Arguments:
- clips: bfloat16 [16, 8, 128, 1024], P('clip', 'tm'), may hold values from -6 to 6
- w_qkv: bfloat16 [1024, 3072], replicated, may hold values from -8 to 8
- w_out: bfloat16 [1024, 1024], replicated, may hold values from -0.1875 to 0.1875
- cotangent: bfloat16 [16, 8, 128, 1024], P('clip', 'tm'), may hold values from -6 to 6
Outputs:
- grad_clips: bfloat16 [16, 8, 128, 1024], P('clip', 'tm')
- grad_qkv: float32 [1024, 3072], P(('clip', 'tm'))
- grad_out: float32 [1024, 1024], P(('clip', 'tm'))
The draws below stay inside these ranges and needn't reach their ends.
All inputs are finite; a program needn't handle non-finite values.
Results may differ from the reference program's by a relative error of at most 0.0093.
Values may be sent and summed in bfloat16 or wider, within the bound.
No kernel may reach another device: no remote copies, remote signals or barrier semaphores. Data moves between devices by JAX's collectives and lax.ppermute only.
A program may use at most 128 MiB of HBM per device.

```python
import jax
import jax.numpy as jnp
from jax import lax

D = 1024
HEADS = 16
PATCH = 128
CLIPS = 16
FRAMES = 8


def draw_w_qkv(key, part):
    key = jax.random.fold_in(key, 11)
    first = jax.random.fold_in(key, 0)
    base = jax.random.normal(first, (D, 3 * D), jnp.float32) * D ** (-0.5)
    return jnp.clip(base, -8.0, 8.0).astype(jnp.bfloat16)


def strengthened(values, stream_key, source, target, parts, factor):
    def block_of(dim):
        return (jnp.arange(values.shape[dim]) // (values.shape[dim] // parts)).reshape((-1,) + (1,) * (values.ndim - 1 - dim))

    first = jax.random.permutation(stream_key, parts)[block_of(target)]
    other_side = (block_of(target) + parts // 2) % parts
    return jnp.where((block_of(source) == first) | (block_of(source) == other_side), factor * values, values)


def block_scale(rng, dims, shards, smallest, largest):
    def one(position, blocks):
        draws = jax.random.uniform(jax.random.fold_in(jax.random.fold_in(rng, 6), position), (blocks,), jnp.float32, smallest / len(shards), largest / len(shards))
        return jnp.repeat(jnp.exp(draws), dims[position] // blocks).reshape((-1,) + (1,) * (len(dims) - position - 1))

    loudness = one(*shards[0])
    for cut in shards[1:]:
        loudness = loudness * one(*cut)
    return loudness


def gaussian(stream_key, extent, deviation, limit, cuts=(), dtype=jnp.bfloat16):
    entries = deviation * jax.random.normal(stream_key, extent, jnp.float32)
    if cuts:
        entries = entries * block_scale(stream_key, extent, cuts, -0.22, 0.18)
    return jnp.clip(entries, -limit, limit).astype(dtype)


def heavy_noise(rng, shape, deviation, limit, cuts, heavy, kind=jnp.bfloat16):
    values = deviation * jax.random.normal(rng, shape, jnp.float32)
    if cuts:
        values = values * block_scale(rng, shape, cuts, -0.22, 0.18)
    return jnp.clip(strengthened(values, jax.random.fold_in(rng, 3), *heavy), -limit, limit).astype(kind)


def setup_inputs(seed: int = 0) -> dict:
    key_of = jax.random.split(jax.random.key(seed), 5)
    clips = heavy_noise(key_of[0], (CLIPS, FRAMES, PATCH, D), 1.0, 6.0, ((0, 4), (1, 8)), (1, 3, 8, 2.0))
    w_qkv = draw_w_qkv(jax.random.fold_in(key_of[4], 71), 0)
    w_out = gaussian(key_of[2], (D, D), D ** -0.5, 0.1875)
    cotangent = gaussian(key_of[3], (CLIPS, FRAMES, PATCH, D), 1.0, 6.0, ((0, 4), (1, 8)))
    return dict(clips=clips, w_qkv=w_qkv, w_out=w_out, cotangent=cotangent)


epsilon = 1e-06

def normalize(clips):
    values32 = clips.astype(jnp.float32)
    centred = values32 - lax.optimization_barrier(jnp.mean(values32, axis=-1, keepdims=True))
    inverse = lax.rsqrt(lax.optimization_barrier(jnp.mean(centred * centred, axis=-1, keepdims=True)) + epsilon)
    return (centred * inverse, inverse)

def split_heads(array):
    return array.reshape(array.shape[:-1] + (HEADS, array.shape[-1] // HEADS))

def unpack(packed):
    width = packed.shape[-1] // 3
    queries = split_heads(packed[..., :width]).astype(jnp.float32)
    key_rows = split_heads(packed[..., width:2 * width]).astype(jnp.float32)
    value_rows = split_heads(packed[..., 2 * width:]).astype(jnp.float32)
    return (queries, key_rows, value_rows, width)

def attend(packed):
    queries, key_rows, value_rows, width = unpack(packed)
    scaling = (width // HEADS) ** (-0.5)
    scores = jnp.einsum('cfphd,cgphd->cphfg', queries, key_rows) * scaling
    highest = lax.optimization_barrier(jnp.max(scores, axis=-1, keepdims=True))
    expo = jnp.exp(scores - highest)
    full_weights = expo / lax.optimization_barrier(jnp.sum(expo, axis=-1, keepdims=True))
    low_weights = full_weights.astype(jnp.bfloat16)
    mixed = jnp.einsum('cphfg,cgphd->cfphd', low_weights.astype(jnp.float32), value_rows)
    mixed = mixed.astype(jnp.bfloat16).reshape(packed.shape[:3] + (width,))
    return (mixed, full_weights, low_weights)

def attend_back(packed, full_weights, low_weights, mixed_grad):
    queries, key_rows, value_rows, width = unpack(packed)
    scaling = (width // HEADS) ** (-0.5)
    grad_heads = split_heads(mixed_grad).astype(jnp.float32)
    dots = jnp.einsum('cfphd,cgphd->cphfg', grad_heads, value_rows)
    score_grad = full_weights * (dots - lax.optimization_barrier(jnp.sum(full_weights * dots, axis=-1, keepdims=True)))
    score_grad = (score_grad * scaling).astype(jnp.bfloat16).astype(jnp.float32)
    query_grad = jnp.einsum('cphfg,cgphd->cfphd', score_grad, key_rows).astype(jnp.bfloat16)
    key_grad = jnp.einsum('cphfg,cfphd->cgphd', score_grad, queries).astype(jnp.bfloat16)
    value_grad = jnp.einsum('cphfg,cfphd->cgphd', low_weights.astype(jnp.float32), grad_heads).astype(jnp.bfloat16)
    lead = packed.shape[:3] + (width,)
    return jnp.concatenate([query_grad.reshape(lead), key_grad.reshape(lead), value_grad.reshape(lead)], axis=-1)

def reference(clips, w_qkv, w_out, cotangent):
    unit_rows, inverse = normalize(clips)
    normed = unit_rows.astype(jnp.bfloat16)
    flat_normed = normed.reshape(-1, D)
    packed = jnp.dot(flat_normed, w_qkv, preferred_element_type=jnp.float32).astype(jnp.bfloat16)
    packed = packed.reshape(clips.shape[:3] + (3 * D,))
    mixed, full_weights, low_weights = attend(packed)
    flat_cot = cotangent.reshape(-1, D)
    grad_out = jnp.dot(mixed.reshape(-1, D).T, flat_cot, preferred_element_type=jnp.float32)
    mixed_grad = jnp.dot(flat_cot, w_out.T, preferred_element_type=jnp.float32).astype(jnp.bfloat16)
    packed_grad = attend_back(packed, full_weights, low_weights, mixed_grad.reshape(mixed.shape))
    flat_grad = packed_grad.reshape(-1, 3 * D)
    grad_qkv = jnp.dot(flat_normed.T, flat_grad, preferred_element_type=jnp.float32)
    normed_grad = jnp.dot(flat_grad, w_qkv.T, preferred_element_type=jnp.float32).reshape(clips.shape)
    input_grad = inverse * (normed_grad - lax.optimization_barrier(jnp.mean(normed_grad, axis=-1, keepdims=True)) - unit_rows * lax.optimization_barrier(jnp.mean(normed_grad * unit_rows, axis=-1, keepdims=True)))
    grad_clips = (cotangent.astype(jnp.float32) + input_grad).astype(jnp.bfloat16)
    return (grad_clips, grad_qkv, grad_out)
```

```python
import functools

import jax
import jax.numpy as jnp
from jax import lax
from jax.experimental import pallas as pl
from jax.experimental.pallas import tpu as pltpu
from jax.sharding import PartitionSpec as P

HEADS = 16
GROUP = 4
CHUNKS = 2
EPSILON = 1e-06
LOWEST = -1e30
VMEM_LIMIT = 48 * 1024 * 1024


def contract(left, right, dims):
    return lax.dot_general(left, right, (dims, ((), ())), preferred_element_type=jnp.float32)


def statistics(rows32):
    mean = jnp.mean(rows32, axis=-1, keepdims=True)
    centred = rows32 - mean
    inverse = lax.rsqrt(jnp.mean(centred * centred, axis=-1, keepdims=True) + EPSILON)
    return centred * inverse, inverse


def pick_kernel(n_slots, n_chunks, me_ref, x_ref, cot_ref, *out_refs):
    depth = x_ref.shape[0] // n_chunks
    for chunk in range(n_chunks):
        here = pl.ds(chunk * depth, depth)
        for slot in range(n_slots):
            out = out_refs[chunk * n_slots + slot]
            block = me_ref[0] ^ slot
            out[0] = x_ref[here, block]
            out[1] = cot_ref[here, block]


def pick(me, clips, cotangent, n_slots, n_chunks):
    n_clips, _, n_patches, width = clips.shape
    cut = (n_clips, n_slots, n_patches // n_slots, width)
    piece = jax.ShapeDtypeStruct((2, n_clips // n_chunks) + cut[2:], clips.dtype)
    out = pl.pallas_call(
        functools.partial(pick_kernel, n_slots, n_chunks),
        out_shape=[piece] * (n_slots * n_chunks),
        in_specs=[
            pl.BlockSpec(memory_space=pltpu.SMEM),
            pl.BlockSpec(memory_space=pltpu.VMEM),
            pl.BlockSpec(memory_space=pltpu.VMEM),
        ],
        out_specs=[pl.BlockSpec(memory_space=pltpu.VMEM)] * (n_slots * n_chunks),
        compiler_params=pltpu.CompilerParams(vmem_limit_bytes=VMEM_LIMIT),
    )(me, clips.reshape(cut), cotangent.reshape(cut))
    return [out[chunk * n_slots : (chunk + 1) * n_slots] for chunk in range(n_chunks)]


def place_kernel(n_slots, me_ref, *refs):
    out_ref = refs[n_slots]
    for slot in range(n_slots):
        out_ref[:, me_ref[0] ^ slot] = refs[slot][...]


def place(me, blocks):
    n_slots = len(blocks)
    n_clips, n_positions, width = blocks[0].shape
    return pl.pallas_call(
        functools.partial(place_kernel, n_slots),
        out_shape=jax.ShapeDtypeStruct((n_clips, n_slots, n_positions, width), blocks[0].dtype),
        in_specs=[pl.BlockSpec(memory_space=pltpu.SMEM)]
        + [pl.BlockSpec(memory_space=pltpu.VMEM)] * n_slots,
        out_specs=pl.BlockSpec(memory_space=pltpu.VMEM),
        compiler_params=pltpu.CompilerParams(vmem_limit_bytes=VMEM_LIMIT),
    )(me, *blocks)


def sublayer_kernel(n_clips, n_positions, n_pieces, n_aliased, *refs):
    pieces, refs = refs[:n_pieces], refs[n_pieces:]
    wq_ref, wk_ref, wv_ref, wo_ref = refs[:4]
    refs = refs[4 + n_aliased :]
    normed_ref, cot_ref, mixed_ref, grads_ref = refs[:4]
    dx_refs, total_ref = refs[4:-1], refs[-1]
    step = pl.program_id(0)
    rows = normed_ref.shape[0] // n_clips
    span = rows // n_pieces
    wide = wo_ref.shape[0]
    depth = wide // GROUP
    scaling = depth**-0.5

    def raw_rows():
        return jnp.concatenate(
            [pieces[k][0, clip] for clip in range(n_clips) for k in range(n_pieces)], axis=0
        ).astype(jnp.float32)

    @pl.when(step == 0)
    def _():
        unit, _ = statistics(raw_rows())
        normed_ref[...] = unit.astype(jnp.bfloat16)
        for clip in range(n_clips):
            for k in range(n_pieces):
                cot_ref[pl.ds(clip * rows + k * span, span)] = pieces[k][1, clip]

    normed = normed_ref[...]
    all_queries = contract(normed, wq_ref[...], ((1,), (0,))).astype(jnp.bfloat16)
    all_keys = contract(normed, wk_ref[...], ((1,), (0,))).astype(jnp.bfloat16)
    all_values = contract(normed, wv_ref[...], ((1,), (0,))).astype(jnp.bfloat16)
    mixed_grad = contract(cot_ref[...], wo_ref[...], ((1,), (1,))).astype(jnp.bfloat16)

    lane_head = lax.broadcasted_iota(jnp.int32, (rows, wide), 1) // depth
    head_masks = [(lane_head == h).astype(jnp.float32).astype(jnp.bfloat16) for h in range(GROUP)]
    key_pos = lax.broadcasted_iota(jnp.int32, (rows, rows), 0) % n_positions
    query_pos = lax.broadcasted_iota(jnp.int32, (rows, rows), 1) % n_positions
    same = (key_pos == query_pos)[None]

    def stacked(block):
        return jnp.concatenate([block * mask for mask in head_masks], axis=0)

    def side_by_side(blocks):
        return jnp.concatenate([blocks[h] for h in range(GROUP)], axis=1)

    for clip in range(n_clips):
        here = slice(clip * rows, (clip + 1) * rows)
        queries = all_queries[here]
        keys = stacked(all_keys[here])
        values = stacked(all_values[here])
        upstream = mixed_grad[here]
        scores = contract(keys, queries, ((1,), (1,))).reshape(GROUP, rows, rows)
        scores = jnp.where(same, scores * scaling, LOWEST)
        expo = jnp.exp(scores - jnp.max(scores, axis=1, keepdims=True))
        full = expo * (1.0 / jnp.sum(expo, axis=1, keepdims=True))
        low = full.astype(jnp.bfloat16)
        dots = contract(values, upstream, ((1,), (1,))).reshape(GROUP, rows, rows)
        score_grad = full * (dots - jnp.sum(full * dots, axis=1, keepdims=True))
        score_grad = (score_grad * scaling).astype(jnp.bfloat16)
        mixed = contract(low.reshape(GROUP * rows, rows), values, ((0,), (0,)))
        mixed_ref[here] = mixed.astype(jnp.bfloat16)
        dq = contract(score_grad.reshape(GROUP * rows, rows), keys, ((0,), (0,)))
        grads_ref[here, :wide] = dq.astype(jnp.bfloat16)
        dk = contract(side_by_side(score_grad), stacked(queries), ((1,), (0,)))
        grads_ref[here, wide : 2 * wide] = dk.astype(jnp.bfloat16)
        dv = contract(side_by_side(low), stacked(upstream), ((1,), (0,)))
        grads_ref[here, 2 * wide :] = dv.astype(jnp.bfloat16)

    part = contract(grads_ref[:, :wide], wq_ref[...], ((1,), (1,)))
    part += contract(grads_ref[:, wide : 2 * wide], wk_ref[...], ((1,), (1,)))
    part += contract(grads_ref[:, 2 * wide :], wv_ref[...], ((1,), (1,)))

    @pl.when(step == 0)
    def _():
        total_ref[...] = part

    @pl.when(step > 0)
    def _():
        total_ref[...] += part

    @pl.when(step == pl.num_programs(0) - 1)
    def _():
        unit, inverse = statistics(raw_rows())
        total = total_ref[...]
        grad = inverse * (
            total
            - jnp.mean(total, axis=-1, keepdims=True)
            - unit * jnp.mean(total * unit, axis=-1, keepdims=True)
        )
        dx = (cot_ref[...].astype(jnp.float32) + grad).astype(jnp.bfloat16)
        for clip in range(n_clips):
            for k in range(n_pieces):
                start = clip * rows + k * span
                dx_refs[k][clip] = dx[start : start + span]


def sublayer(pieces, w_qkv, w_out, chunk, n_chunks, n_positions, before):
    n_pieces = len(pieces)
    _, n_clips, span, width = pieces[0].shape
    rows = n_clips * n_pieces * span
    groups = HEADS // GROUP
    wide = width // groups

    def whole(shape):
        return pl.BlockSpec(shape, lambda j: (0,) * len(shape))

    flat = jax.ShapeDtypeStruct((n_chunks * rows, width), jnp.bfloat16)
    grads = jax.ShapeDtypeStruct((n_chunks * rows, 3 * width), jnp.bfloat16)
    dx = jax.ShapeDtypeStruct((n_chunks * n_clips, span, width), jnp.bfloat16)
    out_shape = [flat, flat, flat, grads] + [dx] * n_pieces
    aliased = [] if before is None else list(before)
    first = n_pieces + 4
    return pl.pallas_call(
        functools.partial(sublayer_kernel, n_clips, n_positions, n_pieces, len(aliased)),
        grid=(groups,),
        out_shape=out_shape,
        in_specs=[whole(piece.shape) for piece in pieces]
        + [pl.BlockSpec((width, wide), lambda j, i=i: (0, i * groups + j)) for i in range(3)]
        + [pl.BlockSpec((wide, width), lambda j: (j, 0))]
        + [pl.BlockSpec(memory_space=pl.ANY)] * len(aliased),
        out_specs=[
            pl.BlockSpec((rows, width), lambda j: (chunk, 0)),
            pl.BlockSpec((rows, width), lambda j: (chunk, 0)),
            pl.BlockSpec((rows, wide), lambda j: (chunk, j)),
            pl.BlockSpec((rows, 3 * wide), lambda j: (chunk, j)),
        ]
        + [pl.BlockSpec((n_clips, span, width), lambda j: (chunk, 0, 0))] * n_pieces,
        scratch_shapes=[pltpu.VMEM((rows, width), jnp.float32)],
        input_output_aliases={first + i: i for i in range(len(aliased))},
        compiler_params=pltpu.CompilerParams(vmem_limit_bytes=VMEM_LIMIT),
        cost_estimate=pl.CostEstimate(
            flops=2 * rows * width * (7 * width + 24 * 128),
            bytes_accessed=16 * rows * width + 8 * width * width,
            transcendentals=rows * 128 * HEADS,
        ),
    )(*pieces, w_qkv, w_qkv, w_qkv, w_out, *aliased)


def swap(block, axis, size, distance):
    return lax.ppermute(block, axis, [(i, i ^ distance) for i in range(size)])


def scatter_sum(parts, axis, size, stride, count):
    me = lax.axis_index(axis) // stride % count
    total = lax.dynamic_index_in_dim(parts, me, 0, keepdims=False).astype(jnp.float32)
    for j in range(1, count):
        block = lax.dynamic_index_in_dim(parts, me ^ j, 0, keepdims=False)
        total += swap(block.astype(jnp.bfloat16), axis, size, j * stride).astype(jnp.float32)
    return total


def shards(n_clip_devices, n_tm, clips, w_qkv, w_out, cotangent):
    n_clips, _, n_patches, width = clips.shape
    n_positions = n_patches // n_tm
    me = lax.axis_index("tm").reshape(1)

    chunks = pick(me, clips, cotangent, n_tm, CHUNKS)
    joined = n_positions % 16 != 0
    results = None
    for chunk, blocks in enumerate(chunks):
        pieces = [blocks[0]] + [swap(blocks[k], "tm", n_tm, k) for k in range(1, n_tm)]
        if joined:
            pieces = [jnp.stack(pieces, axis=2).reshape(2, n_clips // CHUNKS, -1, width)]
        results = sublayer(pieces, w_qkv, w_out, chunk, CHUNKS, n_positions, results)
    normed, cot, mixed, grads = results[:4]
    dx = list(results[4:])
    if joined:
        cut = dx[0].reshape(n_clips, n_tm, n_positions, width)
        dx = [cut[:, k] for k in range(n_tm)]
    dx = [dx[0]] + [swap(dx[k], "tm", n_tm, k) for k in range(1, n_tm)]
    grad_clips = place(me, dx).reshape(clips.shape)

    cores = 2
    n_x = n_clip_devices // cores
    n_y = 2
    n_z = n_tm // n_y
    core = lax.axis_index("clip") % cores
    rest = width // (n_x * cores)

    def chosen(rows, which):
        cut = rows.reshape(rows.shape[0], n_x, cores, rest)
        return lax.dynamic_index_in_dim(cut, which, 2, keepdims=False).reshape(rows.shape[0], -1)

    half = 2 * width

    def first_half(which):
        left = chosen(normed, which)
        return contract(left, grads[:, :half], ((0,), (0,))).astype(jnp.bfloat16)

    def second_half(which):
        left = contract(chosen(normed, which), grads[:, half:], ((0,), (0,)))
        right = contract(chosen(mixed, which), cot, ((0,), (0,)))
        return jnp.concatenate([left, right], axis=1).astype(jnp.bfloat16)

    sums = []
    for product in (first_half, second_half):
        other = swap(product(1 - core), "clip", n_clip_devices, 1)
        total = product(core).astype(jnp.float32) + other.astype(jnp.float32)
        sums.append(total.reshape(n_x, n_z, n_y, -1, half))
    first, second = sums
    first = scatter_sum(first, "clip", n_clip_devices, cores, n_x)
    second = scatter_sum(second.transpose(2, 0, 1, 3, 4), "tm", n_tm, 1, n_y)
    first = scatter_sum(first.transpose(1, 0, 2, 3), "tm", n_tm, 1, n_y)
    second = scatter_sum(second, "clip", n_clip_devices, cores, n_x)
    first = scatter_sum(first, "tm", n_tm, n_y, n_z)
    second = scatter_sum(second, "tm", n_tm, n_y, n_z)

    groups = HEADS // GROUP
    grad_qkv = jnp.concatenate([first, second[:, :width]], axis=1)
    grad_qkv = grad_qkv.reshape(-1, groups, 3, width // groups).transpose(0, 2, 1, 3)
    return (grad_clips, grad_qkv.reshape(-1, 3 * width), second[:, width:])


def solution(mesh):
    return jax.shard_map(
        functools.partial(shards, mesh.shape["clip"], mesh.shape["tm"]),
        mesh=mesh,
        in_specs=(P("clip", "tm", None, None), P(), P(), P("clip", "tm", None, None)),
        out_specs=(P("clip", "tm", None, None), P(("clip", "tm"), None), P(("clip", "tm"), None)),
        check_vma=False,
    )
```

```python
import functools

import jax
import jax.numpy as jnp
from jax import lax
from jax.experimental import pallas as pl
from jax.experimental.pallas import tpu as pltpu
from jax.sharding import PartitionSpec as P

HEADS = 16
GROUP = 4
CHUNKS = 2
EPSILON = 1e-06
LOWEST = -1e30
MIB = 1024 * 1024


def contract(left, right, dims):
    return lax.dot_general(left, right, (dims, ((), ())), preferred_element_type=jnp.float32)


def statistics(rows32):
    mean = jnp.mean(rows32, axis=-1, keepdims=True)
    centred = rows32 - mean
    inverse = lax.rsqrt(jnp.mean(centred * centred, axis=-1, keepdims=True) + EPSILON)
    return centred * inverse, inverse


def pick_kernel(n_slots, n_chunks, me_ref, x_ref, cot_ref, *out_refs):
    depth = x_ref.shape[0] // n_chunks
    for chunk in range(n_chunks):
        here = pl.ds(chunk * depth, depth)
        for slot in range(n_slots):
            out = out_refs[chunk * n_slots + slot]
            block = me_ref[0] ^ slot
            out[0] = x_ref[here, block]
            out[1] = cot_ref[here, block]


def pick(me, clips, cotangent, n_slots, n_chunks):
    n_clips, _, n_patches, width = clips.shape
    cut = (n_clips, n_slots, n_patches // n_slots, width)
    piece = jax.ShapeDtypeStruct((2, n_clips // n_chunks) + cut[2:], clips.dtype)
    out = pl.pallas_call(
        functools.partial(pick_kernel, n_slots, n_chunks),
        out_shape=[piece] * (n_slots * n_chunks),
        in_specs=[
            pl.BlockSpec(memory_space=pltpu.SMEM),
            pl.BlockSpec(memory_space=pltpu.VMEM),
            pl.BlockSpec(memory_space=pltpu.VMEM),
        ],
        out_specs=[pl.BlockSpec(memory_space=pltpu.VMEM)] * (n_slots * n_chunks),
        compiler_params=pltpu.CompilerParams(vmem_limit_bytes=16 * MIB),
    )(me, clips.reshape(cut), cotangent.reshape(cut))
    return [out[chunk * n_slots : (chunk + 1) * n_slots] for chunk in range(n_chunks)]


def place_kernel(n_slots, me_ref, *refs):
    out_ref = refs[-1]
    for i, ref in enumerate(refs[:-1]):
        depth = ref.shape[0]
        here = pl.ds(i // n_slots * depth, depth)
        out_ref[here, me_ref[0] ^ (i % n_slots)] = ref[...]


def place(me, chunks):
    n_slots = len(chunks[0])
    n_clips, n_positions, width = chunks[0][0].shape
    blocks = [block for chunk in chunks for block in chunk]
    shape = (n_clips * len(chunks), n_slots, n_positions, width)
    return pl.pallas_call(
        functools.partial(place_kernel, n_slots),
        out_shape=jax.ShapeDtypeStruct(shape, blocks[0].dtype),
        in_specs=[pl.BlockSpec(memory_space=pltpu.SMEM)]
        + [pl.BlockSpec(memory_space=pltpu.VMEM)] * len(blocks),
        out_specs=pl.BlockSpec(memory_space=pltpu.VMEM),
        compiler_params=pltpu.CompilerParams(vmem_limit_bytes=16 * MIB),
    )(me, *blocks)


def product_kernel(n_x, which_ref, normed_ref, mixed_ref, dq_ref, dk_ref, dv_ref, cot_ref, first_ref, second_ref):
    width = normed_ref.shape[1]
    rest = width // (2 * n_x)
    for x in range(n_x):
        columns = pl.ds(pl.multiple_of((2 * x + which_ref[0]) * rest, rest), rest)
        rows = pl.ds(x * rest, rest)
        left = normed_ref[:, columns].T
        for ref, right, start in ((first_ref, dq_ref, 0), (first_ref, dk_ref, width), (second_ref, dv_ref, 0)):
            ref[rows, pl.ds(start, width)] = contract(left, right[...], ((1,), (0,))).astype(jnp.bfloat16)
        left = mixed_ref[:, columns].T
        second_ref[rows, pl.ds(width, width)] = contract(left, cot_ref[...], ((1,), (0,))).astype(jnp.bfloat16)


def products(which, n_x, normed, mixed, dq, dk, dv, cot):
    rows, width = normed.shape
    half = jax.ShapeDtypeStruct((width // 2, 2 * width), jnp.bfloat16)
    return pl.pallas_call(
        functools.partial(product_kernel, n_x),
        out_shape=[half, half],
        in_specs=[pl.BlockSpec(memory_space=pltpu.SMEM)]
        + [pl.BlockSpec(memory_space=pltpu.VMEM)] * 6,
        out_specs=[pl.BlockSpec(memory_space=pltpu.VMEM)] * 2,
        compiler_params=pltpu.CompilerParams(vmem_limit_bytes=24 * MIB),
        cost_estimate=pl.CostEstimate(
            flops=4 * rows * width * width,
            bytes_accessed=12 * rows * width + 4 * width * width,
            transcendentals=0,
        ),
    )(which, normed, mixed, dq, dk, dv, cot)


def sublayer_kernel(n_clips, n_positions, n_pieces, n_aliased, *refs):
    pieces, refs = refs[:n_pieces], refs[n_pieces:]
    wq_ref, wk_ref, wv_ref, wo_ref = refs[:4]
    refs = refs[4 + n_aliased :]
    normed_ref, cot_ref, mixed_ref, dq_ref, dk_ref, dv_ref = refs[:6]
    dx_refs, total_ref = refs[6:-1], refs[-1]
    step = pl.program_id(0)
    rows = normed_ref.shape[0] // n_clips
    span = rows // n_pieces
    wide = wo_ref.shape[0]
    depth = wide // GROUP
    scaling = depth**-0.5

    def raw_rows():
        return jnp.concatenate(
            [pieces[k][0, clip] for clip in range(n_clips) for k in range(n_pieces)], axis=0
        ).astype(jnp.float32)

    @pl.when(step == 0)
    def _():
        unit, _ = statistics(raw_rows())
        normed_ref[...] = unit.astype(jnp.bfloat16)
        for clip in range(n_clips):
            for k in range(n_pieces):
                cot_ref[pl.ds(clip * rows + k * span, span)] = pieces[k][1, clip]

    normed = normed_ref[...]
    all_queries = contract(normed, wq_ref[...], ((1,), (0,))).astype(jnp.bfloat16)
    all_keys = contract(normed, wk_ref[...], ((1,), (0,))).astype(jnp.bfloat16)
    all_values = contract(normed, wv_ref[...], ((1,), (0,))).astype(jnp.bfloat16)
    mixed_grad = contract(cot_ref[...], wo_ref[...], ((1,), (1,))).astype(jnp.bfloat16)

    lane_head = lax.broadcasted_iota(jnp.int32, (rows, wide), 1) // depth
    head_masks = [(lane_head == h).astype(jnp.float32).astype(jnp.bfloat16) for h in range(GROUP)]
    key_pos = lax.broadcasted_iota(jnp.int32, (rows, rows), 0) % n_positions
    query_pos = lax.broadcasted_iota(jnp.int32, (rows, rows), 1) % n_positions
    same = (key_pos == query_pos)[None]

    def stacked(block):
        return jnp.concatenate([block * mask for mask in head_masks], axis=0)

    def side_by_side(blocks):
        return jnp.concatenate([blocks[h] for h in range(GROUP)], axis=1)

    for clip in range(n_clips):
        here = slice(clip * rows, (clip + 1) * rows)
        queries = all_queries[here]
        keys = stacked(all_keys[here])
        values = stacked(all_values[here])
        upstream = mixed_grad[here]
        scores = contract(keys, queries, ((1,), (1,))).reshape(GROUP, rows, rows)
        scores = jnp.where(same, scores * scaling, LOWEST)
        expo = jnp.exp(scores - jnp.max(scores, axis=1, keepdims=True))
        full = expo * (1.0 / jnp.sum(expo, axis=1, keepdims=True))
        low = full.astype(jnp.bfloat16)
        dots = contract(values, upstream, ((1,), (1,))).reshape(GROUP, rows, rows)
        score_grad = full * (dots - jnp.sum(full * dots, axis=1, keepdims=True))
        score_grad = (score_grad * scaling).astype(jnp.bfloat16)
        mixed = contract(low.reshape(GROUP * rows, rows), values, ((0,), (0,)))
        mixed_ref[here] = mixed.astype(jnp.bfloat16)
        dq = contract(score_grad.reshape(GROUP * rows, rows), keys, ((0,), (0,)))
        dq_ref[here] = dq.astype(jnp.bfloat16)
        dk = contract(side_by_side(score_grad), stacked(queries), ((1,), (0,)))
        dk_ref[here] = dk.astype(jnp.bfloat16)
        dv = contract(side_by_side(low), stacked(upstream), ((1,), (0,)))
        dv_ref[here] = dv.astype(jnp.bfloat16)

    part = contract(dq_ref[...], wq_ref[...], ((1,), (1,)))
    part += contract(dk_ref[...], wk_ref[...], ((1,), (1,)))
    part += contract(dv_ref[...], wv_ref[...], ((1,), (1,)))

    @pl.when(step == 0)
    def _():
        total_ref[...] = part

    @pl.when(step > 0)
    def _():
        total_ref[...] += part

    @pl.when(step == pl.num_programs(0) - 1)
    def _():
        unit, inverse = statistics(raw_rows())
        total = total_ref[...]
        grad = inverse * (
            total
            - jnp.mean(total, axis=-1, keepdims=True)
            - unit * jnp.mean(total * unit, axis=-1, keepdims=True)
        )
        dx = (cot_ref[...].astype(jnp.float32) + grad).astype(jnp.bfloat16)
        for clip in range(n_clips):
            for k in range(n_pieces):
                start = clip * rows + k * span
                dx_refs[k][clip] = dx[start : start + span]


def sublayer(pieces, w_qkv, w_out, chunk, n_chunks, n_positions, before):
    n_pieces = len(pieces)
    _, n_clips, span, width = pieces[0].shape
    rows = n_clips * n_pieces * span
    groups = HEADS // GROUP
    wide = width // groups

    def whole(shape):
        return pl.BlockSpec(shape, lambda j: (0,) * len(shape))

    flat = jax.ShapeDtypeStruct((n_chunks * rows, width), jnp.bfloat16)
    dx = jax.ShapeDtypeStruct((n_clips, span, width), jnp.bfloat16)
    out_shape = [flat] * 6 + [dx] * n_pieces
    aliased = [] if before is None else list(before)
    first = n_pieces + 4
    return pl.pallas_call(
        functools.partial(sublayer_kernel, n_clips, n_positions, n_pieces, len(aliased)),
        grid=(groups,),
        out_shape=out_shape,
        in_specs=[whole(piece.shape) for piece in pieces]
        + [pl.BlockSpec((width, wide), lambda j, i=i: (0, i * groups + j)) for i in range(3)]
        + [pl.BlockSpec((wide, width), lambda j: (j, 0))]
        + [pl.BlockSpec(memory_space=pl.ANY)] * len(aliased),
        out_specs=[
            pl.BlockSpec((rows, width), lambda j: (chunk, 0)),
            pl.BlockSpec((rows, width), lambda j: (chunk, 0)),
        ]
        + [pl.BlockSpec((rows, wide), lambda j: (chunk, j))] * 4
        + [whole(dx.shape)] * n_pieces,
        scratch_shapes=[pltpu.VMEM((rows, width), jnp.float32)],
        input_output_aliases={first + i: i for i in range(len(aliased))},
        compiler_params=pltpu.CompilerParams(vmem_limit_bytes=28 * MIB),
        cost_estimate=pl.CostEstimate(
            flops=2 * rows * width * (7 * width + 24 * 128),
            bytes_accessed=16 * rows * width + 8 * width * width,
            transcendentals=rows * 128 * HEADS,
        ),
    )(*pieces, w_qkv, w_qkv, w_qkv, w_out, *aliased)


def swap(block, axis, size, distance):
    return lax.ppermute(block, axis, [(i, i ^ distance) for i in range(size)])


def digit(axis, stride, count):
    return lax.axis_index(axis) // stride % count


def part(addends, index, dim):
    return [lax.dynamic_index_in_dim(a, index, dim, keepdims=False) for a in addends]


def summed(addends):
    total = addends[0].astype(jnp.float32)
    for a in addends[1:]:
        total += a.astype(jnp.float32)
    return total


def scatter(addends, dim, axis, size, stride, count):
    me = digit(axis, stride, count)
    kept = part(addends, me, dim)
    for j in range(1, count):
        sent = summed(part(addends, me ^ j, dim)).astype(jnp.bfloat16)
        kept.append(swap(sent, axis, size, j * stride))
    return kept


def after(values, done):
    values, _ = lax.optimization_barrier((values, done))
    return values


def shards(n_clip_devices, n_tm, clips, w_qkv, w_out, cotangent):
    n_clips, _, n_patches, width = clips.shape
    n_positions = n_patches // n_tm
    me = lax.axis_index("tm").reshape(1)
    joined = n_positions % 16 != 0
    order = range(n_tm - 1, 0, -1)
    far = range(n_tm // 2, n_tm)

    def exchanged(blocks):
        return {0: blocks[0]} | {k: swap(blocks[k], "tm", n_tm, k) for k in order}

    arrived = []
    for blocks in pick(me, clips, cotangent, n_tm, CHUNKS):
        if arrived:
            blocks = after(blocks, [arrived[-1][k] for k in far])
        arrived.append(exchanged(blocks))
    results, dx = None, []
    for chunk, pieces in enumerate(arrived):
        pieces = [pieces[k] for k in range(n_tm)]
        if joined:
            pieces = [jnp.stack(pieces, axis=2).reshape(2, n_clips // CHUNKS, -1, width)]
        out = sublayer(pieces, w_qkv, w_out, chunk, CHUNKS, n_positions, results)
        results, blocks = out[:6], list(out[6:])
        if joined:
            cut = blocks[0].reshape(n_clips // CHUNKS, n_tm, n_positions, width)
            blocks = [cut[:, k] for k in range(n_tm)]
        dx.append(blocks)
    normed, cot, mixed, dq, dk, dv = results

    cores, n_y = 2, 2
    n_x, n_z = n_clip_devices // cores, n_tm // n_y
    core = digit("clip", 1, cores)
    rest = width // (cores * n_x * n_z * n_y)
    factors = (normed, mixed, dq, dk, dv, cot)
    sent = products((1 - core).reshape(1), n_x, *factors)
    kept = products(core.reshape(1), n_x, *after(factors, sent))
    first, second = (
        [a.reshape(n_x, n_z, n_y, rest, -1) for a in (mine, swap(theirs, "clip", n_clip_devices, 1))]
        for mine, theirs in zip(kept, sent)
    )
    for chunk in range(CHUNKS):
        done = [arrived[-1][k] for k in far] if chunk < CHUNKS - 1 else sent
        dx[chunk] = exchanged(after(dx[chunk], done))
    grad_clips = place(me, [[d[k] for k in range(n_tm)] for d in dx]).reshape(clips.shape)

    first = scatter(first, 0, "clip", n_clip_devices, cores, n_x)
    second = scatter(second, 2, "tm", n_tm, 1, n_y)
    first = scatter(first, 1, "tm", n_tm, 1, n_y)
    second = scatter(second, 0, "clip", n_clip_devices, cores, n_x)
    z = digit("tm", n_y, n_z)

    def both(index):
        return jnp.concatenate([summed(part(a, index, 0)) for a in (first, second)], axis=-1)

    total = both(z)
    for j in range(1, n_z):
        other = swap(both(z ^ j).astype(jnp.bfloat16), "tm", n_tm, j * n_y)
        total += other.astype(jnp.float32)
    return (grad_clips, total[:, : 3 * width], total[:, 3 * width :])


def solution(mesh):
    return jax.shard_map(
        functools.partial(shards, mesh.shape["clip"], mesh.shape["tm"]),
        mesh=mesh,
        in_specs=(P("clip", "tm", None, None), P(), P(), P("clip", "tm", None, None)),
        out_specs=(P("clip", "tm", None, None), P(("clip", "tm"), None), P(("clip", "tm"), None)),
        check_vma=False,
    )
```

```python
import functools
import itertools

import jax
import jax.numpy as jnp
from jax import lax
from jax.experimental import pallas as pl
from jax.experimental.pallas import tpu as pltpu
from jax.sharding import PartitionSpec as P

HEADS = 16
GROUP = 4
CHUNKS = 2
WINDOW = 5
CORES = 2
N_Y = 2
EPSILON = 1e-06
LOWEST = -1e30
MIB = 1024 * 1024


def contract(left, right, dims):
    return lax.dot_general(left, right, (dims, ((), ())), preferred_element_type=jnp.float32)


def statistics(rows32):
    mean = jnp.mean(rows32, axis=-1, keepdims=True)
    centred = rows32 - mean
    inverse = lax.rsqrt(jnp.mean(centred * centred, axis=-1, keepdims=True) + EPSILON)
    return centred * inverse, inverse


def pick_kernel(n_slots, n_chunks, ids_ref, x_ref, cot_ref, *out_refs):
    depth = x_ref.shape[0] // n_chunks
    for chunk in range(n_chunks):
        here = pl.ds(chunk * depth, depth)
        for slot in range(n_slots):
            out = out_refs[chunk * n_slots + slot]
            block = ids_ref[1] ^ slot
            out[0] = x_ref[here, block]
            out[1] = cot_ref[here, block]


def pick(ids, clips, cotangent, n_slots, n_chunks):
    n_clips, _, n_patches, width = clips.shape
    cut = (n_clips, n_slots, n_patches // n_slots, width)
    piece = jax.ShapeDtypeStruct((2, n_clips // n_chunks) + cut[2:], clips.dtype)
    out = pl.pallas_call(
        functools.partial(pick_kernel, n_slots, n_chunks),
        out_shape=[piece] * (n_slots * n_chunks),
        in_specs=[
            pl.BlockSpec(memory_space=pltpu.SMEM),
            pl.BlockSpec(memory_space=pltpu.VMEM),
            pl.BlockSpec(memory_space=pltpu.VMEM),
        ],
        out_specs=[pl.BlockSpec(memory_space=pltpu.VMEM)] * (n_slots * n_chunks),
        compiler_params=pltpu.CompilerParams(vmem_limit_bytes=16 * MIB),
    )(ids, clips.reshape(cut), cotangent.reshape(cut))
    return [out[chunk * n_slots : (chunk + 1) * n_slots] for chunk in range(n_chunks)]


def place_kernel(ids_ref, *refs):
    for slot, ref in enumerate(refs[:-1]):
        refs[-1][:, ids_ref[1] ^ slot] = ref[...]


def place(ids, blocks):
    n_clips, n_positions, width = blocks[0].shape
    return pl.pallas_call(
        place_kernel,
        out_shape=jax.ShapeDtypeStruct((n_clips, len(blocks), n_positions, width), blocks[0].dtype),
        in_specs=[pl.BlockSpec(memory_space=pltpu.SMEM)]
        + [pl.BlockSpec(memory_space=pltpu.VMEM)] * len(blocks),
        out_specs=pl.BlockSpec(memory_space=pltpu.VMEM),
        compiler_params=pltpu.CompilerParams(vmem_limit_bytes=8 * MIB),
    )(ids, *blocks)


def product_kernel(n_x, flip, ids_ref, normed_ref, mixed_ref, dq_ref, dk_ref, dv_ref, cot_ref, first_ref, second_ref):
    width = normed_ref.shape[1]
    rest = width // (CORES * n_x)
    core = lax.rem(ids_ref[0], CORES) ^ flip
    cut = first_ref.shape[1:4]
    for x in range(n_x):
        columns = pl.ds(pl.multiple_of((CORES * x + core) * rest, rest), rest)

        def store(ref, start, left, right):
            product = contract(left, right[...], ((1,), (0,)))
            product = product.reshape(cut + (width,)).astype(jnp.bfloat16)
            ref[x, :, :, :, pl.ds(start, width)] = product

        left = normed_ref[:, columns].T
        store(first_ref, 0, left, dq_ref)
        store(first_ref, width, left, dk_ref)
        store(second_ref, 0, left, dv_ref)
        store(second_ref, width, mixed_ref[:, columns].T, cot_ref)


def products(ids, flip, n_x, n_z, normed, mixed, dq, dk, dv, cot):
    rows, width = normed.shape
    rest = width // (CORES * n_x * n_z * N_Y)
    half = jax.ShapeDtypeStruct((n_x, n_z, N_Y, rest, 2 * width), jnp.bfloat16)
    return pl.pallas_call(
        functools.partial(product_kernel, n_x, flip),
        out_shape=[half, half],
        in_specs=[pl.BlockSpec(memory_space=pltpu.SMEM)]
        + [pl.BlockSpec(memory_space=pltpu.VMEM)] * 6,
        out_specs=[pl.BlockSpec(memory_space=pltpu.VMEM)] * 2,
        compiler_params=pltpu.CompilerParams(vmem_limit_bytes=24 * MIB),
        cost_estimate=pl.CostEstimate(
            flops=4 * rows * width * width,
            bytes_accessed=12 * rows * width + 4 * width * width,
            transcendentals=0,
        ),
    )(ids, normed, mixed, dq, dk, dv, cot)


def summed(refs, index):
    total = refs[0][index].astype(jnp.float32)
    for ref in refs[1:]:
        total += ref[index].astype(jnp.float32)
    return total


def halve_kernel(dim, axis, stride, ids_ref, *refs):
    addends, sent_ref, kept_ref = refs[:-2], refs[-2], refs[-1]
    me = lax.rem(lax.div(ids_ref[axis], stride), 2)
    for index in itertools.product(*(range(n) for n in sent_ref.shape[:-2])):
        sent_ref[index] = summed(addends, index[:dim] + (me ^ 1,) + index[dim:]).astype(jnp.bfloat16)
    for index in itertools.product(*(range(n) for n in sent_ref.shape[:-2])):
        kept_ref[index] = summed(addends, index[:dim] + (me,) + index[dim:])


def halve(ids, addends, dim, axis, stride):
    shape = addends[0].shape[:dim] + addends[0].shape[dim + 1 :]
    return pl.pallas_call(
        functools.partial(halve_kernel, dim, axis, stride),
        out_shape=[jax.ShapeDtypeStruct(shape, jnp.bfloat16), jax.ShapeDtypeStruct(shape, jnp.float32)],
        in_specs=[pl.BlockSpec(memory_space=pltpu.SMEM)]
        + [pl.BlockSpec(memory_space=pltpu.VMEM)] * len(addends),
        out_specs=[pl.BlockSpec(memory_space=pltpu.VMEM)] * 2,
        compiler_params=pltpu.CompilerParams(vmem_limit_bytes=16 * MIB),
    )(ids, *addends)


def join_kernel(n_z, n_first, ids_ref, *refs):
    addends, outs = refs[:-n_z], refs[-n_z:]
    me = lax.div(ids_ref[1], N_Y)
    half = addends[0].shape[-1]
    for j in [*range(1, n_z), 0]:
        for side, part in enumerate((addends[:n_first], addends[n_first:])):
            total = summed(part, (me ^ j,))
            outs[j][:, pl.ds(side * half, half)] = total.astype(outs[j].dtype)


def join(ids, first, second, n_z):
    rows, half = first[0].shape[1:]
    own = jax.ShapeDtypeStruct((rows, 2 * half), jnp.float32)
    other = jax.ShapeDtypeStruct((rows, 2 * half), jnp.bfloat16)
    return pl.pallas_call(
        functools.partial(join_kernel, n_z, len(first)),
        out_shape=[own] + [other] * (n_z - 1),
        in_specs=[pl.BlockSpec(memory_space=pltpu.SMEM)]
        + [pl.BlockSpec(memory_space=pltpu.VMEM)] * (len(first) + len(second)),
        out_specs=[pl.BlockSpec(memory_space=pltpu.VMEM)] * n_z,
        compiler_params=pltpu.CompilerParams(vmem_limit_bytes=12 * MIB),
    )(ids, *first, *second)


def finish_kernel(*refs):
    addends, (grad_qkv_ref, grad_out_ref) = refs[:-2], refs[-2:]
    wide = grad_qkv_ref.shape[1]
    everything = slice(None)
    grad_qkv_ref[...] = summed(addends, (everything, pl.ds(0, wide)))
    grad_out_ref[...] = summed(addends, (everything, pl.ds(wide, grad_out_ref.shape[1])))


def finish(addends):
    rows, columns = addends[0].shape
    return pl.pallas_call(
        finish_kernel,
        out_shape=[
            jax.ShapeDtypeStruct((rows, columns // 4 * 3), jnp.float32),
            jax.ShapeDtypeStruct((rows, columns // 4), jnp.float32),
        ],
        in_specs=[pl.BlockSpec(memory_space=pltpu.VMEM)] * len(addends),
        out_specs=[pl.BlockSpec(memory_space=pltpu.VMEM)] * 2,
        compiler_params=pltpu.CompilerParams(vmem_limit_bytes=8 * MIB),
    )(*addends)


def sublayer_kernel(n_clips, n_positions, n_pieces, n_aliased, *refs):
    pieces, refs = refs[:n_pieces], refs[n_pieces:]
    wq_ref, wk_ref, wv_ref, wo_ref = refs[:4]
    refs = refs[4 + n_aliased :]
    normed_ref, cot_ref, mixed_ref, dq_ref, dk_ref, dv_ref = refs[:6]
    dx_refs, total_ref = refs[6:-1], refs[-1]
    step = pl.program_id(0)
    rows = normed_ref.shape[0] // n_clips
    span = rows // n_pieces
    wide = wo_ref.shape[0]
    depth = wide // GROUP
    scaling = depth**-0.5

    def raw_rows():
        return jnp.concatenate(
            [pieces[k][0, clip] for clip in range(n_clips) for k in range(n_pieces)], axis=0
        ).astype(jnp.float32)

    @pl.when(step == 0)
    def _():
        unit, _ = statistics(raw_rows())
        normed_ref[...] = unit.astype(jnp.bfloat16)
        for clip in range(n_clips):
            for k in range(n_pieces):
                cot_ref[pl.ds(clip * rows + k * span, span)] = pieces[k][1, clip]

    normed = normed_ref[...]
    all_queries = contract(normed, wq_ref[...], ((1,), (0,))).astype(jnp.bfloat16)
    all_keys = contract(normed, wk_ref[...], ((1,), (0,))).astype(jnp.bfloat16)
    all_values = contract(normed, wv_ref[...], ((1,), (0,))).astype(jnp.bfloat16)
    mixed_grad = contract(cot_ref[...], wo_ref[...], ((1,), (1,))).astype(jnp.bfloat16)

    lane_head = lax.broadcasted_iota(jnp.int32, (rows, wide), 1) // depth
    head_masks = [(lane_head == h).astype(jnp.float32).astype(jnp.bfloat16) for h in range(GROUP)]
    key_pos = lax.broadcasted_iota(jnp.int32, (rows, rows), 0) % n_positions
    query_pos = lax.broadcasted_iota(jnp.int32, (rows, rows), 1) % n_positions
    same = (key_pos == query_pos)[None]

    def stacked(block):
        return jnp.concatenate([block * mask for mask in head_masks], axis=0)

    def side_by_side(blocks):
        return jnp.concatenate([blocks[h] for h in range(GROUP)], axis=1)

    for clip in range(n_clips):
        here = slice(clip * rows, (clip + 1) * rows)
        queries = all_queries[here]
        keys = stacked(all_keys[here])
        values = stacked(all_values[here])
        upstream = mixed_grad[here]
        scores = contract(keys, queries, ((1,), (1,))).reshape(GROUP, rows, rows)
        scores = jnp.where(same, scores * scaling, LOWEST)
        expo = jnp.exp(scores - jnp.max(scores, axis=1, keepdims=True))
        full = expo * (1.0 / jnp.sum(expo, axis=1, keepdims=True))
        low = full.astype(jnp.bfloat16)
        dots = contract(values, upstream, ((1,), (1,))).reshape(GROUP, rows, rows)
        score_grad = full * (dots - jnp.sum(full * dots, axis=1, keepdims=True))
        score_grad = (score_grad * scaling).astype(jnp.bfloat16)
        mixed = contract(low.reshape(GROUP * rows, rows), values, ((0,), (0,)))
        mixed_ref[here] = mixed.astype(jnp.bfloat16)
        dq = contract(score_grad.reshape(GROUP * rows, rows), keys, ((0,), (0,)))
        dq_ref[here] = dq.astype(jnp.bfloat16)
        dk = contract(side_by_side(score_grad), stacked(queries), ((1,), (0,)))
        dk_ref[here] = dk.astype(jnp.bfloat16)
        dv = contract(side_by_side(low), stacked(upstream), ((1,), (0,)))
        dv_ref[here] = dv.astype(jnp.bfloat16)

    part = contract(dq_ref[...], wq_ref[...], ((1,), (1,)))
    part += contract(dk_ref[...], wk_ref[...], ((1,), (1,)))
    part += contract(dv_ref[...], wv_ref[...], ((1,), (1,)))

    @pl.when(step == 0)
    def _():
        total_ref[...] = part

    @pl.when(step > 0)
    def _():
        total_ref[...] += part

    @pl.when(step == pl.num_programs(0) - 1)
    def _():
        unit, inverse = statistics(raw_rows())
        total = total_ref[...]
        grad = inverse * (
            total
            - jnp.mean(total, axis=-1, keepdims=True)
            - unit * jnp.mean(total * unit, axis=-1, keepdims=True)
        )
        dx = (cot_ref[...].astype(jnp.float32) + grad).astype(jnp.bfloat16)
        for clip in range(n_clips):
            for k in range(n_pieces):
                start = clip * rows + k * span
                dx_refs[k][clip] = dx[start : start + span]


def sublayer(pieces, w_qkv, w_out, chunk, n_chunks, n_positions, before):
    n_pieces = len(pieces)
    _, n_clips, span, width = pieces[0].shape
    rows = n_clips * n_pieces * span
    groups = HEADS // GROUP
    wide = width // groups

    def whole(shape):
        return pl.BlockSpec(shape, lambda j: (0,) * len(shape))

    flat = jax.ShapeDtypeStruct((n_chunks * rows, width), jnp.bfloat16)
    dx = jax.ShapeDtypeStruct((n_chunks * n_clips, span, width), jnp.bfloat16)
    out_shape = [flat] * 6 + [dx] * n_pieces
    aliased = [] if before is None else list(before)
    first = n_pieces + 4
    return pl.pallas_call(
        functools.partial(sublayer_kernel, n_clips, n_positions, n_pieces, len(aliased)),
        grid=(groups,),
        out_shape=out_shape,
        in_specs=[whole(piece.shape) for piece in pieces]
        + [pl.BlockSpec((width, wide), lambda j, i=i: (0, i * groups + j)) for i in range(3)]
        + [pl.BlockSpec((wide, width), lambda j: (j, 0))]
        + [pl.BlockSpec(memory_space=pl.ANY)] * len(aliased),
        out_specs=[
            pl.BlockSpec((rows, width), lambda j: (chunk, 0)),
            pl.BlockSpec((rows, width), lambda j: (chunk, 0)),
        ]
        + [pl.BlockSpec((rows, wide), lambda j: (chunk, j))] * 4
        + [pl.BlockSpec((n_clips, span, width), lambda j: (chunk, 0, 0))] * n_pieces,
        scratch_shapes=[pltpu.VMEM((rows, width), jnp.float32)],
        input_output_aliases={first + i: i for i in range(len(aliased))},
        compiler_params=pltpu.CompilerParams(vmem_limit_bytes=28 * MIB),
        cost_estimate=pl.CostEstimate(
            flops=2 * rows * width * (7 * width + 24 * 128),
            bytes_accessed=16 * rows * width + 8 * width * width,
            transcendentals=rows * 128 * HEADS,
        ),
    )(*pieces, w_qkv, w_qkv, w_qkv, w_out, *aliased)


def swap(block, axis, size, distance):
    return lax.ppermute(block, axis, [(i, i ^ distance) for i in range(size)])


def after(values, done):
    values, _ = lax.optimization_barrier((values, done))
    return values


def inbound_order(n_tm, chunk):
    far, near = list(range(n_tm - 1, n_tm // 2 - 1, -1)), list(range(1, n_tm // 2))
    if chunk == CHUNKS - 1:
        return far + near
    cut = len(far) // 2
    return far[:cut] + near[:1] + far[cut:] + near[1:]


def shards(n_clip_devices, n_tm, clips, w_qkv, w_out, cotangent):
    n_clips, _, n_patches, width = clips.shape
    n_positions = n_patches // n_tm
    n_x, n_z = n_clip_devices // CORES, n_tm // N_Y
    joined = n_positions % 16 != 0
    ids = jnp.stack([lax.axis_index("clip"), lax.axis_index("tm")]).astype(jnp.int32)

    arrived, line = [], []
    for chunk, blocks in enumerate(pick(ids, clips, cotangent, n_tm, CHUNKS)):
        pieces = {0: blocks[0]}
        for k in inbound_order(n_tm, chunk):
            block = blocks[k]
            if len(line) >= WINDOW:
                block = after(block, line[-WINDOW])
            pieces[k] = swap(block, "tm", n_tm, k)
            line.append(pieces[k])
        arrived.append([pieces[k] for k in range(n_tm)])
    results = None
    for chunk, pieces in enumerate(arrived):
        if joined:
            pieces = [jnp.stack(pieces, axis=2).reshape(2, n_clips // CHUNKS, -1, width)]
        results = sublayer(pieces, w_qkv, w_out, chunk, CHUNKS, n_positions, results)
    normed, cot, mixed, dq, dk, dv = results[:6]
    dx = list(results[6:])
    if joined:
        cut = dx[0].reshape(n_clips, n_tm, n_positions, width)
        dx = [cut[:, k] for k in range(n_tm)]

    factors = (normed, mixed, dq, dk, dv, cot)
    sent = products(ids, 1, n_x, n_z, *factors)
    first, second = (swap(half, "clip", n_clip_devices, 1) for half in sent)
    dx = after(dx, sent)
    dx = [dx[0]] + [swap(dx[k], "tm", n_tm, k) for k in range(1, n_tm)]
    own_first, own_second = products(ids, 0, n_x, n_z, *after(factors, sent))

    sent, own_first = halve(ids, (own_first, first), 0, 0, CORES)
    first = swap(sent, "clip", n_clip_devices, CORES)
    sent, own_second = halve(ids, (own_second, second), 2, 1, 1)
    second = swap(sent, "tm", n_tm, 1)
    first, second = after((first, second), dx)
    sent, own_first = halve(ids, (own_first, first), 1, 1, 1)
    first = swap(sent, "tm", n_tm, 1)
    sent, own_second = halve(ids, (own_second, second), 0, 0, CORES)
    second = swap(sent, "clip", n_clip_devices, CORES)
    total, *sent = join(ids, (own_first, first), (own_second, second), n_z)
    grad_clips = place(ids, dx).reshape(clips.shape)
    others = [swap(block, "tm", n_tm, (j + 1) * N_Y) for j, block in enumerate(sent)]
    grad_qkv, grad_out = finish((total, *others))
    return (grad_clips, grad_qkv, grad_out)


def solution(mesh):
    return jax.shard_map(
        functools.partial(shards, mesh.shape["clip"], mesh.shape["tm"]),
        mesh=mesh,
        in_specs=(P("clip", "tm", None, None), P(), P(), P("clip", "tm", None, None)),
        out_specs=(P("clip", "tm", None, None), P(("clip", "tm"), None), P(("clip", "tm"), None)),
        check_vma=False,
    )
```

```python
import functools
import itertools

import jax
import jax.numpy as jnp
from jax import lax
from jax.experimental import pallas as pl
from jax.experimental.pallas import tpu as pltpu
from jax.sharding import PartitionSpec as P

HEADS = 16
GROUP = 4
CHUNKS = 2
CORES = 2
N_Y = 2
EPSILON = 1e-06
LOWEST = -1e30
MIB = 1024 * 1024


def contract(left, right, dims):
    return lax.dot_general(left, right, (dims, ((), ())), preferred_element_type=jnp.float32)


def statistics(rows32):
    mean = jnp.mean(rows32, axis=-1, keepdims=True)
    centred = rows32 - mean
    inverse = lax.rsqrt(jnp.mean(centred * centred, axis=-1, keepdims=True) + EPSILON)
    return centred * inverse, inverse


def pick_kernel(n_slots, n_chunks, ids_ref, x_ref, cot_ref, *out_refs):
    depth = x_ref.shape[0] // n_chunks
    for chunk in range(n_chunks):
        here = pl.ds(chunk * depth, depth)
        for slot in range(n_slots):
            out = out_refs[chunk * n_slots + slot]
            block = ids_ref[1] ^ slot
            out[0] = x_ref[here, block]
            out[1] = cot_ref[here, block]


def pick(ids, clips, cotangent, n_slots, n_chunks):
    n_clips, _, n_patches, width = clips.shape
    cut = (n_clips, n_slots, n_patches // n_slots, width)
    piece = jax.ShapeDtypeStruct((2, n_clips // n_chunks) + cut[2:], clips.dtype)
    out = pl.pallas_call(
        functools.partial(pick_kernel, n_slots, n_chunks),
        out_shape=[piece] * (n_slots * n_chunks),
        in_specs=[
            pl.BlockSpec(memory_space=pltpu.SMEM),
            pl.BlockSpec(memory_space=pltpu.VMEM),
            pl.BlockSpec(memory_space=pltpu.VMEM),
        ],
        out_specs=[pl.BlockSpec(memory_space=pltpu.VMEM)] * (n_slots * n_chunks),
        compiler_params=pltpu.CompilerParams(vmem_limit_bytes=16 * MIB),
    )(ids, clips.reshape(cut), cotangent.reshape(cut))
    return [out[chunk * n_slots : (chunk + 1) * n_slots] for chunk in range(n_chunks)]


def place_kernel(ids_ref, *refs):
    for slot, ref in enumerate(refs[:-1]):
        refs[-1][:, ids_ref[1] ^ slot] = ref[...]


def place(ids, blocks):
    n_clips, n_positions, width = blocks[0].shape
    return pl.pallas_call(
        place_kernel,
        out_shape=jax.ShapeDtypeStruct((n_clips, len(blocks), n_positions, width), blocks[0].dtype),
        in_specs=[pl.BlockSpec(memory_space=pltpu.SMEM)]
        + [pl.BlockSpec(memory_space=pltpu.VMEM)] * len(blocks),
        out_specs=pl.BlockSpec(memory_space=pltpu.VMEM),
        compiler_params=pltpu.CompilerParams(vmem_limit_bytes=8 * MIB),
    )(ids, *blocks)


def product_kernel(n_x, flip, n_lefts, ids_ref, *refs):
    lefts, rights, out_ref = refs[:n_lefts], refs[n_lefts:-1], refs[-1]
    width = lefts[0].shape[1]
    rest = width // (CORES * n_x)
    core = lax.rem(ids_ref[0], CORES) ^ flip
    cut = out_ref.shape[1:4]
    for x in range(n_x):
        columns = pl.ds(pl.multiple_of((CORES * x + core) * rest, rest), rest)
        turned = [left[:, columns].T for left in lefts]
        for i, right in enumerate(rights):
            product = contract(turned[min(i, n_lefts - 1)], right[...], ((1,), (0,)))
            product = product.reshape(cut + (width,)).astype(jnp.bfloat16)
            out_ref[x, :, :, :, pl.ds(i * width, width)] = product


def products(ids, flip, n_x, n_z, lefts, rights):
    rows, width = rights[0].shape
    rest = width // (CORES * n_x * n_z * N_Y)
    return pl.pallas_call(
        functools.partial(product_kernel, n_x, flip, len(lefts)),
        out_shape=jax.ShapeDtypeStruct((n_x, n_z, N_Y, rest, len(rights) * width), jnp.bfloat16),
        in_specs=[pl.BlockSpec(memory_space=pltpu.SMEM)]
        + [pl.BlockSpec(memory_space=pltpu.VMEM)] * (len(lefts) + len(rights)),
        out_specs=pl.BlockSpec(memory_space=pltpu.VMEM),
        compiler_params=pltpu.CompilerParams(vmem_limit_bytes=20 * MIB),
        cost_estimate=pl.CostEstimate(
            flops=2 * rows * width * width,
            bytes_accessed=8 * rows * width + 2 * width * width,
            transcendentals=0,
        ),
    )(ids, *lefts, *rights)


def summed(refs, index):
    total = refs[0][index].astype(jnp.float32)
    for ref in refs[1:]:
        total += ref[index].astype(jnp.float32)
    return total


def halve_kernel(dim, axis, stride, ids_ref, *refs):
    addends, sent_ref, kept_ref = refs[:-2], refs[-2], refs[-1]
    me = lax.rem(lax.div(ids_ref[axis], stride), 2)
    for index in itertools.product(*(range(n) for n in sent_ref.shape[:-2])):
        sent_ref[index] = summed(addends, index[:dim] + (me ^ 1,) + index[dim:]).astype(jnp.bfloat16)
    for index in itertools.product(*(range(n) for n in sent_ref.shape[:-2])):
        kept_ref[index] = summed(addends, index[:dim] + (me,) + index[dim:])


def halve(ids, addends, dim, axis, stride):
    shape = addends[0].shape[:dim] + addends[0].shape[dim + 1 :]
    return pl.pallas_call(
        functools.partial(halve_kernel, dim, axis, stride),
        out_shape=[jax.ShapeDtypeStruct(shape, jnp.bfloat16), jax.ShapeDtypeStruct(shape, jnp.float32)],
        in_specs=[pl.BlockSpec(memory_space=pltpu.SMEM)]
        + [pl.BlockSpec(memory_space=pltpu.VMEM)] * len(addends),
        out_specs=[pl.BlockSpec(memory_space=pltpu.VMEM)] * 2,
        compiler_params=pltpu.CompilerParams(vmem_limit_bytes=16 * MIB),
    )(ids, *addends)


def join_kernel(n_z, n_first, ids_ref, *refs):
    addends, outs = refs[:-n_z], refs[-n_z:]
    me = lax.div(ids_ref[1], N_Y)
    half = addends[0].shape[-1]
    for j in [*range(1, n_z), 0]:
        for side, part in enumerate((addends[:n_first], addends[n_first:])):
            total = summed(part, (me ^ j,))
            outs[j][:, pl.ds(side * half, half)] = total.astype(outs[j].dtype)


def join(ids, first, second, n_z):
    rows, half = first[0].shape[1:]
    own = jax.ShapeDtypeStruct((rows, 2 * half), jnp.float32)
    other = jax.ShapeDtypeStruct((rows, 2 * half), jnp.bfloat16)
    return pl.pallas_call(
        functools.partial(join_kernel, n_z, len(first)),
        out_shape=[own] + [other] * (n_z - 1),
        in_specs=[pl.BlockSpec(memory_space=pltpu.SMEM)]
        + [pl.BlockSpec(memory_space=pltpu.VMEM)] * (len(first) + len(second)),
        out_specs=[pl.BlockSpec(memory_space=pltpu.VMEM)] * n_z,
        compiler_params=pltpu.CompilerParams(vmem_limit_bytes=12 * MIB),
    )(ids, *first, *second)


def finish_kernel(*refs):
    addends, (grad_qkv_ref, grad_out_ref) = refs[:-2], refs[-2:]
    wide = grad_qkv_ref.shape[1]
    everything = slice(None)
    grad_qkv_ref[...] = summed(addends, (everything, pl.ds(0, wide)))
    grad_out_ref[...] = summed(addends, (everything, pl.ds(wide, grad_out_ref.shape[1])))


def finish(addends):
    rows, columns = addends[0].shape
    return pl.pallas_call(
        finish_kernel,
        out_shape=[
            jax.ShapeDtypeStruct((rows, columns // 4 * 3), jnp.float32),
            jax.ShapeDtypeStruct((rows, columns // 4), jnp.float32),
        ],
        in_specs=[pl.BlockSpec(memory_space=pltpu.VMEM)] * len(addends),
        out_specs=[pl.BlockSpec(memory_space=pltpu.VMEM)] * 2,
        compiler_params=pltpu.CompilerParams(vmem_limit_bytes=8 * MIB),
    )(*addends)


def sublayer_kernel(n_clips, n_positions, n_pieces, n_aliased, *refs):
    pieces, refs = refs[:n_pieces], refs[n_pieces:]
    wq_ref, wk_ref, wv_ref, wo_ref = refs[:4]
    refs = refs[4 + n_aliased :]
    normed_ref, cot_ref, mixed_ref, dq_ref, dk_ref, dv_ref = refs[:6]
    dx_refs, total_ref = refs[6:-1], refs[-1]
    step = pl.program_id(0)
    rows = normed_ref.shape[0] // n_clips
    span = rows // n_pieces
    wide = wo_ref.shape[0]
    depth = wide // GROUP
    scaling = depth**-0.5

    def raw_rows():
        return jnp.concatenate(
            [pieces[k][0, clip] for clip in range(n_clips) for k in range(n_pieces)], axis=0
        ).astype(jnp.float32)

    @pl.when(step == 0)
    def _():
        unit, _ = statistics(raw_rows())
        normed_ref[...] = unit.astype(jnp.bfloat16)
        for clip in range(n_clips):
            for k in range(n_pieces):
                cot_ref[pl.ds(clip * rows + k * span, span)] = pieces[k][1, clip]

    normed = normed_ref[...]
    all_queries = contract(normed, wq_ref[...], ((1,), (0,))).astype(jnp.bfloat16)
    all_keys = contract(normed, wk_ref[...], ((1,), (0,))).astype(jnp.bfloat16)
    all_values = contract(normed, wv_ref[...], ((1,), (0,))).astype(jnp.bfloat16)
    mixed_grad = contract(cot_ref[...], wo_ref[...], ((1,), (1,))).astype(jnp.bfloat16)

    lane_head = lax.broadcasted_iota(jnp.int32, (rows, wide), 1) // depth
    head_masks = [(lane_head == h).astype(jnp.float32).astype(jnp.bfloat16) for h in range(GROUP)]
    key_pos = lax.broadcasted_iota(jnp.int32, (rows, rows), 0) % n_positions
    query_pos = lax.broadcasted_iota(jnp.int32, (rows, rows), 1) % n_positions
    same = (key_pos == query_pos)[None]

    def stacked(block):
        return jnp.concatenate([block * mask for mask in head_masks], axis=0)

    def side_by_side(blocks):
        return jnp.concatenate([blocks[h] for h in range(GROUP)], axis=1)

    for clip in range(n_clips):
        here = slice(clip * rows, (clip + 1) * rows)
        queries = all_queries[here]
        keys = stacked(all_keys[here])
        values = stacked(all_values[here])
        upstream = mixed_grad[here]
        scores = contract(keys, queries, ((1,), (1,))).reshape(GROUP, rows, rows)
        scores = jnp.where(same, scores * scaling, LOWEST)
        expo = jnp.exp(scores - jnp.max(scores, axis=1, keepdims=True))
        full = expo * (1.0 / jnp.sum(expo, axis=1, keepdims=True))
        low = full.astype(jnp.bfloat16)
        dots = contract(values, upstream, ((1,), (1,))).reshape(GROUP, rows, rows)
        score_grad = full * (dots - jnp.sum(full * dots, axis=1, keepdims=True))
        score_grad = (score_grad * scaling).astype(jnp.bfloat16)
        mixed = contract(low.reshape(GROUP * rows, rows), values, ((0,), (0,)))
        mixed_ref[here] = mixed.astype(jnp.bfloat16)
        dq = contract(score_grad.reshape(GROUP * rows, rows), keys, ((0,), (0,)))
        dq_ref[here] = dq.astype(jnp.bfloat16)
        dk = contract(side_by_side(score_grad), stacked(queries), ((1,), (0,)))
        dk_ref[here] = dk.astype(jnp.bfloat16)
        dv = contract(side_by_side(low), stacked(upstream), ((1,), (0,)))
        dv_ref[here] = dv.astype(jnp.bfloat16)

    part = contract(dq_ref[...], wq_ref[...], ((1,), (1,)))
    part += contract(dk_ref[...], wk_ref[...], ((1,), (1,)))
    part += contract(dv_ref[...], wv_ref[...], ((1,), (1,)))

    @pl.when(step == 0)
    def _():
        total_ref[...] = part

    @pl.when(step > 0)
    def _():
        total_ref[...] += part

    @pl.when(step == pl.num_programs(0) - 1)
    def _():
        unit, inverse = statistics(raw_rows())
        total = total_ref[...]
        grad = inverse * (
            total
            - jnp.mean(total, axis=-1, keepdims=True)
            - unit * jnp.mean(total * unit, axis=-1, keepdims=True)
        )
        dx = (cot_ref[...].astype(jnp.float32) + grad).astype(jnp.bfloat16)
        for clip in range(n_clips):
            for k in range(n_pieces):
                start = clip * rows + k * span
                dx_refs[k][clip] = dx[start : start + span]


def sublayer(pieces, w_qkv, w_out, chunk, n_chunks, n_positions, before):
    n_pieces = len(pieces)
    _, n_clips, span, width = pieces[0].shape
    rows = n_clips * n_pieces * span
    groups = HEADS // GROUP
    wide = width // groups

    def whole(shape):
        return pl.BlockSpec(shape, lambda j: (0,) * len(shape))

    flat = jax.ShapeDtypeStruct((n_chunks * rows, width), jnp.bfloat16)
    dx = jax.ShapeDtypeStruct((n_chunks * n_clips, span, width), jnp.bfloat16)
    out_shape = [flat] * 6 + [dx] * n_pieces
    aliased = [] if before is None else list(before)
    first = n_pieces + 4
    return pl.pallas_call(
        functools.partial(sublayer_kernel, n_clips, n_positions, n_pieces, len(aliased)),
        grid=(groups,),
        out_shape=out_shape,
        in_specs=[whole(piece.shape) for piece in pieces]
        + [pl.BlockSpec((width, wide), lambda j, i=i: (0, i * groups + j)) for i in range(3)]
        + [pl.BlockSpec((wide, width), lambda j: (j, 0))]
        + [pl.BlockSpec(memory_space=pl.ANY)] * len(aliased),
        out_specs=[
            pl.BlockSpec((rows, width), lambda j: (chunk, 0)),
            pl.BlockSpec((rows, width), lambda j: (chunk, 0)),
        ]
        + [pl.BlockSpec((rows, wide), lambda j: (chunk, j))] * 4
        + [pl.BlockSpec((n_clips, span, width), lambda j: (chunk, 0, 0))] * n_pieces,
        scratch_shapes=[pltpu.VMEM((rows, width), jnp.float32)],
        input_output_aliases={first + i: i for i in range(len(aliased))},
        compiler_params=pltpu.CompilerParams(vmem_limit_bytes=28 * MIB),
        cost_estimate=pl.CostEstimate(
            flops=2 * rows * width * (7 * width + 24 * 128),
            bytes_accessed=16 * rows * width + 8 * width * width,
            transcendentals=rows * 128 * HEADS,
        ),
    )(*pieces, w_qkv, w_qkv, w_qkv, w_out, *aliased)


def swap(block, axis, size, distance):
    return lax.ppermute(block, axis, [(i, i ^ distance) for i in range(size)])


def after(values, done):
    values, _ = lax.optimization_barrier((values, done))
    return values


def inbound(chunks, n_tm):
    half = n_tm // 2
    arrived = []
    for blocks in chunks:
        pieces = {0: blocks[0]}
        for k in range(1, half):
            gate = arrived[-1][k] if arrived else None
            pieces[k] = swap(blocks[k] if gate is None else after(blocks[k], gate), "tm", n_tm, k)
        for i, k in enumerate(range(n_tm - 1, half - 1, -1)):
            gate = arrived[-1][k] if arrived else None
            if not arrived and i >= half // 2:
                gate = pieces[i - half // 2 + 1]
            pieces[k] = swap(blocks[k] if gate is None else after(blocks[k], gate), "tm", n_tm, k)
        arrived.append([pieces[k] for k in range(n_tm)])
    return arrived


def shards(n_clip_devices, n_tm, clips, w_qkv, w_out, cotangent):
    n_clips, _, n_patches, width = clips.shape
    n_positions = n_patches // n_tm
    n_x, n_z = n_clip_devices // CORES, n_tm // N_Y
    joined = n_positions % 16 != 0
    ids = jnp.stack([lax.axis_index("clip"), lax.axis_index("tm")]).astype(jnp.int32)

    arrived = inbound(pick(ids, clips, cotangent, n_tm, CHUNKS), n_tm)
    results = None
    for chunk, pieces in enumerate(arrived):
        if joined:
            pieces = [jnp.stack(pieces, axis=2).reshape(2, n_clips // CHUNKS, -1, width)]
        results = sublayer(pieces, w_qkv, w_out, chunk, CHUNKS, n_positions, results)
    normed, cot, mixed, dq, dk, dv = results[:6]
    dx = list(results[6:])
    if joined:
        cut = dx[0].reshape(n_clips, n_tm, n_positions, width)
        dx = [cut[:, k] for k in range(n_tm)]

    halves = ([normed], [dq, dk]), ([normed, mixed], [dv, cot])
    sent_first = products(ids, 1, n_x, n_z, *halves[0])
    first = swap(sent_first, "clip", n_clip_devices, 1)
    sent_second = products(ids, 1, n_x, n_z, *after(halves[1], sent_first))
    second = swap(sent_second, "clip", n_clip_devices, 1)
    dx = after(dx, sent_second)
    back = {}
    for k in range(n_tm - 1, 1, -1):
        block = dx[k] if k + 3 >= n_tm else after(dx[k], back[k + 3])
        back[k] = swap(block, "tm", n_tm, k)
    own_first = products(ids, 0, n_x, n_z, *after(halves[0], sent_second))
    own_second = products(ids, 0, n_x, n_z, *after(halves[1], own_first))

    sent, own_first = halve(ids, (own_first, first), 0, 0, CORES)
    first = swap(sent, "clip", n_clip_devices, CORES)
    sent, own_second = halve(ids, (own_second, second), 2, 1, 1)
    second = swap(sent, "tm", n_tm, 1)
    first, second = after((first, second), back)
    sent, own_first = halve(ids, (own_first, first), 1, 1, 1)
    first = swap(sent, "tm", n_tm, 1)
    sent, own_second = halve(ids, (own_second, second), 0, 0, CORES)
    second = swap(sent, "clip", n_clip_devices, CORES)
    total, *sent = join(ids, (own_first, first), (own_second, second), n_z)
    others = [swap(block, "tm", n_tm, (j + 1) * N_Y) for j, block in enumerate(sent)]
    back[0] = dx[0]
    back[1] = swap(after(dx[1], sent), "tm", n_tm, 1)
    grad_clips = place(ids, [back[k] for k in range(n_tm)]).reshape(clips.shape)
    grad_qkv, grad_out = finish((total, *others))
    return (grad_clips, grad_qkv, grad_out)


def solution(mesh):
    return jax.shard_map(
        functools.partial(shards, mesh.shape["clip"], mesh.shape["tm"]),
        mesh=mesh,
        in_specs=(P("clip", "tm", None, None), P(), P(), P("clip", "tm", None, None)),
        out_specs=(P("clip", "tm", None, None), P(("clip", "tm"), None), P(("clip", "tm"), None)),
        check_vma=False,
    )
```

```python
import functools
import itertools

import jax
import jax.numpy as jnp
from jax import lax
from jax.experimental import pallas as pl
from jax.experimental.pallas import tpu as pltpu
from jax.sharding import PartitionSpec as P

HEADS = 16
GROUP = 4
CHUNKS = 2
CORES = 2
N_Y = 2
EPSILON = 1e-06
LOWEST = -1e30
MIB = 1024 * 1024


def contract(left, right, dims):
    return lax.dot_general(left, right, (dims, ((), ())), preferred_element_type=jnp.float32)


def statistics(rows32):
    mean = jnp.mean(rows32, axis=-1, keepdims=True)
    centred = rows32 - mean
    inverse = lax.rsqrt(jnp.mean(centred * centred, axis=-1, keepdims=True) + EPSILON)
    return centred * inverse, inverse


def pick_kernel(n_slots, n_chunks, n_clips, ids_ref, x_ref, cot_ref, *out_refs):
    clip = pl.program_id(0)
    half = n_slots // 2
    for slot in range(half):
        out_refs[slot][0, 0] = x_ref[0, ids_ref[1] ^ slot]
        out_refs[slot][1, 0] = cot_ref[0, ids_ref[1] ^ slot]
    for chunk in range(n_chunks):

        @pl.when(clip // (n_clips // n_chunks) == chunk)
        def _():
            for slot in range(half, n_slots):
                out = out_refs[chunk * half + slot]
                out[0, 0] = x_ref[0, ids_ref[1] ^ slot]
                out[1, 0] = cot_ref[0, ids_ref[1] ^ slot]


def pick(ids, clips, cotangent, n_slots, n_chunks):
    n_clips, _, n_patches, width = clips.shape
    n_positions = n_patches // n_slots
    cut = (n_clips, n_slots, n_positions, width)
    half, depth = n_slots // 2, n_clips // n_chunks

    def block(index):
        return pl.BlockSpec((2, 1, n_positions, width), lambda c: (0, index(c), 0, 0))

    def piece(count):
        return jax.ShapeDtypeStruct((2, count, n_positions, width), clips.dtype)

    out = pl.pallas_call(
        functools.partial(pick_kernel, n_slots, n_chunks, n_clips),
        grid=(n_clips,),
        out_shape=[piece(n_clips)] * half + [piece(depth)] * (half * n_chunks),
        in_specs=[pl.BlockSpec(memory_space=pltpu.SMEM)]
        + [pl.BlockSpec((1,) + cut[1:], lambda c: (c, 0, 0, 0))] * 2,
        out_specs=[block(lambda c: c)] * half
        + [
            block(lambda c, chunk=chunk: jnp.clip(c - chunk * depth, 0, depth - 1))
            for chunk in range(n_chunks)
            for _ in range(half)
        ],
        compiler_params=pltpu.CompilerParams(vmem_limit_bytes=12 * MIB),
    )(ids, clips.reshape(cut), cotangent.reshape(cut))
    far = [out[half + chunk * half :][:half] for chunk in range(n_chunks)]
    return out[:half], far


def place_kernel(ids_ref, *refs):
    for slot, ref in enumerate(refs[:-1]):
        refs[-1][:, ids_ref[1] ^ slot] = ref[...]


def place(ids, blocks):
    n_clips, n_positions, width = blocks[0].shape
    return pl.pallas_call(
        place_kernel,
        out_shape=jax.ShapeDtypeStruct((n_clips, len(blocks), n_positions, width), blocks[0].dtype),
        in_specs=[pl.BlockSpec(memory_space=pltpu.SMEM)]
        + [pl.BlockSpec(memory_space=pltpu.VMEM)] * len(blocks),
        out_specs=pl.BlockSpec(memory_space=pltpu.VMEM),
        compiler_params=pltpu.CompilerParams(vmem_limit_bytes=8 * MIB),
    )(ids, *blocks)


def product_kernel(n_x, flip, n_lefts, ids_ref, *refs):
    lefts, rights, out_ref = refs[:n_lefts], refs[n_lefts:-1], refs[-1]
    width = lefts[0].shape[1]
    rest = width // (CORES * n_x)
    core = lax.rem(ids_ref[0], CORES) ^ flip
    cut = out_ref.shape[1:4]
    for x in range(n_x):
        columns = pl.ds(pl.multiple_of((CORES * x + core) * rest, rest), rest)
        turned = [left[:, columns].T for left in lefts]
        for i, right in enumerate(rights):
            product = contract(turned[min(i, n_lefts - 1)], right[...], ((1,), (0,)))
            product = product.reshape(cut + (width,)).astype(jnp.bfloat16)
            out_ref[x, :, :, :, pl.ds(i * width, width)] = product


def products(ids, flip, n_x, n_z, lefts, rights):
    rows, width = rights[0].shape
    rest = width // (CORES * n_x * n_z * N_Y)
    return pl.pallas_call(
        functools.partial(product_kernel, n_x, flip, len(lefts)),
        out_shape=jax.ShapeDtypeStruct((n_x, n_z, N_Y, rest, len(rights) * width), jnp.bfloat16),
        in_specs=[pl.BlockSpec(memory_space=pltpu.SMEM)]
        + [pl.BlockSpec(memory_space=pltpu.VMEM)] * (len(lefts) + len(rights)),
        out_specs=pl.BlockSpec(memory_space=pltpu.VMEM),
        compiler_params=pltpu.CompilerParams(vmem_limit_bytes=20 * MIB),
        cost_estimate=pl.CostEstimate(
            flops=2 * rows * width * width,
            bytes_accessed=8 * rows * width + 2 * width * width,
            transcendentals=0,
        ),
    )(ids, *lefts, *rights)


def summed(refs, index):
    total = refs[0][index].astype(jnp.float32)
    for ref in refs[1:]:
        total += ref[index].astype(jnp.float32)
    return total


def halve_kernel(dim, axis, stride, ids_ref, *refs):
    addends, sent_ref, kept_ref = refs[:-2], refs[-2], refs[-1]
    me = lax.rem(lax.div(ids_ref[axis], stride), 2)
    for index in itertools.product(*(range(n) for n in sent_ref.shape[:-2])):
        sent_ref[index] = summed(addends, index[:dim] + (me ^ 1,) + index[dim:]).astype(jnp.bfloat16)
    for index in itertools.product(*(range(n) for n in sent_ref.shape[:-2])):
        kept_ref[index] = summed(addends, index[:dim] + (me,) + index[dim:])


def halve(ids, addends, dim, axis, stride):
    shape = addends[0].shape[:dim] + addends[0].shape[dim + 1 :]
    return pl.pallas_call(
        functools.partial(halve_kernel, dim, axis, stride),
        out_shape=[jax.ShapeDtypeStruct(shape, jnp.bfloat16), jax.ShapeDtypeStruct(shape, jnp.float32)],
        in_specs=[pl.BlockSpec(memory_space=pltpu.SMEM)]
        + [pl.BlockSpec(memory_space=pltpu.VMEM)] * len(addends),
        out_specs=[pl.BlockSpec(memory_space=pltpu.VMEM)] * 2,
        compiler_params=pltpu.CompilerParams(vmem_limit_bytes=16 * MIB),
    )(ids, *addends)


def join_kernel(n_z, n_first, ids_ref, *refs):
    addends, outs = refs[:-n_z], refs[-n_z:]
    me = lax.div(ids_ref[1], N_Y)
    half = addends[0].shape[-1]
    for j in [*range(1, n_z), 0]:
        for side, part in enumerate((addends[:n_first], addends[n_first:])):
            total = summed(part, (me ^ j,))
            outs[j][:, pl.ds(side * half, half)] = total.astype(outs[j].dtype)


def join(ids, first, second, n_z):
    rows, half = first[0].shape[1:]
    own = jax.ShapeDtypeStruct((rows, 2 * half), jnp.float32)
    other = jax.ShapeDtypeStruct((rows, 2 * half), jnp.bfloat16)
    return pl.pallas_call(
        functools.partial(join_kernel, n_z, len(first)),
        out_shape=[own] + [other] * (n_z - 1),
        in_specs=[pl.BlockSpec(memory_space=pltpu.SMEM)]
        + [pl.BlockSpec(memory_space=pltpu.VMEM)] * (len(first) + len(second)),
        out_specs=[pl.BlockSpec(memory_space=pltpu.VMEM)] * n_z,
        compiler_params=pltpu.CompilerParams(vmem_limit_bytes=12 * MIB),
    )(ids, *first, *second)


def finish_kernel(*refs):
    addends, (grad_qkv_ref, grad_out_ref) = refs[:-2], refs[-2:]
    wide = grad_qkv_ref.shape[1]
    everything = slice(None)
    grad_qkv_ref[...] = summed(addends, (everything, pl.ds(0, wide)))
    grad_out_ref[...] = summed(addends, (everything, pl.ds(wide, grad_out_ref.shape[1])))


def finish(addends):
    rows, columns = addends[0].shape
    return pl.pallas_call(
        finish_kernel,
        out_shape=[
            jax.ShapeDtypeStruct((rows, columns // 4 * 3), jnp.float32),
            jax.ShapeDtypeStruct((rows, columns // 4), jnp.float32),
        ],
        in_specs=[pl.BlockSpec(memory_space=pltpu.VMEM)] * len(addends),
        out_specs=[pl.BlockSpec(memory_space=pltpu.VMEM)] * 2,
        compiler_params=pltpu.CompilerParams(vmem_limit_bytes=8 * MIB),
    )(*addends)


def sublayer_kernel(n_clips, n_positions, n_pieces, n_aliased, *refs):
    pieces, refs = refs[:n_pieces], refs[n_pieces:]
    wq_ref, wk_ref, wv_ref, wo_ref = refs[:4]
    refs = refs[4 + n_aliased :]
    normed_ref, cot_ref, mixed_ref, dq_ref, dk_ref, dv_ref = refs[:6]
    dx_refs, total_ref = refs[6:-1], refs[-1]
    step = pl.program_id(0)
    rows = normed_ref.shape[0] // n_clips
    span = rows // n_pieces
    wide = wo_ref.shape[0]
    depth = wide // GROUP
    scaling = depth**-0.5

    def raw_rows():
        return jnp.concatenate(
            [pieces[k][0, clip] for clip in range(n_clips) for k in range(n_pieces)], axis=0
        ).astype(jnp.float32)

    @pl.when(step == 0)
    def _():
        unit, _ = statistics(raw_rows())
        normed_ref[...] = unit.astype(jnp.bfloat16)
        for clip in range(n_clips):
            for k in range(n_pieces):
                cot_ref[pl.ds(clip * rows + k * span, span)] = pieces[k][1, clip]

    normed = normed_ref[...]
    all_queries = contract(normed, wq_ref[...], ((1,), (0,))).astype(jnp.bfloat16)
    all_keys = contract(normed, wk_ref[...], ((1,), (0,))).astype(jnp.bfloat16)
    all_values = contract(normed, wv_ref[...], ((1,), (0,))).astype(jnp.bfloat16)
    mixed_grad = contract(cot_ref[...], wo_ref[...], ((1,), (1,))).astype(jnp.bfloat16)

    lane_head = lax.broadcasted_iota(jnp.int32, (rows, wide), 1) // depth
    head_masks = [(lane_head == h).astype(jnp.float32).astype(jnp.bfloat16) for h in range(GROUP)]
    key_pos = lax.broadcasted_iota(jnp.int32, (rows, rows), 0) % n_positions
    query_pos = lax.broadcasted_iota(jnp.int32, (rows, rows), 1) % n_positions
    same = (key_pos == query_pos)[None]

    def stacked(block):
        return jnp.concatenate([block * mask for mask in head_masks], axis=0)

    def side_by_side(blocks):
        return jnp.concatenate([blocks[h] for h in range(GROUP)], axis=1)

    for clip in range(n_clips):
        here = slice(clip * rows, (clip + 1) * rows)
        queries = all_queries[here]
        keys = stacked(all_keys[here])
        values = stacked(all_values[here])
        upstream = mixed_grad[here]
        scores = contract(keys, queries, ((1,), (1,))).reshape(GROUP, rows, rows)
        scores = jnp.where(same, scores * scaling, LOWEST)
        expo = jnp.exp(scores - jnp.max(scores, axis=1, keepdims=True))
        full = expo * (1.0 / jnp.sum(expo, axis=1, keepdims=True))
        low = full.astype(jnp.bfloat16)
        dots = contract(values, upstream, ((1,), (1,))).reshape(GROUP, rows, rows)
        score_grad = full * (dots - jnp.sum(full * dots, axis=1, keepdims=True))
        score_grad = (score_grad * scaling).astype(jnp.bfloat16)
        mixed = contract(low.reshape(GROUP * rows, rows), values, ((0,), (0,)))
        mixed_ref[here] = mixed.astype(jnp.bfloat16)
        dq = contract(score_grad.reshape(GROUP * rows, rows), keys, ((0,), (0,)))
        dq_ref[here] = dq.astype(jnp.bfloat16)
        dk = contract(side_by_side(score_grad), stacked(queries), ((1,), (0,)))
        dk_ref[here] = dk.astype(jnp.bfloat16)
        dv = contract(side_by_side(low), stacked(upstream), ((1,), (0,)))
        dv_ref[here] = dv.astype(jnp.bfloat16)

    part = contract(dq_ref[...], wq_ref[...], ((1,), (1,)))
    part += contract(dk_ref[...], wk_ref[...], ((1,), (1,)))
    part += contract(dv_ref[...], wv_ref[...], ((1,), (1,)))

    @pl.when(step == 0)
    def _():
        total_ref[...] = part

    @pl.when(step > 0)
    def _():
        total_ref[...] += part

    @pl.when(step == pl.num_programs(0) - 1)
    def _():
        unit, inverse = statistics(raw_rows())
        total = total_ref[...]
        grad = inverse * (
            total
            - jnp.mean(total, axis=-1, keepdims=True)
            - unit * jnp.mean(total * unit, axis=-1, keepdims=True)
        )
        dx = (cot_ref[...].astype(jnp.float32) + grad).astype(jnp.bfloat16)
        for clip in range(n_clips):
            for k in range(n_pieces):
                start = clip * rows + k * span
                dx_refs[k][clip] = dx[start : start + span]


def sublayer(pieces, n_clips, w_qkv, w_out, chunk, n_chunks, n_positions, before):
    n_pieces = len(pieces)
    _, _, span, width = pieces[0].shape
    rows = n_clips * n_pieces * span
    groups = HEADS // GROUP
    wide = width // groups

    flat = jax.ShapeDtypeStruct((n_chunks * rows, width), jnp.bfloat16)
    dx = jax.ShapeDtypeStruct((n_chunks * n_clips, span, width), jnp.bfloat16)
    out_shape = [flat] * 6 + [dx] * n_pieces
    aliased = [] if before is None else list(before)
    first = n_pieces + 4
    return pl.pallas_call(
        functools.partial(sublayer_kernel, n_clips, n_positions, n_pieces, len(aliased)),
        grid=(groups,),
        out_shape=out_shape,
        in_specs=[
            pl.BlockSpec(
                (2, n_clips, span, width),
                lambda j, i=chunk if piece.shape[1] > n_clips else 0: (0, i, 0, 0),
            )
            for piece in pieces
        ]
        + [pl.BlockSpec((width, wide), lambda j, i=i: (0, i * groups + j)) for i in range(3)]
        + [pl.BlockSpec((wide, width), lambda j: (j, 0))]
        + [pl.BlockSpec(memory_space=pl.ANY)] * len(aliased),
        out_specs=[
            pl.BlockSpec((rows, width), lambda j: (chunk, 0)),
            pl.BlockSpec((rows, width), lambda j: (chunk, 0)),
        ]
        + [pl.BlockSpec((rows, wide), lambda j: (chunk, j))] * 4
        + [pl.BlockSpec((n_clips, span, width), lambda j: (chunk, 0, 0))] * n_pieces,
        scratch_shapes=[pltpu.VMEM((rows, width), jnp.float32)],
        input_output_aliases={first + i: i for i in range(len(aliased))},
        compiler_params=pltpu.CompilerParams(vmem_limit_bytes=50 * MIB),
        cost_estimate=pl.CostEstimate(
            flops=2 * rows * width * (7 * width + 24 * 128),
            bytes_accessed=16 * rows * width + 8 * width * width,
            transcendentals=rows * 128 * HEADS,
        ),
    )(*pieces, w_qkv, w_qkv, w_qkv, w_out, *aliased)


def swap(block, axis, size, distance):
    return lax.ppermute(block, axis, [(i, i ^ distance) for i in range(size)])


def after(values, done):
    values, _ = lax.optimization_barrier((values, done))
    return values


def inbound(near, far, n_tm):
    half = n_tm // 2
    near = [near[0]] + [swap(near[k], "tm", n_tm, k) for k in range(1, half)]
    gates = [near[i + 1] if i < half // 2 else None for i in range(half)]
    arrived = []
    for blocks in far:
        blocks = [block if gate is None else after(block, gate) for block, gate in zip(blocks, gates)]
        gates = [swap(block, "tm", n_tm, half + i) for i, block in enumerate(blocks)]
        arrived.append(gates)
    return near, arrived


def shards(n_clip_devices, n_tm, clips, w_qkv, w_out, cotangent):
    n_clips, _, n_patches, width = clips.shape
    n_positions = n_patches // n_tm
    n_x, n_z = n_clip_devices // CORES, n_tm // N_Y
    joined = n_positions % 16 != 0
    ids = jnp.stack([lax.axis_index("clip"), lax.axis_index("tm")]).astype(jnp.int32)

    near, far = inbound(*pick(ids, clips, cotangent, n_tm, CHUNKS), n_tm)
    depth = n_clips // CHUNKS
    results = None
    for chunk in range(CHUNKS):
        pieces = near + far[chunk]
        if joined:
            pieces = [p[:, chunk * depth :][:, :depth] for p in near] + far[chunk]
            pieces = [jnp.stack(pieces, axis=2).reshape(2, depth, -1, width)]
        results = sublayer(pieces, depth, w_qkv, w_out, chunk, CHUNKS, n_positions, results)
    normed, cot, mixed, dq, dk, dv = results[:6]
    dx = list(results[6:])
    if joined:
        cut = dx[0].reshape(n_clips, n_tm, n_positions, width)
        dx = [cut[:, k] for k in range(n_tm)]

    halves = ([normed], [dq, dk]), ([normed, mixed], [dv, cot])
    sent_first = products(ids, 1, n_x, n_z, *halves[0])
    first = swap(sent_first, "clip", n_clip_devices, 1)
    sent_second = products(ids, 1, n_x, n_z, *after(halves[1], sent_first))
    second = swap(sent_second, "clip", n_clip_devices, 1)
    dx = after(dx, sent_second)
    back = {}
    for k in range(n_tm - 1, 1, -1):
        block = dx[k] if k + 3 >= n_tm else after(dx[k], back[k + 3])
        back[k] = swap(block, "tm", n_tm, k)
    own_first = products(ids, 0, n_x, n_z, *after(halves[0], sent_second))
    own_second = products(ids, 0, n_x, n_z, *after(halves[1], own_first))

    sent, own_first = halve(ids, (own_first, first), 0, 0, CORES)
    first = swap(sent, "clip", n_clip_devices, CORES)
    sent, own_second = halve(ids, (own_second, second), 2, 1, 1)
    second = swap(sent, "tm", n_tm, 1)
    first, second = after((first, second), back)
    sent, own_first = halve(ids, (own_first, first), 1, 1, 1)
    first = swap(sent, "tm", n_tm, 1)
    sent, own_second = halve(ids, (own_second, second), 0, 0, CORES)
    second = swap(sent, "clip", n_clip_devices, CORES)
    total, *sent = join(ids, (own_first, first), (own_second, second), n_z)
    others = [swap(block, "tm", n_tm, (j + 1) * N_Y) for j, block in enumerate(sent)]
    back[0] = dx[0]
    back[1] = swap(after(dx[1], sent), "tm", n_tm, 1)
    grad_clips = place(ids, [back[k] for k in range(n_tm)]).reshape(clips.shape)
    grad_qkv, grad_out = finish((total, *others))
    return (grad_clips, grad_qkv, grad_out)


def solution(mesh):
    return jax.shard_map(
        functools.partial(shards, mesh.shape["clip"], mesh.shape["tm"]),
        mesh=mesh,
        in_specs=(P("clip", "tm", None, None), P(), P(), P("clip", "tm", None, None)),
        out_specs=(P("clip", "tm", None, None), P(("clip", "tm"), None), P(("clip", "tm"), None)),
        check_vma=False,
    )
```

```python
import functools
import itertools

import jax
import jax.numpy as jnp
from jax import lax
from jax.experimental import pallas as pl
from jax.experimental.pallas import tpu as pltpu
from jax.sharding import PartitionSpec as P

HEADS = 16
GROUP = 4
CHUNKS = 2
CORES = 2
N_Y = 2
EPSILON = 1e-06
LOWEST = -1e30
MIB = 1024 * 1024


def contract(left, right, dims):
    return lax.dot_general(left, right, (dims, ((), ())), preferred_element_type=jnp.float32)


def statistics(rows32):
    mean = jnp.mean(rows32, axis=-1, keepdims=True)
    centred = rows32 - mean
    inverse = lax.rsqrt(jnp.mean(centred * centred, axis=-1, keepdims=True) + EPSILON)
    return centred * inverse, inverse


def pick_kernel(n_slots, n_chunks, ids_ref, x_ref, cot_ref, near_ref, *far_refs):
    half = n_slots // 2
    base = ids_ref[1] - lax.rem(ids_ref[1], half)
    for j in range(half):
        near_ref[j, 0] = x_ref[:, base + j]
        near_ref[j, 1] = cot_ref[:, base + j]
    depth = x_ref.shape[0] // n_chunks
    for i, ref in enumerate(far_refs):
        here = pl.ds(i // half * depth, depth)
        slot = ids_ref[1] ^ (half + i % half)
        ref[0] = x_ref[here, slot]
        ref[1] = cot_ref[here, slot]


def pick(ids, clips, cotangent, n_slots, n_chunks):
    n_clips, _, n_patches, width = clips.shape
    cut = (n_clips, n_slots, n_patches // n_slots, width)
    half = n_slots // 2
    near = jax.ShapeDtypeStruct((half, 2, n_clips) + cut[2:], clips.dtype)
    far = jax.ShapeDtypeStruct((2, n_clips // n_chunks) + cut[2:], clips.dtype)
    near, *far = pl.pallas_call(
        functools.partial(pick_kernel, n_slots, n_chunks),
        out_shape=[near] + [far] * (half * n_chunks),
        in_specs=[pl.BlockSpec(memory_space=pltpu.SMEM)]
        + [pl.BlockSpec(memory_space=pltpu.VMEM)] * 2,
        out_specs=[pl.BlockSpec(memory_space=pltpu.VMEM)] * (1 + half * n_chunks),
        compiler_params=pltpu.CompilerParams(vmem_limit_bytes=12 * MIB),
    )(ids, clips.reshape(cut), cotangent.reshape(cut))
    return near, [far[chunk * half :][:half] for chunk in range(n_chunks)]


def place_kernel(ids_ref, near_ref, *refs):
    half = len(refs) - 1
    base = ids_ref[1] - lax.rem(ids_ref[1], half)
    for i in range(half):
        refs[-1][:, base + i] = near_ref[i]
        refs[-1][:, ids_ref[1] ^ (half + i)] = refs[i][...]


def place(ids, near, far):
    half, n_clips, n_positions, width = near.shape
    return pl.pallas_call(
        place_kernel,
        out_shape=jax.ShapeDtypeStruct((n_clips, 2 * half, n_positions, width), near.dtype),
        in_specs=[pl.BlockSpec(memory_space=pltpu.SMEM)]
        + [pl.BlockSpec(memory_space=pltpu.VMEM)] * (1 + half),
        out_specs=pl.BlockSpec(memory_space=pltpu.VMEM),
        compiler_params=pltpu.CompilerParams(vmem_limit_bytes=8 * MIB),
    )(ids, near, *far)


def product_kernel(n_x, flip, n_lefts, ids_ref, *refs):
    lefts, rights, out_ref = refs[:n_lefts], refs[n_lefts:-1], refs[-1]
    width = lefts[0].shape[1]
    rest = width // (CORES * n_x)
    core = lax.rem(ids_ref[0], CORES) ^ flip
    cut = out_ref.shape[1:4]
    for x in range(n_x):
        columns = pl.ds(pl.multiple_of((CORES * x + core) * rest, rest), rest)
        turned = [left[:, columns].T for left in lefts]
        for i, right in enumerate(rights):
            product = contract(turned[min(i, n_lefts - 1)], right[...], ((1,), (0,)))
            product = product.reshape(cut + (width,)).astype(jnp.bfloat16)
            out_ref[x, :, :, :, pl.ds(i * width, width)] = product


def products(ids, flip, n_x, n_z, lefts, rights):
    rows, width = rights[0].shape
    rest = width // (CORES * n_x * n_z * N_Y)
    return pl.pallas_call(
        functools.partial(product_kernel, n_x, flip, len(lefts)),
        out_shape=jax.ShapeDtypeStruct((n_x, n_z, N_Y, rest, len(rights) * width), jnp.bfloat16),
        in_specs=[pl.BlockSpec(memory_space=pltpu.SMEM)]
        + [pl.BlockSpec(memory_space=pltpu.VMEM)] * (len(lefts) + len(rights)),
        out_specs=pl.BlockSpec(memory_space=pltpu.VMEM),
        compiler_params=pltpu.CompilerParams(vmem_limit_bytes=20 * MIB),
        cost_estimate=pl.CostEstimate(
            flops=2 * rows * width * width,
            bytes_accessed=8 * rows * width + 2 * width * width,
            transcendentals=0,
        ),
    )(ids, *lefts, *rights)


def summed(refs, index):
    total = refs[0][index].astype(jnp.float32)
    for ref in refs[1:]:
        total += ref[index].astype(jnp.float32)
    return total


def halve_kernel(dim, axis, stride, ids_ref, *refs):
    addends, sent_ref, kept_ref = refs[:-2], refs[-2], refs[-1]
    me = lax.rem(lax.div(ids_ref[axis], stride), 2)
    for index in itertools.product(*(range(n) for n in sent_ref.shape[:-2])):
        sent_ref[index] = summed(addends, index[:dim] + (me ^ 1,) + index[dim:]).astype(jnp.bfloat16)
    for index in itertools.product(*(range(n) for n in sent_ref.shape[:-2])):
        kept_ref[index] = summed(addends, index[:dim] + (me,) + index[dim:])


def halve(ids, addends, dim, axis, stride):
    shape = addends[0].shape[:dim] + addends[0].shape[dim + 1 :]
    return pl.pallas_call(
        functools.partial(halve_kernel, dim, axis, stride),
        out_shape=[jax.ShapeDtypeStruct(shape, jnp.bfloat16), jax.ShapeDtypeStruct(shape, jnp.float32)],
        in_specs=[pl.BlockSpec(memory_space=pltpu.SMEM)]
        + [pl.BlockSpec(memory_space=pltpu.VMEM)] * len(addends),
        out_specs=[pl.BlockSpec(memory_space=pltpu.VMEM)] * 2,
        compiler_params=pltpu.CompilerParams(vmem_limit_bytes=16 * MIB),
    )(ids, *addends)


def join_kernel(n_z, n_first, ids_ref, *refs):
    addends, outs = refs[:-n_z], refs[-n_z:]
    me = lax.div(ids_ref[1], N_Y)
    half = addends[0].shape[-1]
    for j in [*range(1, n_z), 0]:
        for side, part in enumerate((addends[:n_first], addends[n_first:])):
            total = summed(part, (me ^ j,))
            outs[j][:, pl.ds(side * half, half)] = total.astype(outs[j].dtype)


def join(ids, first, second, n_z):
    rows, half = first[0].shape[1:]
    own = jax.ShapeDtypeStruct((rows, 2 * half), jnp.float32)
    other = jax.ShapeDtypeStruct((rows, 2 * half), jnp.bfloat16)
    return pl.pallas_call(
        functools.partial(join_kernel, n_z, len(first)),
        out_shape=[own] + [other] * (n_z - 1),
        in_specs=[pl.BlockSpec(memory_space=pltpu.SMEM)]
        + [pl.BlockSpec(memory_space=pltpu.VMEM)] * (len(first) + len(second)),
        out_specs=[pl.BlockSpec(memory_space=pltpu.VMEM)] * n_z,
        compiler_params=pltpu.CompilerParams(vmem_limit_bytes=12 * MIB),
    )(ids, *first, *second)


def finish_kernel(*refs):
    addends, (grad_qkv_ref, grad_out_ref) = refs[:-2], refs[-2:]
    wide = grad_qkv_ref.shape[1]
    everything = slice(None)
    grad_qkv_ref[...] = summed(addends, (everything, pl.ds(0, wide)))
    grad_out_ref[...] = summed(addends, (everything, pl.ds(wide, grad_out_ref.shape[1])))


def finish(addends):
    rows, columns = addends[0].shape
    return pl.pallas_call(
        finish_kernel,
        out_shape=[
            jax.ShapeDtypeStruct((rows, columns // 4 * 3), jnp.float32),
            jax.ShapeDtypeStruct((rows, columns // 4), jnp.float32),
        ],
        in_specs=[pl.BlockSpec(memory_space=pltpu.VMEM)] * len(addends),
        out_specs=[pl.BlockSpec(memory_space=pltpu.VMEM)] * 2,
        compiler_params=pltpu.CompilerParams(vmem_limit_bytes=8 * MIB),
    )(*addends)


def sublayer_kernel(n_clips, n_positions, n_far, n_aliased, near_ref, *refs):
    far_refs, refs = refs[:n_far], refs[n_far:]
    wq_ref, wk_ref, wv_ref, wo_ref = refs[:4]
    refs = refs[4 + n_aliased :]
    normed_ref, cot_ref, mixed_ref, dq_ref, dk_ref, dv_ref = refs[:6]
    dx_refs, total_ref = refs[6:-1], refs[-1]
    n_near = near_ref.shape[0]
    n_pieces = n_near + n_far
    step = pl.program_id(0)
    rows = normed_ref.shape[0] // n_clips
    span = rows // n_pieces
    wide = wo_ref.shape[0]
    depth = wide // GROUP
    scaling = depth**-0.5

    def piece(k, which, clip):
        return near_ref[k, which, clip] if k < n_near else far_refs[k - n_near][which, clip]

    def raw_rows():
        return jnp.concatenate(
            [piece(k, 0, clip) for clip in range(n_clips) for k in range(n_pieces)], axis=0
        ).astype(jnp.float32)

    @pl.when(step == 0)
    def _():
        unit, _ = statistics(raw_rows())
        normed_ref[...] = unit.astype(jnp.bfloat16)
        for clip in range(n_clips):
            for k in range(n_pieces):
                cot_ref[pl.ds(clip * rows + k * span, span)] = piece(k, 1, clip)

    normed = normed_ref[...]
    all_queries = contract(normed, wq_ref[...], ((1,), (0,))).astype(jnp.bfloat16)
    all_keys = contract(normed, wk_ref[...], ((1,), (0,))).astype(jnp.bfloat16)
    all_values = contract(normed, wv_ref[...], ((1,), (0,))).astype(jnp.bfloat16)
    mixed_grad = contract(cot_ref[...], wo_ref[...], ((1,), (1,))).astype(jnp.bfloat16)

    lane_head = lax.broadcasted_iota(jnp.int32, (rows, wide), 1) // depth
    head_masks = [(lane_head == h).astype(jnp.float32).astype(jnp.bfloat16) for h in range(GROUP)]
    key_pos = lax.broadcasted_iota(jnp.int32, (rows, rows), 0) % n_positions
    query_pos = lax.broadcasted_iota(jnp.int32, (rows, rows), 1) % n_positions
    same = (key_pos == query_pos)[None]

    def stacked(block):
        return jnp.concatenate([block * mask for mask in head_masks], axis=0)

    def side_by_side(blocks):
        return jnp.concatenate([blocks[h] for h in range(GROUP)], axis=1)

    for clip in range(n_clips):
        here = slice(clip * rows, (clip + 1) * rows)
        queries = all_queries[here]
        keys = stacked(all_keys[here])
        values = stacked(all_values[here])
        upstream = mixed_grad[here]
        scores = contract(keys, queries, ((1,), (1,))).reshape(GROUP, rows, rows)
        scores = jnp.where(same, scores * scaling, LOWEST)
        expo = jnp.exp(scores - jnp.max(scores, axis=1, keepdims=True))
        full = expo * (1.0 / jnp.sum(expo, axis=1, keepdims=True))
        low = full.astype(jnp.bfloat16)
        dots = contract(values, upstream, ((1,), (1,))).reshape(GROUP, rows, rows)
        score_grad = full * (dots - jnp.sum(full * dots, axis=1, keepdims=True))
        score_grad = (score_grad * scaling).astype(jnp.bfloat16)
        mixed = contract(low.reshape(GROUP * rows, rows), values, ((0,), (0,)))
        mixed_ref[here] = mixed.astype(jnp.bfloat16)
        dq = contract(score_grad.reshape(GROUP * rows, rows), keys, ((0,), (0,)))
        dq_ref[here] = dq.astype(jnp.bfloat16)
        dk = contract(side_by_side(score_grad), stacked(queries), ((1,), (0,)))
        dk_ref[here] = dk.astype(jnp.bfloat16)
        dv = contract(side_by_side(low), stacked(upstream), ((1,), (0,)))
        dv_ref[here] = dv.astype(jnp.bfloat16)

    part = contract(dq_ref[...], wq_ref[...], ((1,), (1,)))
    part += contract(dk_ref[...], wk_ref[...], ((1,), (1,)))
    part += contract(dv_ref[...], wv_ref[...], ((1,), (1,)))

    @pl.when(step == 0)
    def _():
        total_ref[...] = part

    @pl.when(step > 0)
    def _():
        total_ref[...] += part

    @pl.when(step == pl.num_programs(0) - 1)
    def _():
        unit, inverse = statistics(raw_rows())
        total = total_ref[...]
        grad = inverse * (
            total
            - jnp.mean(total, axis=-1, keepdims=True)
            - unit * jnp.mean(total * unit, axis=-1, keepdims=True)
        )
        dx = (cot_ref[...].astype(jnp.float32) + grad).astype(jnp.bfloat16)
        for clip in range(n_clips):
            for k in range(n_pieces):
                start = clip * rows + k * span
                if k < n_near:
                    dx_refs[0][k, clip] = dx[start : start + span]
                else:
                    dx_refs[1 + k - n_near][clip] = dx[start : start + span]


def sublayer(near, far, n_clips, w_qkv, w_out, chunk, n_chunks, n_positions, before):
    n_near, _, total_clips, span, width = near.shape
    rows = n_clips * (n_near + len(far)) * span
    groups = HEADS // GROUP
    wide = width // groups
    flat = jax.ShapeDtypeStruct((n_chunks * rows, width), jnp.bfloat16)
    dx = jax.ShapeDtypeStruct((n_chunks * n_clips, span, width), jnp.bfloat16)
    dx_near = jax.ShapeDtypeStruct((n_near,) + dx.shape, jnp.bfloat16)
    aliased = [] if before is None else list(before)
    first = len(far) + 5
    at = chunk if total_clips > n_clips else 0
    return pl.pallas_call(
        functools.partial(sublayer_kernel, n_clips, n_positions, len(far), len(aliased)),
        grid=(groups,),
        out_shape=[flat] * 6 + [dx_near] + [dx] * len(far),
        in_specs=[pl.BlockSpec((n_near, 2, n_clips, span, width), lambda j: (0, 0, at, 0, 0))]
        + [pl.BlockSpec(piece.shape, lambda j: (0, 0, 0, 0)) for piece in far]
        + [pl.BlockSpec((width, wide), lambda j, i=i: (0, i * groups + j)) for i in range(3)]
        + [pl.BlockSpec((wide, width), lambda j: (j, 0))]
        + [pl.BlockSpec(memory_space=pl.ANY)] * len(aliased),
        out_specs=[pl.BlockSpec((rows, width), lambda j: (chunk, 0))] * 2
        + [pl.BlockSpec((rows, wide), lambda j: (chunk, j))] * 4
        + [pl.BlockSpec((n_near, n_clips, span, width), lambda j: (0, chunk, 0, 0))]
        + [pl.BlockSpec((n_clips, span, width), lambda j: (chunk, 0, 0))] * len(far),
        scratch_shapes=[pltpu.VMEM((rows, width), jnp.float32)],
        input_output_aliases={first + i: i for i in range(len(aliased))},
        compiler_params=pltpu.CompilerParams(vmem_limit_bytes=28 * MIB),
        cost_estimate=pl.CostEstimate(
            flops=2 * rows * width * (7 * width + 24 * 128),
            bytes_accessed=16 * rows * width + 8 * width * width,
            transcendentals=rows * 128 * HEADS,
        ),
    )(near, *far, w_qkv, w_qkv, w_qkv, w_out, *aliased)


def swap(block, axis, size, distance):
    return lax.ppermute(block, axis, [(i, i ^ distance) for i in range(size)])


def after(values, done):
    values, _ = lax.optimization_barrier((values, done))
    return values


def near_exchange(blocks, n_tm):
    half = n_tm // 2
    groups = [list(range(half)), list(range(half, n_tm))]
    return lax.all_to_all(blocks, "tm", 0, 0, axis_index_groups=groups, tiled=True)


def shards(n_clip_devices, n_tm, clips, w_qkv, w_out, cotangent):
    n_clips, _, n_patches, width = clips.shape
    n_positions = n_patches // n_tm
    n_x, n_z = n_clip_devices // CORES, n_tm // N_Y
    half = n_tm // 2
    depth = n_clips // CHUNKS
    joined = n_positions % 16 != 0
    ids = jnp.stack([lax.axis_index("clip"), lax.axis_index("tm")]).astype(jnp.int32)

    near, blocks = pick(ids, clips, cotangent, n_tm, CHUNKS)
    near = near_exchange(near, n_tm)
    far = []
    for chunk in range(CHUNKS):
        if far:
            blocks[chunk] = [after(block, done) for block, done in zip(blocks[chunk], far[-1])]
        far.append([swap(block, "tm", n_tm, half + i) for i, block in enumerate(blocks[chunk])])
    results = None
    for chunk in range(CHUNKS):
        here, there = near, far[chunk]
        if joined:
            here = near[:, :, chunk * depth :][:, :, :depth]
            here = jnp.concatenate([here, jnp.stack(there)]).transpose(1, 2, 0, 3, 4)
            here, there = here.reshape(1, 2, depth, -1, width), []
        results = sublayer(here, there, depth, w_qkv, w_out, chunk, CHUNKS, n_positions, results)
    normed, cot, mixed, dq, dk, dv = results[:6]
    back_near, *back = results[6:]
    if joined:
        cut = back_near.reshape(n_clips, n_tm, n_positions, width).transpose(1, 0, 2, 3)
        back_near, back = cut[:half], list(cut[half:])

    halves = ([normed], [dq, dk]), ([normed, mixed], [dv, cot])
    sent_second = products(ids, 1, n_x, n_z, *halves[1])
    second = swap(sent_second, "clip", n_clip_devices, 1)
    sent_first = products(ids, 1, n_x, n_z, *after(halves[0], sent_second))
    first = swap(sent_first, "clip", n_clip_devices, 1)
    own_second = products(ids, 0, n_x, n_z, *after(halves[1], sent_first))
    sent, own_second = halve(ids, (own_second, second), 2, 1, 1)
    second = swap(sent, "tm", n_tm, 1)
    own_first = products(ids, 0, n_x, n_z, *after(halves[0], own_second))
    sent, own_first = halve(ids, (own_first, first), 0, 0, CORES)
    first = swap(sent, "clip", n_clip_devices, CORES)
    back_near, back = after((back_near, back), sent_first)
    back = [swap(block, "tm", n_tm, half + i) for i, block in enumerate(back)]
    back_near = near_exchange(back_near, n_tm)
    first, second = after((first, second), (back, back_near))
    sent, own_first = halve(ids, (own_first, first), 1, 1, 1)
    first = swap(sent, "tm", n_tm, 1)
    sent, own_second = halve(ids, (own_second, second), 0, 0, CORES)
    second = swap(sent, "clip", n_clip_devices, CORES)
    total, *sent = join(ids, (own_first, first), (own_second, second), n_z)
    others = [swap(block, "tm", n_tm, (j + 1) * N_Y) for j, block in enumerate(sent)]
    grad_clips = place(ids, back_near, back).reshape(clips.shape)
    grad_qkv, grad_out = finish((total, *others))
    return (grad_clips, grad_qkv, grad_out)


def solution(mesh):
    return jax.shard_map(
        functools.partial(shards, mesh.shape["clip"], mesh.shape["tm"]),
        mesh=mesh,
        in_specs=(P("clip", "tm", None, None), P(), P(), P("clip", "tm", None, None)),
        out_specs=(P("clip", "tm", None, None), P(("clip", "tm"), None), P(("clip", "tm"), None)),
        check_vma=False,
    )
```

```python
import functools
import itertools

import jax
import jax.numpy as jnp
from jax import lax
from jax.experimental import pallas as pl
from jax.experimental.pallas import tpu as pltpu
from jax.sharding import PartitionSpec as P

HEADS = 16
GROUP = 4
STEP = 2
CHUNKS = 2
CORES = 2
N_Y = 2
EPSILON = 1e-06
LOWEST = -1e30
MIB = 1024 * 1024


def contract(left, right, dims):
    return lax.dot_general(left, right, (dims, ((), ())), preferred_element_type=jnp.float32)


def statistics(rows32):
    mean = jnp.mean(rows32, axis=-1, keepdims=True)
    centred = rows32 - mean
    inverse = lax.rsqrt(jnp.mean(centred * centred, axis=-1, keepdims=True) + EPSILON)
    return centred * inverse, inverse


def pick_kernel(n_slots, n_chunks, ids_ref, x_ref, cot_ref, *out_refs):
    half = n_slots // 2
    depth = x_ref.shape[0] // n_chunks
    for i, ref in enumerate(out_refs):
        far = i - half
        here = slice(None) if far < 0 else pl.ds(far // half * depth, depth)
        slot = ids_ref[1] ^ (i if far < 0 else half + far % half)
        ref[0] = x_ref[here, slot]
        ref[1] = cot_ref[here, slot]


def pick(ids, clips, cotangent, n_slots, n_chunks):
    n_clips, _, n_patches, width = clips.shape
    cut = (n_clips, n_slots, n_patches // n_slots, width)
    half = n_slots // 2

    def piece(count):
        return jax.ShapeDtypeStruct((2, count) + cut[2:], clips.dtype)

    out = pl.pallas_call(
        functools.partial(pick_kernel, n_slots, n_chunks),
        out_shape=[piece(n_clips)] * half + [piece(n_clips // n_chunks)] * (half * n_chunks),
        in_specs=[pl.BlockSpec(memory_space=pltpu.SMEM)]
        + [pl.BlockSpec(memory_space=pltpu.VMEM)] * 2,
        out_specs=[pl.BlockSpec(memory_space=pltpu.VMEM)] * (half * (1 + n_chunks)),
        compiler_params=pltpu.CompilerParams(vmem_limit_bytes=12 * MIB),
    )(ids, clips.reshape(cut), cotangent.reshape(cut))
    far = [out[half + chunk * half :][:half] for chunk in range(n_chunks)]
    return out[:half], far


def place_kernel(ids_ref, *refs):
    for slot, ref in enumerate(refs[:-1]):
        refs[-1][:, ids_ref[1] ^ slot] = ref[...]


def place(ids, blocks):
    n_clips, n_positions, width = blocks[0].shape
    return pl.pallas_call(
        place_kernel,
        out_shape=jax.ShapeDtypeStruct((n_clips, len(blocks), n_positions, width), blocks[0].dtype),
        in_specs=[pl.BlockSpec(memory_space=pltpu.SMEM)]
        + [pl.BlockSpec(memory_space=pltpu.VMEM)] * len(blocks),
        out_specs=pl.BlockSpec(memory_space=pltpu.VMEM),
        compiler_params=pltpu.CompilerParams(vmem_limit_bytes=8 * MIB),
    )(ids, *blocks)


def product_kernel(n_x, flip, n_lefts, ids_ref, *refs):
    lefts, rights, out_ref = refs[:n_lefts], refs[n_lefts:-1], refs[-1]
    width = lefts[0].shape[1]
    rest = width // (CORES * n_x)
    core = lax.rem(ids_ref[0], CORES) ^ flip
    cut = out_ref.shape[1:4]
    for x in range(n_x):
        columns = pl.ds(pl.multiple_of((CORES * x + core) * rest, rest), rest)
        turned = [left[:, columns].T for left in lefts]
        for i, right in enumerate(rights):
            product = contract(turned[min(i, n_lefts - 1)], right[...], ((1,), (0,)))
            product = product.reshape(cut + (width,)).astype(jnp.bfloat16)
            out_ref[x, :, :, :, pl.ds(i * width, width)] = product


def products(ids, flip, n_x, n_z, lefts, rights):
    rows, width = rights[0].shape
    rest = width // (CORES * n_x * n_z * N_Y)
    return pl.pallas_call(
        functools.partial(product_kernel, n_x, flip, len(lefts)),
        out_shape=jax.ShapeDtypeStruct((n_x, n_z, N_Y, rest, len(rights) * width), jnp.bfloat16),
        in_specs=[pl.BlockSpec(memory_space=pltpu.SMEM)]
        + [pl.BlockSpec(memory_space=pltpu.VMEM)] * (len(lefts) + len(rights)),
        out_specs=pl.BlockSpec(memory_space=pltpu.VMEM),
        compiler_params=pltpu.CompilerParams(vmem_limit_bytes=20 * MIB),
        cost_estimate=pl.CostEstimate(
            flops=2 * rows * width * width,
            bytes_accessed=8 * rows * width + 2 * width * width,
            transcendentals=0,
        ),
    )(ids, *lefts, *rights)


def summed(refs, index):
    total = refs[0][index].astype(jnp.float32)
    for ref in refs[1:]:
        total += ref[index].astype(jnp.float32)
    return total


def halve_kernel(dim, axis, stride, ids_ref, *refs):
    addends, sent_ref, kept_ref = refs[:-2], refs[-2], refs[-1]
    me = lax.rem(lax.div(ids_ref[axis], stride), 2)
    for index in itertools.product(*(range(n) for n in sent_ref.shape[:-2])):
        sent_ref[index] = summed(addends, index[:dim] + (me ^ 1,) + index[dim:]).astype(jnp.bfloat16)
    for index in itertools.product(*(range(n) for n in sent_ref.shape[:-2])):
        kept_ref[index] = summed(addends, index[:dim] + (me,) + index[dim:])


def halve(ids, addends, dim, axis, stride):
    shape = addends[0].shape[:dim] + addends[0].shape[dim + 1 :]
    return pl.pallas_call(
        functools.partial(halve_kernel, dim, axis, stride),
        out_shape=[jax.ShapeDtypeStruct(shape, jnp.bfloat16), jax.ShapeDtypeStruct(shape, jnp.float32)],
        in_specs=[pl.BlockSpec(memory_space=pltpu.SMEM)]
        + [pl.BlockSpec(memory_space=pltpu.VMEM)] * len(addends),
        out_specs=[pl.BlockSpec(memory_space=pltpu.VMEM)] * 2,
        compiler_params=pltpu.CompilerParams(vmem_limit_bytes=16 * MIB),
    )(ids, *addends)


def join_kernel(n_z, n_first, ids_ref, *refs):
    addends, outs = refs[:-n_z], refs[-n_z:]
    me = lax.div(ids_ref[1], N_Y)
    half = addends[0].shape[-1]
    for j in [*range(1, n_z), 0]:
        for side, part in enumerate((addends[:n_first], addends[n_first:])):
            total = summed(part, (me ^ j,))
            outs[j][:, pl.ds(side * half, half)] = total.astype(outs[j].dtype)


def join(ids, first, second, n_z):
    rows, half = first[0].shape[1:]
    own = jax.ShapeDtypeStruct((rows, 2 * half), jnp.float32)
    other = jax.ShapeDtypeStruct((rows, 2 * half), jnp.bfloat16)
    return pl.pallas_call(
        functools.partial(join_kernel, n_z, len(first)),
        out_shape=[own] + [other] * (n_z - 1),
        in_specs=[pl.BlockSpec(memory_space=pltpu.SMEM)]
        + [pl.BlockSpec(memory_space=pltpu.VMEM)] * (len(first) + len(second)),
        out_specs=[pl.BlockSpec(memory_space=pltpu.VMEM)] * n_z,
        compiler_params=pltpu.CompilerParams(vmem_limit_bytes=12 * MIB),
    )(ids, *first, *second)


def finish_kernel(*refs):
    addends, (grad_qkv_ref, grad_out_ref) = refs[:-2], refs[-2:]
    wide = grad_qkv_ref.shape[1]
    everything = slice(None)
    grad_qkv_ref[...] = summed(addends, (everything, pl.ds(0, wide)))
    grad_out_ref[...] = summed(addends, (everything, pl.ds(wide, grad_out_ref.shape[1])))


def finish(addends):
    rows, columns = addends[0].shape
    return pl.pallas_call(
        finish_kernel,
        out_shape=[
            jax.ShapeDtypeStruct((rows, columns // 4 * 3), jnp.float32),
            jax.ShapeDtypeStruct((rows, columns // 4), jnp.float32),
        ],
        in_specs=[pl.BlockSpec(memory_space=pltpu.VMEM)] * len(addends),
        out_specs=[pl.BlockSpec(memory_space=pltpu.VMEM)] * 2,
        compiler_params=pltpu.CompilerParams(vmem_limit_bytes=8 * MIB),
    )(*addends)


def sublayer_kernel(n_clips, n_positions, n_pieces, n_aliased, *refs):
    pieces, refs = refs[:n_pieces], refs[n_pieces:]
    wq_ref, wk_ref, wv_ref, wo_ref = refs[:4]
    refs = refs[4 + n_aliased :]
    normed_ref, cot_ref, mixed_ref, dq_ref, dk_ref, dv_ref = refs[:6]
    dx_refs, total_ref = refs[6:-1], refs[-1]
    step = pl.program_id(0)
    rows = normed_ref.shape[0] // n_clips
    span = rows // n_pieces
    step_wide = wo_ref.shape[0]
    wide = step_wide // STEP
    depth = wide // GROUP
    scaling = depth**-0.5

    def raw_rows():
        return jnp.concatenate(
            [pieces[k][0, clip] for clip in range(n_clips) for k in range(n_pieces)], axis=0
        ).astype(jnp.float32)

    @pl.when(step == 0)
    def _():
        unit, _ = statistics(raw_rows())
        normed_ref[...] = unit.astype(jnp.bfloat16)
        for clip in range(n_clips):
            for k in range(n_pieces):
                cot_ref[pl.ds(clip * rows + k * span, span)] = pieces[k][1, clip]

    normed = normed_ref[...]
    all_queries = contract(normed, wq_ref[...], ((1,), (0,))).astype(jnp.bfloat16)
    all_keys = contract(normed, wk_ref[...], ((1,), (0,))).astype(jnp.bfloat16)
    all_values = contract(normed, wv_ref[...], ((1,), (0,))).astype(jnp.bfloat16)
    mixed_grad = contract(cot_ref[...], wo_ref[...], ((1,), (1,))).astype(jnp.bfloat16)

    lane_head = lax.broadcasted_iota(jnp.int32, (rows, wide), 1) // depth
    head_masks = [(lane_head == h).astype(jnp.float32).astype(jnp.bfloat16) for h in range(GROUP)]
    key_pos = lax.broadcasted_iota(jnp.int32, (rows, rows), 0) % n_positions
    query_pos = lax.broadcasted_iota(jnp.int32, (rows, rows), 1) % n_positions
    same = (key_pos == query_pos)[None]

    def stacked(block):
        return jnp.concatenate([block * mask for mask in head_masks], axis=0)

    def side_by_side(blocks):
        return jnp.concatenate([blocks[h] for h in range(GROUP)], axis=1)

    for clip, group in itertools.product(range(n_clips), range(STEP)):
        here = slice(clip * rows, (clip + 1) * rows)
        columns = slice(group * wide, (group + 1) * wide)
        queries = all_queries[here, columns]
        keys = stacked(all_keys[here, columns])
        values = stacked(all_values[here, columns])
        upstream = mixed_grad[here, columns]
        scores = contract(keys, queries, ((1,), (1,))).reshape(GROUP, rows, rows)
        scores = jnp.where(same, scores * scaling, LOWEST)
        expo = jnp.exp(scores - jnp.max(scores, axis=1, keepdims=True))
        full = expo * (1.0 / jnp.sum(expo, axis=1, keepdims=True))
        low = full.astype(jnp.bfloat16)
        dots = contract(values, upstream, ((1,), (1,))).reshape(GROUP, rows, rows)
        score_grad = full * (dots - jnp.sum(full * dots, axis=1, keepdims=True))
        score_grad = (score_grad * scaling).astype(jnp.bfloat16)
        mixed = contract(low.reshape(GROUP * rows, rows), values, ((0,), (0,)))
        mixed_ref[here, columns] = mixed.astype(jnp.bfloat16)
        dq = contract(score_grad.reshape(GROUP * rows, rows), keys, ((0,), (0,)))
        dq_ref[here, columns] = dq.astype(jnp.bfloat16)
        dk = contract(side_by_side(score_grad), stacked(queries), ((1,), (0,)))
        dk_ref[here, columns] = dk.astype(jnp.bfloat16)
        dv = contract(side_by_side(low), stacked(upstream), ((1,), (0,)))
        dv_ref[here, columns] = dv.astype(jnp.bfloat16)

    part = contract(dq_ref[...], wq_ref[...], ((1,), (1,)))
    part += contract(dk_ref[...], wk_ref[...], ((1,), (1,)))
    part += contract(dv_ref[...], wv_ref[...], ((1,), (1,)))

    @pl.when(step == 0)
    def _():
        total_ref[...] = part

    @pl.when(step > 0)
    def _():
        total_ref[...] += part

    @pl.when(step == pl.num_programs(0) - 1)
    def _():
        unit, inverse = statistics(raw_rows())
        total = total_ref[...]
        grad = inverse * (
            total
            - jnp.mean(total, axis=-1, keepdims=True)
            - unit * jnp.mean(total * unit, axis=-1, keepdims=True)
        )
        dx = (cot_ref[...].astype(jnp.float32) + grad).astype(jnp.bfloat16)
        for clip in range(n_clips):
            for k in range(n_pieces):
                start = clip * rows + k * span
                dx_refs[k][clip] = dx[start : start + span]


def sublayer(pieces, n_clips, w_qkv, w_out, chunk, n_chunks, n_positions, before):
    n_pieces = len(pieces)
    _, _, span, width = pieces[0].shape
    rows = n_clips * n_pieces * span
    groups = HEADS // (GROUP * STEP)
    wide = width // groups

    flat = jax.ShapeDtypeStruct((n_chunks * rows, width), jnp.bfloat16)
    dx = jax.ShapeDtypeStruct((n_chunks * n_clips, span, width), jnp.bfloat16)
    out_shape = [flat] * 6 + [dx] * n_pieces
    aliased = [] if before is None else list(before)
    first = n_pieces + 4
    return pl.pallas_call(
        functools.partial(sublayer_kernel, n_clips, n_positions, n_pieces, len(aliased)),
        grid=(groups,),
        out_shape=out_shape,
        in_specs=[
            pl.BlockSpec(
                (2, n_clips, span, width),
                lambda j, i=chunk if piece.shape[1] > n_clips else 0: (0, i, 0, 0),
            )
            for piece in pieces
        ]
        + [pl.BlockSpec((width, wide), lambda j, i=i: (0, i * groups + j)) for i in range(3)]
        + [pl.BlockSpec((wide, width), lambda j: (j, 0))]
        + [pl.BlockSpec(memory_space=pl.ANY)] * len(aliased),
        out_specs=[
            pl.BlockSpec((rows, width), lambda j: (chunk, 0)),
            pl.BlockSpec((rows, width), lambda j: (chunk, 0)),
        ]
        + [pl.BlockSpec((rows, wide), lambda j: (chunk, j))] * 4
        + [pl.BlockSpec((n_clips, span, width), lambda j: (chunk, 0, 0))] * n_pieces,
        scratch_shapes=[pltpu.VMEM((rows, width), jnp.float32)],
        input_output_aliases={first + i: i for i in range(len(aliased))},
        compiler_params=pltpu.CompilerParams(vmem_limit_bytes=28 * MIB),
        cost_estimate=pl.CostEstimate(
            flops=2 * rows * width * (7 * width + 24 * 128),
            bytes_accessed=16 * rows * width + 8 * width * width,
            transcendentals=rows * 128 * HEADS,
        ),
    )(*pieces, w_qkv, w_qkv, w_qkv, w_out, *aliased)


def swap(block, axis, size, distance):
    return lax.ppermute(block, axis, [(i, i ^ distance) for i in range(size)])


def after(values, done):
    values, _ = lax.optimization_barrier((values, done))
    return values


def inbound(near, far, n_tm):
    half = n_tm // 2
    near = [near[0]] + [swap(near[k], "tm", n_tm, k) for k in range(1, half)]
    arrived = []
    for blocks in far:
        gates = arrived[-1] if arrived else [near[2]] + [None] * (half - 1)
        blocks = [block if gate is None else after(block, gate) for block, gate in zip(blocks, gates)]
        done = {i: swap(blocks[i], "tm", n_tm, half + i) for i in reversed(range(half))}
        arrived.append([done[i] for i in range(half)])
    return near, arrived


def shards(n_clip_devices, n_tm, clips, w_qkv, w_out, cotangent):
    n_clips, _, n_patches, width = clips.shape
    n_positions = n_patches // n_tm
    n_x, n_z = n_clip_devices // CORES, n_tm // N_Y
    joined = n_positions % 16 != 0
    ids = jnp.stack([lax.axis_index("clip"), lax.axis_index("tm")]).astype(jnp.int32)

    near, far = inbound(*pick(ids, clips, cotangent, n_tm, CHUNKS), n_tm)
    depth = n_clips // CHUNKS
    results = None
    for chunk in range(CHUNKS):
        pieces = near + far[chunk]
        if joined:
            pieces = [p[:, chunk * depth :][:, :depth] for p in near] + far[chunk]
            pieces = [jnp.stack(pieces, axis=2).reshape(2, depth, -1, width)]
        results = sublayer(pieces, depth, w_qkv, w_out, chunk, CHUNKS, n_positions, results)
    normed, cot, mixed, dq, dk, dv = results[:6]
    dx = list(results[6:])
    if joined:
        cut = dx[0].reshape(n_clips, n_tm, n_positions, width)
        dx = [cut[:, k] for k in range(n_tm)]

    halves = ([normed], [dq, dk]), ([normed, mixed], [dv, cot])
    sent_second = products(ids, 1, n_x, n_z, *halves[1])
    second = swap(sent_second, "clip", n_clip_devices, 1)
    sent_first = products(ids, 1, n_x, n_z, *after(halves[0], sent_second))
    first = swap(sent_first, "clip", n_clip_devices, 1)
    own_second = products(ids, 0, n_x, n_z, *after(halves[1], sent_first))
    sent, own_second = halve(ids, (own_second, second), 2, 1, 1)
    second = swap(sent, "tm", n_tm, 1)
    own_first = products(ids, 0, n_x, n_z, *after(halves[0], own_second))
    sent, own_first = halve(ids, (own_first, first), 0, 0, CORES)
    first = swap(sent, "clip", n_clip_devices, CORES)
    dx = after(dx, sent_first)
    back = {}
    for k in range(n_tm - 1, 1, -1):
        block = dx[k] if k + 3 >= n_tm else after(dx[k], back[k + 3])
        back[k] = swap(block, "tm", n_tm, k)
    first, second = after((first, second), back)
    sent, own_first = halve(ids, (own_first, first), 1, 1, 1)
    first = swap(sent, "tm", n_tm, 1)
    sent, own_second = halve(ids, (own_second, second), 0, 0, CORES)
    second = swap(sent, "clip", n_clip_devices, CORES)
    total, *sent = join(ids, (own_first, first), (own_second, second), n_z)
    others = [swap(block, "tm", n_tm, (j + 1) * N_Y) for j, block in enumerate(sent)]
    back[0] = dx[0]
    back[1] = swap(after(dx[1], sent), "tm", n_tm, 1)
    grad_clips = place(ids, [back[k] for k in range(n_tm)]).reshape(clips.shape)
    grad_qkv, grad_out = finish((total, *others))
    return (grad_clips, grad_qkv, grad_out)


def solution(mesh):
    return jax.shard_map(
        functools.partial(shards, mesh.shape["clip"], mesh.shape["tm"]),
        mesh=mesh,
        in_specs=(P("clip", "tm", None, None), P(), P(), P("clip", "tm", None, None)),
        out_specs=(P("clip", "tm", None, None), P(("clip", "tm"), None), P(("clip", "tm"), None)),
        check_vma=False,
    )
```

```python
import functools
import itertools

import jax
import jax.numpy as jnp
from jax import lax
from jax.experimental import pallas as pl
from jax.experimental.pallas import tpu as pltpu
from jax.sharding import PartitionSpec as P

HEADS = 16
GROUP = 4
FIRST = 9 / 16
CHUNKS = 2
CORES = 2
N_Y = 2
EPSILON = 1e-06
LOWEST = -1e30
LOG2E = 1.4426950408889634
MIB = 1024 * 1024


def contract(left, right, dims):
    return lax.dot_general(left, right, (dims, ((), ())), preferred_element_type=jnp.float32)


def statistics(rows32):
    mean = jnp.mean(rows32, axis=-1, keepdims=True)
    centred = rows32 - mean
    inverse = lax.rsqrt(jnp.mean(centred * centred, axis=-1, keepdims=True) + EPSILON)
    return centred * inverse, inverse


def pick_kernel(n_slots, n_chunks, ids_ref, x_ref, cot_ref, *refs):
    out_refs, sem = refs[:-1], refs[-1]
    half = n_slots // 2
    depth = x_ref.shape[0] // n_chunks
    copies = []
    for i, ref in enumerate(out_refs):
        far = i - half
        here = slice(None) if far < 0 else pl.ds(far // half * depth, depth)
        slot = ids_ref[1] ^ (i if far < 0 else half + far % half)
        for which, source in enumerate((x_ref, cot_ref)):
            copy = pltpu.make_async_copy(source.at[here, slot], ref.at[which], sem.at[2 * i + which])
            copy.start()
            copies.append(copy)
    for copy in copies:
        copy.wait()


def pick(ids, clips, cotangent, n_slots, n_chunks):
    n_clips, _, n_patches, width = clips.shape
    cut = (n_clips, n_slots, n_patches // n_slots, width)
    half = n_slots // 2

    def piece(count):
        return jax.ShapeDtypeStruct((2, count) + cut[2:], clips.dtype)

    out = pl.pallas_call(
        functools.partial(pick_kernel, n_slots, n_chunks),
        out_shape=[piece(n_clips)] * half + [piece(n_clips // n_chunks)] * (half * n_chunks),
        in_specs=[pl.BlockSpec(memory_space=pltpu.SMEM)] + [pl.BlockSpec(memory_space=pl.ANY)] * 2,
        out_specs=[pl.BlockSpec(memory_space=pltpu.VMEM)] * (half * (1 + n_chunks)),
        scratch_shapes=[pltpu.SemaphoreType.DMA((2 * half * (1 + n_chunks),))],
        compiler_params=pltpu.CompilerParams(vmem_limit_bytes=12 * MIB),
    )(ids, clips.reshape(cut), cotangent.reshape(cut))
    far = [out[half + chunk * half :][:half] for chunk in range(n_chunks)]
    return out[:half], far


def place_kernel(ids_ref, *refs):
    for slot, ref in enumerate(refs[:-1]):
        refs[-1][:, ids_ref[1] ^ slot] = ref[...]


def place(ids, blocks):
    n_clips, n_positions, width = blocks[0].shape
    return pl.pallas_call(
        place_kernel,
        out_shape=jax.ShapeDtypeStruct((n_clips, len(blocks), n_positions, width), blocks[0].dtype),
        in_specs=[pl.BlockSpec(memory_space=pltpu.SMEM)]
        + [pl.BlockSpec(memory_space=pltpu.VMEM)] * len(blocks),
        out_specs=pl.BlockSpec(memory_space=pltpu.VMEM),
        compiler_params=pltpu.CompilerParams(vmem_limit_bytes=8 * MIB),
    )(ids, *blocks)


def product_kernel(n_x, flip, n_chunks, spans, ids_ref, *refs):
    lefts, rights, out_ref = refs[: -1 - len(spans) * n_chunks], refs[-1 - len(spans) * n_chunks : -1], refs[-1]
    width = lefts[0].shape[1]
    rest = width // (CORES * n_x)
    core = lax.rem(ids_ref[0], CORES) ^ flip
    starts = [pl.multiple_of((CORES * x + core) * rest, rest) for x in range(n_x)]
    turned = []
    for i in range(0, len(lefts), n_chunks):
        parts = [[left[:, pl.ds(start, rest)] for start in starts] for left in lefts[i : i + n_chunks]]
        turned.append(jnp.concatenate([jnp.concatenate(p, axis=1) for p in parts], axis=0).T)
    at = 0
    for i, (which, start, size) in enumerate(spans):
        right = [ref[:, pl.ds(start, size)] for ref in rights[i * n_chunks : (i + 1) * n_chunks]]
        product = contract(turned[which], jnp.concatenate(right, axis=0), ((1,), (0,)))
        out_ref[:, :, :, :, pl.ds(at, size)] = product.reshape(out_ref.shape[:4] + (size,)).astype(jnp.bfloat16)
        at += size


def products(ids, flip, n_x, n_z, lefts, rights, spans):
    n_chunks = len(rights[0])
    rows, width = rights[0][0].shape
    rest = width // (CORES * n_x * n_z * N_Y)
    columns = sum(size for _, _, size in spans)
    operands = [a for factor in lefts + rights for a in factor]
    return pl.pallas_call(
        functools.partial(product_kernel, n_x, flip, n_chunks, spans),
        out_shape=jax.ShapeDtypeStruct((n_x, n_z, N_Y, rest, columns), jnp.bfloat16),
        in_specs=[pl.BlockSpec(memory_space=pltpu.SMEM)]
        + [pl.BlockSpec(memory_space=pltpu.VMEM)] * len(operands),
        out_specs=pl.BlockSpec(memory_space=pltpu.VMEM),
        compiler_params=pltpu.CompilerParams(vmem_limit_bytes=24 * MIB),
        cost_estimate=pl.CostEstimate(
            flops=n_chunks * rows * width * columns,
            bytes_accessed=2 * n_chunks * rows * (width + columns) + width * columns,
            transcendentals=0,
        ),
    )(ids, *operands)


def summed(refs, index):
    total = refs[0][index].astype(jnp.float32)
    for ref in refs[1:]:
        total += ref[index].astype(jnp.float32)
    return total


def halve_kernel(dim, axis, stride, ids_ref, *refs):
    addends, sent_ref, kept_ref = refs[:-2], refs[-2], refs[-1]
    me = lax.rem(lax.div(ids_ref[axis], stride), 2)
    for index in itertools.product(*(range(n) for n in sent_ref.shape[:-2])):
        sent_ref[index] = summed(addends, index[:dim] + (me ^ 1,) + index[dim:]).astype(jnp.bfloat16)
    for index in itertools.product(*(range(n) for n in sent_ref.shape[:-2])):
        kept_ref[index] = summed(addends, index[:dim] + (me,) + index[dim:])


def halve(ids, addends, dim, axis, stride):
    shape = addends[0].shape[:dim] + addends[0].shape[dim + 1 :]
    return pl.pallas_call(
        functools.partial(halve_kernel, dim, axis, stride),
        out_shape=[jax.ShapeDtypeStruct(shape, jnp.bfloat16), jax.ShapeDtypeStruct(shape, jnp.float32)],
        in_specs=[pl.BlockSpec(memory_space=pltpu.SMEM)]
        + [pl.BlockSpec(memory_space=pltpu.VMEM)] * len(addends),
        out_specs=[pl.BlockSpec(memory_space=pltpu.VMEM)] * 2,
        compiler_params=pltpu.CompilerParams(vmem_limit_bytes=16 * MIB),
    )(ids, *addends)


def join_kernel(n_z, n_first, ids_ref, *refs):
    addends, outs = refs[:-n_z], refs[-n_z:]
    me = lax.div(ids_ref[1], N_Y)
    cut = addends[0].shape[-1]
    for j in [*range(1, n_z), 0]:
        outs[j][:, :cut] = summed(addends[:n_first], (me ^ j,)).astype(outs[j].dtype)
        outs[j][:, cut:] = summed(addends[n_first:], (me ^ j,)).astype(outs[j].dtype)


def join(ids, first, second, n_z):
    shape = (first[0].shape[1], first[0].shape[2] + second[0].shape[2])
    own = jax.ShapeDtypeStruct(shape, jnp.float32)
    other = jax.ShapeDtypeStruct(shape, jnp.bfloat16)
    return pl.pallas_call(
        functools.partial(join_kernel, n_z, len(first)),
        out_shape=[own] + [other] * (n_z - 1),
        in_specs=[pl.BlockSpec(memory_space=pltpu.SMEM)]
        + [pl.BlockSpec(memory_space=pltpu.VMEM)] * (len(first) + len(second)),
        out_specs=[pl.BlockSpec(memory_space=pltpu.VMEM)] * n_z,
        compiler_params=pltpu.CompilerParams(vmem_limit_bytes=12 * MIB),
    )(ids, *first, *second)


def finish_kernel(*refs):
    addends, (grad_qkv_ref, grad_out_ref) = refs[:-2], refs[-2:]
    wide = grad_qkv_ref.shape[1]
    everything = slice(None)
    grad_qkv_ref[...] = summed(addends, (everything, pl.ds(0, wide)))
    grad_out_ref[...] = summed(addends, (everything, pl.ds(wide, grad_out_ref.shape[1])))


def finish(addends):
    rows, columns = addends[0].shape
    return pl.pallas_call(
        finish_kernel,
        out_shape=[
            jax.ShapeDtypeStruct((rows, columns // 4 * 3), jnp.float32),
            jax.ShapeDtypeStruct((rows, columns // 4), jnp.float32),
        ],
        in_specs=[pl.BlockSpec(memory_space=pltpu.VMEM)] * len(addends),
        out_specs=[pl.BlockSpec(memory_space=pltpu.VMEM)] * 2,
        compiler_params=pltpu.CompilerParams(vmem_limit_bytes=8 * MIB),
    )(*addends)


def sublayer_kernel(at, n_clips, n_positions, n_pieces, n_before, *refs):
    pieces, refs = refs[:n_pieces], refs[n_pieces:]
    w_qkv_ref, w_out_ref = refs[:2]
    before, refs = refs[2 : 2 + n_before], refs[2 + n_before :]
    normed_ref, cot_ref, mixed_ref, dq_ref, dk_ref, dv_ref = refs[:6]
    dx_refs = refs[6:]
    rows = normed_ref.shape[0] // n_clips
    span = rows // n_pieces
    width = w_out_ref.shape[0]
    wide = width // HEADS * GROUP
    depth = wide // GROUP
    scaling = depth**-0.5

    def piece(k, which, clip):
        return pieces[k][which, clip if pieces[k].shape[1] == n_clips else at + clip]

    raw = jnp.concatenate([piece(k, 0, clip) for clip in range(n_clips) for k in range(n_pieces)], axis=0)
    unit, _ = statistics(raw.astype(jnp.float32))
    normed_ref[...] = unit.astype(jnp.bfloat16)
    for clip in range(n_clips):
        for k in range(n_pieces):
            cot_ref[pl.ds(clip * rows + k * span, span)] = piece(k, 1, clip)

    lane_head = lax.broadcasted_iota(jnp.int32, (rows, wide), 1) // depth
    head_masks = [(lane_head == h).astype(jnp.float32).astype(jnp.bfloat16) for h in range(GROUP)]
    key_pos = lax.broadcasted_iota(jnp.int32, (rows, rows), 0) % n_positions
    query_pos = lax.broadcasted_iota(jnp.int32, (rows, rows), 1) % n_positions
    same = (key_pos == query_pos)[None]

    def stacked(block):
        return jnp.concatenate([block * mask for mask in head_masks], axis=0)

    def side_by_side(blocks):
        return jnp.concatenate([blocks[h] for h in range(GROUP)], axis=1)

    for group in range(HEADS // GROUP):
        columns = slice(group * wide, (group + 1) * wide)
        all_queries, all_keys, all_values = (
            contract(normed_ref[...], w_qkv_ref[:, pl.ds(i * width + group * wide, wide)], ((1,), (0,))).astype(
                jnp.bfloat16
            )
            for i in range(3)
        )
        mixed_grad = contract(cot_ref[...], w_out_ref[columns, :], ((1,), (1,))).astype(jnp.bfloat16)
        for clip in range(n_clips):
            here = slice(clip * rows, (clip + 1) * rows)
            queries = all_queries[here]
            keys = stacked(all_keys[here])
            values = stacked(all_values[here])
            upstream = mixed_grad[here]
            scores = contract(keys, queries, ((1,), (1,))).reshape(GROUP, rows, rows)
            scores = jnp.where(same, scores, LOWEST)
            highest = jnp.max(scores, axis=1, keepdims=True)
            expo = jnp.exp2((scores - highest) * (scaling * LOG2E))
            full = expo * (1.0 / jnp.sum(expo, axis=1, keepdims=True))
            low = full.astype(jnp.bfloat16)
            dots = contract(values, upstream * jnp.bfloat16(scaling), ((1,), (1,)))
            dots = dots.reshape(GROUP, rows, rows)
            score_grad = full * (dots - jnp.sum(full * dots, axis=1, keepdims=True))
            score_grad = score_grad.astype(jnp.bfloat16)
            mixed = contract(low.reshape(GROUP * rows, rows), values, ((0,), (0,)))
            mixed_ref[here, columns] = mixed.astype(jnp.bfloat16)
            dq = contract(score_grad.reshape(GROUP * rows, rows), keys, ((0,), (0,)))
            dq_ref[here, columns] = dq.astype(jnp.bfloat16)
            dk = contract(side_by_side(score_grad), stacked(queries), ((1,), (0,)))
            dk_ref[here, columns] = dk.astype(jnp.bfloat16)
            dv = contract(side_by_side(low), stacked(upstream), ((1,), (0,)))
            dv_ref[here, columns] = dv.astype(jnp.bfloat16)

    grads = jnp.concatenate([dq_ref[...], dk_ref[...], dv_ref[...]], axis=1)
    total = contract(grads, w_qkv_ref[...], ((1,), (1,)))
    unit, inverse = statistics(raw.astype(jnp.float32))
    grad = inverse * (
        total
        - jnp.mean(total, axis=-1, keepdims=True)
        - unit * jnp.mean(total * unit, axis=-1, keepdims=True)
    )
    dx = (cot_ref[...].astype(jnp.float32) + grad).astype(jnp.bfloat16)
    for k in range(n_pieces):
        if before:
            dx_refs[k][:at] = before[k][...]
        for clip in range(n_clips):
            start = clip * rows + k * span
            dx_refs[k][at + clip] = dx[start : start + span]


def sublayer(pieces, at, n_clips, w_qkv, w_out, n_positions, before):
    _, _, span, width = pieces[0].shape
    rows = n_clips * len(pieces) * span
    flat = jax.ShapeDtypeStruct((rows, width), jnp.bfloat16)
    dx = jax.ShapeDtypeStruct((at + n_clips, span, width), jnp.bfloat16)
    operands = (*pieces, w_qkv, w_out, *before)
    return pl.pallas_call(
        functools.partial(sublayer_kernel, at, n_clips, n_positions, len(pieces), len(before)),
        out_shape=[flat] * 6 + [dx] * len(pieces),
        in_specs=[pl.BlockSpec(memory_space=pltpu.VMEM)] * len(operands),
        out_specs=[pl.BlockSpec(memory_space=pltpu.VMEM)] * (6 + len(pieces)),
        compiler_params=pltpu.CompilerParams(vmem_limit_bytes=32 * MIB),
        cost_estimate=pl.CostEstimate(
            flops=2 * rows * width * (7 * width + 24 * 128),
            bytes_accessed=16 * rows * width + 8 * width * width,
            transcendentals=rows * 128 * HEADS,
        ),
    )(*operands)


def swap(block, axis, size, distance):
    return lax.ppermute(block, axis, [(i, i ^ distance) for i in range(size)])


def after(values, done):
    values, _ = lax.optimization_barrier((values, done))
    return values


def inbound(near, far, n_tm):
    half = n_tm // 2
    near = [near[0]] + [swap(near[k], "tm", n_tm, k) for k in range(1, half)]
    arrived = []
    for blocks in far:
        gates = arrived[-1] if arrived else [near[2]] + [None] * (half - 1)
        blocks = [block if gate is None else after(block, gate) for block, gate in zip(blocks, gates)]
        done = {i: swap(blocks[i], "tm", n_tm, half + i) for i in reversed(range(half))}
        arrived.append([done[i] for i in range(half)])
    return near, arrived


def shards(n_clip_devices, n_tm, clips, w_qkv, w_out, cotangent):
    n_clips, _, n_patches, width = clips.shape
    n_positions = n_patches // n_tm
    n_x, n_z = n_clip_devices // CORES, n_tm // N_Y
    joined = n_positions % 16 != 0
    ids = jnp.stack([lax.axis_index("clip"), lax.axis_index("tm")]).astype(jnp.int32)

    near, far = inbound(*pick(ids, clips, cotangent, n_tm, CHUNKS), n_tm)
    depth = n_clips // CHUNKS
    factors, dx = [], []
    for chunk in range(CHUNKS):
        at = chunk * depth
        pieces = near + far[chunk]
        if joined:
            pieces = [p[:, at : at + depth] for p in near] + far[chunk]
            pieces = [jnp.stack(pieces, axis=2).reshape(2, depth, -1, width)]
        out = sublayer(pieces, at, depth, w_qkv, w_out, n_positions, dx)
        factors.append(out[:6])
        dx = list(out[6:])
    normed, cot, mixed, dq, dk, dv = zip(*factors)
    if joined:
        cut = dx[0].reshape(n_clips, n_tm, n_positions, width)
        dx = [cut[:, k] for k in range(n_tm)]

    cut = int(4 * width * FIRST) - 2 * width
    first_parts = ([normed], [dq, dk, dv]), ((0, 0, width), (0, 0, width), (0, 0, cut))
    second_parts = ([normed, mixed], [dv, cot]), ((0, cut, width - cut), (1, 0, width))
    sent_second = products(ids, 1, n_x, n_z, *second_parts[0], second_parts[1])
    second = swap(sent_second, "clip", n_clip_devices, 1)
    sent_first = products(ids, 1, n_x, n_z, *after(first_parts[0], sent_second), first_parts[1])
    first = swap(sent_first, "clip", n_clip_devices, 1)
    own_second = products(ids, 0, n_x, n_z, *after(second_parts[0], sent_first), second_parts[1])
    sent, own_second = halve(ids, (own_second, second), 2, 1, 1)
    second = swap(sent, "tm", n_tm, 1)
    own_first = products(ids, 0, n_x, n_z, *after(first_parts[0], own_second), first_parts[1])
    sent, own_first = halve(ids, (own_first, first), 0, 0, CORES)
    first = swap(sent, "clip", n_clip_devices, CORES)
    dx = after(dx, sent_first)
    late = (1, 3)
    back = {}
    for k in reversed([k for k in range(1, n_tm) if k not in late]):
        block = after(dx[k], back[k + 3]) if k + 3 in back else dx[k]
        back[k] = swap(block, "tm", n_tm, k)
    first, second = after((first, second), back)
    sent, own_first = halve(ids, (own_first, first), 1, 1, 1)
    first = swap(sent, "tm", n_tm, 1)
    sent, own_second = halve(ids, (own_second, second), 0, 0, CORES)
    second = swap(sent, "clip", n_clip_devices, CORES)
    total, *sent = join(ids, (own_first, first), (own_second, second), n_z)
    others = [swap(block, "tm", n_tm, (j + 1) * N_Y) for j, block in enumerate(sent)]
    back[0] = dx[0]
    for k in late:
        back[k] = swap(after(dx[k], sent), "tm", n_tm, k)
    grad_clips = place(ids, [back[k] for k in range(n_tm)]).reshape(clips.shape)
    grad_qkv, grad_out = finish((total, *others))
    return (grad_clips, grad_qkv, grad_out)


def solution(mesh):
    return jax.shard_map(
        functools.partial(shards, mesh.shape["clip"], mesh.shape["tm"]),
        mesh=mesh,
        in_specs=(P("clip", "tm", None, None), P(), P(), P("clip", "tm", None, None)),
        out_specs=(P("clip", "tm", None, None), P(("clip", "tm"), None), P(("clip", "tm"), None)),
        check_vma=False,
    )
```

```python
import functools
import itertools

import jax
import jax.numpy as jnp
from jax import lax
from jax.experimental import pallas as pl
from jax.experimental.pallas import tpu as pltpu
from jax.sharding import PartitionSpec as P

HEADS = 16
GROUP = 4
FIRST = 9 / 16
CHUNKS = 2
CORES = 2
N_Y = 2
EPSILON = 1e-06
LOWEST = -1e30
LOG2E = 1.4426950408889634
MIB = 1024 * 1024


def contract(left, right, dims):
    return lax.dot_general(left, right, (dims, ((), ())), preferred_element_type=jnp.float32)


def statistics(rows32):
    mean = jnp.mean(rows32, axis=-1, keepdims=True)
    centred = rows32 - mean
    inverse = lax.rsqrt(jnp.mean(centred * centred, axis=-1, keepdims=True) + EPSILON)
    return centred * inverse, inverse


def pick_kernel(n_slots, n_chunks, ids_ref, x_ref, cot_ref, *out_refs):
    half = n_slots // 2
    depth = x_ref.shape[0] // n_chunks
    for i, ref in enumerate(out_refs):
        far = i - half
        here = slice(None) if far < 0 else pl.ds(far // half * depth, depth)
        slot = ids_ref[1] ^ (i if far < 0 else half + far % half)
        ref[0] = x_ref[here, slot]
        ref[1] = cot_ref[here, slot]


def pick(ids, clips, cotangent, n_slots, n_chunks):
    n_clips, _, n_patches, width = clips.shape
    cut = (n_clips, n_slots, n_patches // n_slots, width)
    half = n_slots // 2

    def piece(count):
        return jax.ShapeDtypeStruct((2, count) + cut[2:], clips.dtype)

    out = pl.pallas_call(
        functools.partial(pick_kernel, n_slots, n_chunks),
        out_shape=[piece(n_clips)] * half + [piece(n_clips // n_chunks)] * (half * n_chunks),
        in_specs=[pl.BlockSpec(memory_space=pltpu.SMEM)]
        + [pl.BlockSpec(memory_space=pltpu.VMEM)] * 2,
        out_specs=[pl.BlockSpec(memory_space=pltpu.VMEM)] * (half * (1 + n_chunks)),
        compiler_params=pltpu.CompilerParams(vmem_limit_bytes=12 * MIB),
    )(ids, clips.reshape(cut), cotangent.reshape(cut))
    far = [out[half + chunk * half :][:half] for chunk in range(n_chunks)]
    return out[:half], far


def place_kernel(ids_ref, *refs):
    for slot, ref in enumerate(refs[:-1]):
        refs[-1][:, ids_ref[1] ^ slot] = ref[...]


def place(ids, blocks):
    n_clips, n_positions, width = blocks[0].shape
    return pl.pallas_call(
        place_kernel,
        out_shape=jax.ShapeDtypeStruct((n_clips, len(blocks), n_positions, width), blocks[0].dtype),
        in_specs=[pl.BlockSpec(memory_space=pltpu.SMEM)]
        + [pl.BlockSpec(memory_space=pltpu.VMEM)] * len(blocks),
        out_specs=pl.BlockSpec(memory_space=pltpu.VMEM),
        compiler_params=pltpu.CompilerParams(vmem_limit_bytes=8 * MIB),
    )(ids, *blocks)


def product_kernel(n_x, flip, n_chunks, spans, ids_ref, *refs):
    lefts, rights, out_ref = refs[: -1 - len(spans) * n_chunks], refs[-1 - len(spans) * n_chunks : -1], refs[-1]
    width = lefts[0].shape[1]
    rest = width // (CORES * n_x)
    core = lax.rem(ids_ref[0], CORES) ^ flip
    starts = [pl.multiple_of((CORES * x + core) * rest, rest) for x in range(n_x)]
    turned = []
    for i in range(0, len(lefts), n_chunks):
        parts = [[left[:, pl.ds(start, rest)] for start in starts] for left in lefts[i : i + n_chunks]]
        turned.append(jnp.concatenate([jnp.concatenate(p, axis=1) for p in parts], axis=0).T)
    at = 0
    for i, (which, start, size) in enumerate(spans):
        right = [ref[:, pl.ds(start, size)] for ref in rights[i * n_chunks : (i + 1) * n_chunks]]
        product = contract(turned[which], jnp.concatenate(right, axis=0), ((1,), (0,)))
        out_ref[:, :, :, :, pl.ds(at, size)] = product.reshape(out_ref.shape[:4] + (size,)).astype(jnp.bfloat16)
        at += size


def products(ids, flip, n_x, n_z, lefts, rights, spans):
    n_chunks = len(rights[0])
    rows, width = rights[0][0].shape
    rest = width // (CORES * n_x * n_z * N_Y)
    columns = sum(size for _, _, size in spans)
    operands = [a for factor in lefts + rights for a in factor]
    return pl.pallas_call(
        functools.partial(product_kernel, n_x, flip, n_chunks, spans),
        out_shape=jax.ShapeDtypeStruct((n_x, n_z, N_Y, rest, columns), jnp.bfloat16),
        in_specs=[pl.BlockSpec(memory_space=pltpu.SMEM)]
        + [pl.BlockSpec(memory_space=pltpu.VMEM)] * len(operands),
        out_specs=pl.BlockSpec(memory_space=pltpu.VMEM),
        compiler_params=pltpu.CompilerParams(vmem_limit_bytes=24 * MIB),
        cost_estimate=pl.CostEstimate(
            flops=n_chunks * rows * width * columns // 4,
            bytes_accessed=n_chunks * rows * width,
            transcendentals=0,
        ),
    )(ids, *operands)


def summed(refs, index):
    total = refs[0][index].astype(jnp.float32)
    for ref in refs[1:]:
        total += ref[index].astype(jnp.float32)
    return total


def halve_kernel(dim, axis, stride, ids_ref, *refs):
    addends, sent_ref, kept_ref = refs[:-2], refs[-2], refs[-1]
    me = lax.rem(lax.div(ids_ref[axis], stride), 2)
    for index in itertools.product(*(range(n) for n in sent_ref.shape[:-2])):
        sent_ref[index] = summed(addends, index[:dim] + (me ^ 1,) + index[dim:]).astype(jnp.bfloat16)
    for index in itertools.product(*(range(n) for n in sent_ref.shape[:-2])):
        kept_ref[index] = summed(addends, index[:dim] + (me,) + index[dim:])


def halve(ids, addends, dim, axis, stride):
    shape = addends[0].shape[:dim] + addends[0].shape[dim + 1 :]
    return pl.pallas_call(
        functools.partial(halve_kernel, dim, axis, stride),
        out_shape=[jax.ShapeDtypeStruct(shape, jnp.bfloat16), jax.ShapeDtypeStruct(shape, jnp.float32)],
        in_specs=[pl.BlockSpec(memory_space=pltpu.SMEM)]
        + [pl.BlockSpec(memory_space=pltpu.VMEM)] * len(addends),
        out_specs=[pl.BlockSpec(memory_space=pltpu.VMEM)] * 2,
        compiler_params=pltpu.CompilerParams(vmem_limit_bytes=16 * MIB),
    )(ids, *addends)


def join_kernel(n_z, n_first, ids_ref, *refs):
    addends, outs = refs[:-n_z], refs[-n_z:]
    me = lax.div(ids_ref[1], N_Y)
    cut = addends[0].shape[-1]
    for j in [*range(1, n_z), 0]:
        outs[j][:, :cut] = summed(addends[:n_first], (me ^ j,)).astype(outs[j].dtype)
        outs[j][:, cut:] = summed(addends[n_first:], (me ^ j,)).astype(outs[j].dtype)


def join(ids, first, second, n_z):
    shape = (first[0].shape[1], first[0].shape[2] + second[0].shape[2])
    own = jax.ShapeDtypeStruct(shape, jnp.float32)
    other = jax.ShapeDtypeStruct(shape, jnp.bfloat16)
    return pl.pallas_call(
        functools.partial(join_kernel, n_z, len(first)),
        out_shape=[own] + [other] * (n_z - 1),
        in_specs=[pl.BlockSpec(memory_space=pltpu.SMEM)]
        + [pl.BlockSpec(memory_space=pltpu.VMEM)] * (len(first) + len(second)),
        out_specs=[pl.BlockSpec(memory_space=pltpu.VMEM)] * n_z,
        compiler_params=pltpu.CompilerParams(vmem_limit_bytes=12 * MIB),
    )(ids, *first, *second)


def finish_kernel(*refs):
    addends, (grad_qkv_ref, grad_out_ref) = refs[:-2], refs[-2:]
    wide = grad_qkv_ref.shape[1]
    everything = slice(None)
    grad_qkv_ref[...] = summed(addends, (everything, pl.ds(0, wide)))
    grad_out_ref[...] = summed(addends, (everything, pl.ds(wide, grad_out_ref.shape[1])))


def finish(addends):
    rows, columns = addends[0].shape
    return pl.pallas_call(
        finish_kernel,
        out_shape=[
            jax.ShapeDtypeStruct((rows, columns // 4 * 3), jnp.float32),
            jax.ShapeDtypeStruct((rows, columns // 4), jnp.float32),
        ],
        in_specs=[pl.BlockSpec(memory_space=pltpu.VMEM)] * len(addends),
        out_specs=[pl.BlockSpec(memory_space=pltpu.VMEM)] * 2,
        compiler_params=pltpu.CompilerParams(vmem_limit_bytes=8 * MIB),
    )(*addends)


def sublayer_kernel(at, n_clips, n_positions, n_pieces, n_before, *refs):
    pieces, refs = refs[:n_pieces], refs[n_pieces:]
    w_qkv_ref, w_out_ref = refs[:2]
    before, refs = refs[2 : 2 + n_before], refs[2 + n_before :]
    normed_ref, cot_ref, mixed_ref, dq_ref, dk_ref, dv_ref = refs[:6]
    dx_refs = refs[6:]
    rows = normed_ref.shape[0] // n_clips
    span = rows // n_pieces
    width = w_out_ref.shape[0]
    wide = width // HEADS * GROUP
    depth = wide // GROUP
    scaling = depth**-0.5

    def piece(k, which, clip):
        return pieces[k][which, clip if pieces[k].shape[1] == n_clips else at + clip]

    raw = jnp.concatenate([piece(k, 0, clip) for clip in range(n_clips) for k in range(n_pieces)], axis=0)
    unit, _ = statistics(raw.astype(jnp.float32))
    normed_ref[...] = unit.astype(jnp.bfloat16)
    for clip in range(n_clips):
        for k in range(n_pieces):
            cot_ref[pl.ds(clip * rows + k * span, span)] = piece(k, 1, clip)

    lane_head = lax.broadcasted_iota(jnp.int32, (rows, wide), 1) // depth
    head_masks = [(lane_head == h).astype(jnp.float32).astype(jnp.bfloat16) for h in range(GROUP)]
    key_pos = lax.broadcasted_iota(jnp.int32, (rows, rows), 0) % n_positions
    query_pos = lax.broadcasted_iota(jnp.int32, (rows, rows), 1) % n_positions
    same = (key_pos == query_pos)[None]

    def stacked(block):
        return jnp.concatenate([block * mask for mask in head_masks], axis=0)

    def side_by_side(blocks):
        return jnp.concatenate([blocks[h] for h in range(GROUP)], axis=1)

    for group in range(HEADS // GROUP):
        columns = slice(group * wide, (group + 1) * wide)
        all_queries, all_keys, all_values = (
            contract(normed_ref[...], w_qkv_ref[:, pl.ds(i * width + group * wide, wide)], ((1,), (0,))).astype(
                jnp.bfloat16
            )
            for i in range(3)
        )
        mixed_grad = contract(cot_ref[...], w_out_ref[columns, :], ((1,), (1,))).astype(jnp.bfloat16)
        for clip in range(n_clips):
            here = slice(clip * rows, (clip + 1) * rows)
            queries = all_queries[here]
            keys = stacked(all_keys[here])
            values = stacked(all_values[here])
            upstream = mixed_grad[here]
            scores = contract(keys, queries, ((1,), (1,))).reshape(GROUP, rows, rows)
            scores = jnp.where(same, scores, LOWEST)
            highest = jnp.max(scores, axis=1, keepdims=True)
            expo = jnp.exp2((scores - highest) * (scaling * LOG2E))
            full = expo * (1.0 / jnp.sum(expo, axis=1, keepdims=True))
            low = full.astype(jnp.bfloat16)
            dots = contract(values, upstream * jnp.bfloat16(scaling), ((1,), (1,)))
            dots = dots.reshape(GROUP, rows, rows)
            score_grad = full * (dots - jnp.sum(full * dots, axis=1, keepdims=True))
            score_grad = score_grad.astype(jnp.bfloat16)
            mixed = contract(low.reshape(GROUP * rows, rows), values, ((0,), (0,)))
            mixed_ref[here, columns] = mixed.astype(jnp.bfloat16)
            dq = contract(score_grad.reshape(GROUP * rows, rows), keys, ((0,), (0,)))
            dq_ref[here, columns] = dq.astype(jnp.bfloat16)
            dk = contract(side_by_side(score_grad), stacked(queries), ((1,), (0,)))
            dk_ref[here, columns] = dk.astype(jnp.bfloat16)
            dv = contract(side_by_side(low), stacked(upstream), ((1,), (0,)))
            dv_ref[here, columns] = dv.astype(jnp.bfloat16)

    grads = jnp.concatenate([dq_ref[...], dk_ref[...], dv_ref[...]], axis=1)
    total = contract(grads, w_qkv_ref[...], ((1,), (1,)))
    unit, inverse = statistics(raw.astype(jnp.float32))
    grad = inverse * (
        total
        - jnp.mean(total, axis=-1, keepdims=True)
        - unit * jnp.mean(total * unit, axis=-1, keepdims=True)
    )
    dx = (cot_ref[...].astype(jnp.float32) + grad).astype(jnp.bfloat16)
    for k in range(n_pieces):
        if before:
            dx_refs[k][:at] = before[k][...]
        for clip in range(n_clips):
            start = clip * rows + k * span
            dx_refs[k][at + clip] = dx[start : start + span]


def sublayer(pieces, at, n_clips, w_qkv, w_out, n_positions, before):
    _, _, span, width = pieces[0].shape
    rows = n_clips * len(pieces) * span
    flat = jax.ShapeDtypeStruct((rows, width), jnp.bfloat16)
    dx = jax.ShapeDtypeStruct((at + n_clips, span, width), jnp.bfloat16)
    operands = (*pieces, w_qkv, w_out, *before)
    return pl.pallas_call(
        functools.partial(sublayer_kernel, at, n_clips, n_positions, len(pieces), len(before)),
        out_shape=[flat] * 6 + [dx] * len(pieces),
        in_specs=[pl.BlockSpec(memory_space=pltpu.VMEM)] * len(operands),
        out_specs=[pl.BlockSpec(memory_space=pltpu.VMEM)] * (6 + len(pieces)),
        compiler_params=pltpu.CompilerParams(vmem_limit_bytes=32 * MIB),
        cost_estimate=pl.CostEstimate(
            flops=2 * rows * width * (7 * width + 24 * 128),
            bytes_accessed=16 * rows * width + 8 * width * width,
            transcendentals=rows * 128 * HEADS,
        ),
    )(*operands)


def swap(block, axis, size, distance):
    return lax.ppermute(block, axis, [(i, i ^ distance) for i in range(size)])


def after(values, done):
    values, _ = lax.optimization_barrier((values, done))
    return values


def inbound(near, far, n_tm):
    half = n_tm // 2
    near = [near[0]] + [swap(near[k], "tm", n_tm, k) for k in range(1, half)]
    arrived = []
    for blocks in far:
        gates = arrived[-1] if arrived else [near[2]] + [None] * (half - 1)
        blocks = [block if gate is None else after(block, gate) for block, gate in zip(blocks, gates)]
        done = {i: swap(blocks[i], "tm", n_tm, half + i) for i in reversed(range(half))}
        arrived.append([done[i] for i in range(half)])
    return near, arrived


def shards(n_clip_devices, n_tm, clips, w_qkv, w_out, cotangent):
    n_clips, _, n_patches, width = clips.shape
    n_positions = n_patches // n_tm
    n_x, n_z = n_clip_devices // CORES, n_tm // N_Y
    joined = n_positions % 16 != 0
    ids = jnp.stack([lax.axis_index("clip"), lax.axis_index("tm")]).astype(jnp.int32)

    near, far = inbound(*pick(ids, clips, cotangent, n_tm, CHUNKS), n_tm)
    depth = n_clips // CHUNKS
    factors, dx = [], []
    for chunk in range(CHUNKS):
        at = chunk * depth
        pieces = near + far[chunk]
        if joined:
            pieces = [p[:, at : at + depth] for p in near] + far[chunk]
            pieces = [jnp.stack(pieces, axis=2).reshape(2, depth, -1, width)]
        out = sublayer(pieces, at, depth, w_qkv, w_out, n_positions, dx)
        factors.append(out[:6])
        dx = list(out[6:])
    normed, cot, mixed, dq, dk, dv = zip(*factors)
    if joined:
        cut = dx[0].reshape(n_clips, n_tm, n_positions, width)
        dx = [cut[:, k] for k in range(n_tm)]

    cut = int(4 * width * FIRST) - 2 * width
    first_parts = ([normed], [dq, dk, dv]), ((0, 0, width), (0, 0, width), (0, 0, cut))
    second_parts = ([normed, mixed], [dv, cot]), ((0, cut, width - cut), (1, 0, width))
    sent_first = products(ids, 1, n_x, n_z, *first_parts[0], first_parts[1])
    first = swap(sent_first, "clip", n_clip_devices, 1)
    sent_second = products(ids, 1, n_x, n_z, *after(second_parts[0], sent_first), second_parts[1])
    second = swap(sent_second, "clip", n_clip_devices, 1)
    own_first = products(ids, 0, n_x, n_z, *after(first_parts[0], sent_second), first_parts[1])
    sent, own_first = halve(ids, (own_first, first), 0, 0, CORES)
    first = swap(sent, "clip", n_clip_devices, CORES)
    own_second = products(ids, 0, n_x, n_z, *after(second_parts[0], own_first), second_parts[1])
    sent, own_second = halve(ids, (own_second, second), 2, 1, 1)
    second = swap(sent, "tm", n_tm, 1)
    dx = after(dx, sent_second)
    late = (1, 3)
    back = {}
    for k in reversed([k for k in range(1, n_tm) if k not in late]):
        block = after(dx[k], back[k + 3]) if k + 3 in back else dx[k]
        back[k] = swap(block, "tm", n_tm, k)
    first, second = after((first, second), [back[k] for k in range(n_tm - 3, n_tm)])
    sent, own_first = halve(ids, (own_first, first), 1, 1, 1)
    first = swap(sent, "tm", n_tm, 1)
    sent, own_second = halve(ids, (own_second, second), 0, 0, CORES)
    second = swap(sent, "clip", n_clip_devices, CORES)
    first, second = after((first, second), back)
    total, *sent = join(ids, (own_first, first), (own_second, second), n_z)
    others = [swap(sent[j - 1], "tm", n_tm, j * N_Y) for j in reversed(range(1, n_z))]
    back[0] = dx[0]
    for k in late:
        back[k] = swap(after(dx[k], sent), "tm", n_tm, k)
    grad_clips = place(ids, [back[k] for k in range(n_tm)]).reshape(clips.shape)
    grad_qkv, grad_out = finish((total, *others))
    return (grad_clips, grad_qkv, grad_out)


def solution(mesh):
    return jax.shard_map(
        functools.partial(shards, mesh.shape["clip"], mesh.shape["tm"]),
        mesh=mesh,
        in_specs=(P("clip", "tm", None, None), P(), P(), P("clip", "tm", None, None)),
        out_specs=(P("clip", "tm", None, None), P(("clip", "tm"), None), P(("clip", "tm"), None)),
        check_vma=False,
    )
```

```python
import functools
import itertools

import jax
import jax.numpy as jnp
from jax import lax
from jax.experimental import pallas as pl
from jax.experimental.pallas import tpu as pltpu
from jax.sharding import PartitionSpec as P

HEADS = 16
GROUP = 4
FIRST = 5 / 8
CHUNKS = 2
CORES = 2
N_Y = 2
EPSILON = 1e-06
LOWEST = -1e30
LOG2E = 1.4426950408889634
MIB = 1024 * 1024


def contract(left, right, dims):
    return lax.dot_general(left, right, (dims, ((), ())), preferred_element_type=jnp.float32)


def statistics(rows32):
    mean = jnp.mean(rows32, axis=-1, keepdims=True)
    centred = rows32 - mean
    inverse = lax.rsqrt(jnp.mean(centred * centred, axis=-1, keepdims=True) + EPSILON)
    return centred * inverse, inverse


def pick_kernel(n_slots, n_chunks, ids_ref, x_ref, cot_ref, *out_refs):
    half = n_slots // 2
    depth = x_ref.shape[0] // n_chunks
    for i, ref in enumerate(out_refs):
        far = i - half
        here = slice(None) if far < 0 else pl.ds(far // half * depth, depth)
        slot = ids_ref[1] ^ (i if far < 0 else half + far % half)
        ref[0] = x_ref[here, slot]
        ref[1] = cot_ref[here, slot]


def pick(ids, clips, cotangent, n_slots, n_chunks):
    n_clips, _, n_patches, width = clips.shape
    cut = (n_clips, n_slots, n_patches // n_slots, width)
    half = n_slots // 2

    def piece(count):
        return jax.ShapeDtypeStruct((2, count) + cut[2:], clips.dtype)

    out = pl.pallas_call(
        functools.partial(pick_kernel, n_slots, n_chunks),
        out_shape=[piece(n_clips)] * half + [piece(n_clips // n_chunks)] * (half * n_chunks),
        in_specs=[pl.BlockSpec(memory_space=pltpu.SMEM)]
        + [pl.BlockSpec(memory_space=pltpu.VMEM)] * 2,
        out_specs=[pl.BlockSpec(memory_space=pltpu.VMEM)] * (half * (1 + n_chunks)),
        compiler_params=pltpu.CompilerParams(vmem_limit_bytes=12 * MIB),
    )(ids, clips.reshape(cut), cotangent.reshape(cut))
    far = [out[half + chunk * half :][:half] for chunk in range(n_chunks)]
    return out[:half], far


def place_kernel(ids_ref, *refs):
    for slot, ref in enumerate(refs[:-1]):
        refs[-1][:, ids_ref[1] ^ slot] = ref[...]


def place(ids, blocks):
    n_clips, n_positions, width = blocks[0].shape
    return pl.pallas_call(
        place_kernel,
        out_shape=jax.ShapeDtypeStruct((n_clips, len(blocks), n_positions, width), blocks[0].dtype),
        in_specs=[pl.BlockSpec(memory_space=pltpu.SMEM)]
        + [pl.BlockSpec(memory_space=pltpu.VMEM)] * len(blocks),
        out_specs=pl.BlockSpec(memory_space=pltpu.VMEM),
        compiler_params=pltpu.CompilerParams(vmem_limit_bytes=8 * MIB),
    )(ids, *blocks)


def product_kernel(n_x, flip, n_chunks, spans, ids_ref, *refs):
    lefts, rights, out_ref = refs[: -1 - len(spans) * n_chunks], refs[-1 - len(spans) * n_chunks : -1], refs[-1]
    width = lefts[0].shape[1]
    rest = width // (CORES * n_x)
    core = lax.rem(ids_ref[0], CORES) ^ flip
    starts = [pl.multiple_of((CORES * x + core) * rest, rest) for x in range(n_x)]
    turned = []
    for i in range(0, len(lefts), n_chunks):
        parts = [[left[:, pl.ds(start, rest)] for start in starts] for left in lefts[i : i + n_chunks]]
        turned.append(jnp.concatenate([jnp.concatenate(p, axis=1) for p in parts], axis=0).T)
    at = 0
    for i, (which, start, size) in enumerate(spans):
        right = [ref[:, pl.ds(start, size)] for ref in rights[i * n_chunks : (i + 1) * n_chunks]]
        product = contract(turned[which], jnp.concatenate(right, axis=0), ((1,), (0,)))
        out_ref[:, :, :, :, pl.ds(at, size)] = product.reshape(out_ref.shape[:4] + (size,)).astype(jnp.bfloat16)
        at += size


def products(ids, flip, n_x, n_z, lefts, rights, spans):
    n_chunks = len(rights[0])
    rows, width = rights[0][0].shape
    rest = width // (CORES * n_x * n_z * N_Y)
    columns = sum(size for _, _, size in spans)
    operands = [a for factor in lefts + rights for a in factor]
    return pl.pallas_call(
        functools.partial(product_kernel, n_x, flip, n_chunks, spans),
        out_shape=jax.ShapeDtypeStruct((n_x, n_z, N_Y, rest, columns), jnp.bfloat16),
        in_specs=[pl.BlockSpec(memory_space=pltpu.SMEM)]
        + [pl.BlockSpec(memory_space=pltpu.VMEM)] * len(operands),
        out_specs=pl.BlockSpec(memory_space=pltpu.VMEM),
        compiler_params=pltpu.CompilerParams(vmem_limit_bytes=24 * MIB),
        cost_estimate=pl.CostEstimate(
            flops=n_chunks * rows * width * columns // 4,
            bytes_accessed=n_chunks * rows * width,
            transcendentals=0,
        ),
    )(ids, *operands)


def summed(refs, index):
    total = refs[0][index].astype(jnp.float32)
    for ref in refs[1:]:
        total += ref[index].astype(jnp.float32)
    return total


def halve_kernel(dim, axis, stride, ids_ref, *refs):
    addends, sent_ref, kept_ref = refs[:-2], refs[-2], refs[-1]
    me = lax.rem(lax.div(ids_ref[axis], stride), 2)
    for index in itertools.product(*(range(n) for n in sent_ref.shape[:-2])):
        sent_ref[index] = summed(addends, index[:dim] + (me ^ 1,) + index[dim:]).astype(jnp.bfloat16)
    for index in itertools.product(*(range(n) for n in sent_ref.shape[:-2])):
        kept_ref[index] = summed(addends, index[:dim] + (me,) + index[dim:])


def halve(ids, addends, dim, axis, stride):
    shape = addends[0].shape[:dim] + addends[0].shape[dim + 1 :]
    return pl.pallas_call(
        functools.partial(halve_kernel, dim, axis, stride),
        out_shape=[jax.ShapeDtypeStruct(shape, jnp.bfloat16), jax.ShapeDtypeStruct(shape, jnp.float32)],
        in_specs=[pl.BlockSpec(memory_space=pltpu.SMEM)]
        + [pl.BlockSpec(memory_space=pltpu.VMEM)] * len(addends),
        out_specs=[pl.BlockSpec(memory_space=pltpu.VMEM)] * 2,
        compiler_params=pltpu.CompilerParams(vmem_limit_bytes=16 * MIB),
    )(ids, *addends)


def join_kernel(n_z, n_first, ids_ref, *refs):
    addends, outs = refs[:-n_z], refs[-n_z:]
    me = lax.div(ids_ref[1], N_Y)
    cut = addends[0].shape[-1]
    for j in [*range(1, n_z), 0]:
        outs[j][:, :cut] = summed(addends[:n_first], (me ^ j,)).astype(outs[j].dtype)
        outs[j][:, cut:] = summed(addends[n_first:], (me ^ j,)).astype(outs[j].dtype)


def join(ids, first, second, n_z):
    shape = (first[0].shape[1], first[0].shape[2] + second[0].shape[2])
    own = jax.ShapeDtypeStruct(shape, jnp.float32)
    other = jax.ShapeDtypeStruct(shape, jnp.bfloat16)
    return pl.pallas_call(
        functools.partial(join_kernel, n_z, len(first)),
        out_shape=[own] + [other] * (n_z - 1),
        in_specs=[pl.BlockSpec(memory_space=pltpu.SMEM)]
        + [pl.BlockSpec(memory_space=pltpu.VMEM)] * (len(first) + len(second)),
        out_specs=[pl.BlockSpec(memory_space=pltpu.VMEM)] * n_z,
        compiler_params=pltpu.CompilerParams(vmem_limit_bytes=12 * MIB),
    )(ids, *first, *second)


def cross_kernel(n_first, ids_ref, *refs):
    (near_sent, far_sent, near_kept, far_kept), addends = refs[-4:], refs[:-4]
    first, second = addends[:n_first], addends[n_first:]
    me = lax.div(ids_ref[1], N_Y)
    middle = near_sent.shape[2]
    cut = first[0].shape[2]
    rows = slice(None)
    for out, blocks in ((near_sent, (1, 3)), (near_kept, (0, 2))):
        for i, block in enumerate(blocks):
            out[i] = summed(first, (me ^ block, rows, pl.ds(0, middle))).astype(out.dtype)
    for out, blocks in ((far_sent, (2, 3)), (far_kept, (0, 1))):
        for i, block in enumerate(blocks):
            left = summed(first, (me ^ block, rows, pl.ds(middle, cut - middle)))
            out[i, :, pl.ds(0, cut - middle)] = left.astype(out.dtype)
            out[i, :, pl.ds(cut - middle, 2 * middle - cut)] = summed(second, (me ^ block,)).astype(out.dtype)


def cross(ids, first, second):
    rows, columns = first[0].shape[1], first[0].shape[2] + second[0].shape[2]
    shape = (2, rows, columns // 2)
    sent, kept = (jax.ShapeDtypeStruct(shape, kind) for kind in (jnp.bfloat16, jnp.float32))
    return pl.pallas_call(
        functools.partial(cross_kernel, len(first)),
        out_shape=[sent, sent, kept, kept],
        in_specs=[pl.BlockSpec(memory_space=pltpu.SMEM)]
        + [pl.BlockSpec(memory_space=pltpu.VMEM)] * (len(first) + len(second)),
        out_specs=[pl.BlockSpec(memory_space=pltpu.VMEM)] * 4,
        compiler_params=pltpu.CompilerParams(vmem_limit_bytes=12 * MIB),
    )(ids, *first, *second)


def pass_kernel(kept_ref, came_ref, sent_ref):
    sent_ref[...] = summed((kept_ref, came_ref), 1).astype(jnp.bfloat16)


def pass_on(kept, came):
    return pl.pallas_call(
        pass_kernel,
        out_shape=jax.ShapeDtypeStruct(came.shape[1:], jnp.bfloat16),
        in_specs=[pl.BlockSpec(memory_space=pltpu.VMEM)] * 2,
        out_specs=pl.BlockSpec(memory_space=pltpu.VMEM),
        compiler_params=pltpu.CompilerParams(vmem_limit_bytes=8 * MIB),
    )(kept, came)


def gather_kernel(*refs):
    halves, (grad_qkv_ref, grad_out_ref) = (refs[:3], refs[3:6]), refs[6:]
    middle = refs[0].shape[2]
    rest = grad_qkv_ref.shape[1] - middle
    sums = [kept[0] + came[0].astype(jnp.float32) + last[...].astype(jnp.float32) for kept, came, last in halves]
    grad_qkv_ref[:, pl.ds(0, middle)] = sums[0]
    grad_qkv_ref[:, pl.ds(middle, rest)] = sums[1][:, :rest]
    grad_out_ref[...] = sums[1][:, rest:]


def gather(near, far):
    _, rows, half = near[0].shape
    return pl.pallas_call(
        gather_kernel,
        out_shape=[
            jax.ShapeDtypeStruct((rows, half // 2 * 3), jnp.float32),
            jax.ShapeDtypeStruct((rows, half // 2), jnp.float32),
        ],
        in_specs=[pl.BlockSpec(memory_space=pltpu.VMEM)] * 6,
        out_specs=[pl.BlockSpec(memory_space=pltpu.VMEM)] * 2,
        compiler_params=pltpu.CompilerParams(vmem_limit_bytes=8 * MIB),
    )(*near, *far)


def finish_kernel(*refs):
    addends, (grad_qkv_ref, grad_out_ref) = refs[:-2], refs[-2:]
    wide = grad_qkv_ref.shape[1]
    everything = slice(None)
    grad_qkv_ref[...] = summed(addends, (everything, pl.ds(0, wide)))
    grad_out_ref[...] = summed(addends, (everything, pl.ds(wide, grad_out_ref.shape[1])))


def finish(addends):
    rows, columns = addends[0].shape
    return pl.pallas_call(
        finish_kernel,
        out_shape=[
            jax.ShapeDtypeStruct((rows, columns // 4 * 3), jnp.float32),
            jax.ShapeDtypeStruct((rows, columns // 4), jnp.float32),
        ],
        in_specs=[pl.BlockSpec(memory_space=pltpu.VMEM)] * len(addends),
        out_specs=[pl.BlockSpec(memory_space=pltpu.VMEM)] * 2,
        compiler_params=pltpu.CompilerParams(vmem_limit_bytes=8 * MIB),
    )(*addends)


def sublayer_kernel(at, n_clips, n_positions, n_pieces, n_before, *refs):
    pieces, refs = refs[:n_pieces], refs[n_pieces:]
    w_qkv_ref, w_out_ref = refs[:2]
    before, refs = refs[2 : 2 + n_before], refs[2 + n_before :]
    normed_ref, cot_ref, mixed_ref, dq_ref, dk_ref, dv_ref = refs[:6]
    dx_refs = refs[6:]
    rows = normed_ref.shape[0] // n_clips
    span = rows // n_pieces
    width = w_out_ref.shape[0]
    wide = width // HEADS * GROUP
    depth = wide // GROUP
    scaling = depth**-0.5

    def piece(k, which, clip):
        return pieces[k][which, clip if pieces[k].shape[1] == n_clips else at + clip]

    raw = jnp.concatenate([piece(k, 0, clip) for clip in range(n_clips) for k in range(n_pieces)], axis=0)
    unit, _ = statistics(raw.astype(jnp.float32))
    normed_ref[...] = unit.astype(jnp.bfloat16)
    for clip in range(n_clips):
        for k in range(n_pieces):
            cot_ref[pl.ds(clip * rows + k * span, span)] = piece(k, 1, clip)

    lane_head = lax.broadcasted_iota(jnp.int32, (rows, wide), 1) // depth
    head_masks = [(lane_head == h).astype(jnp.float32).astype(jnp.bfloat16) for h in range(GROUP)]
    key_pos = lax.broadcasted_iota(jnp.int32, (rows, rows), 0) % n_positions
    query_pos = lax.broadcasted_iota(jnp.int32, (rows, rows), 1) % n_positions
    same = (key_pos == query_pos)[None]

    def stacked(block):
        return jnp.concatenate([block * mask for mask in head_masks], axis=0)

    def side_by_side(blocks):
        return jnp.concatenate([blocks[h] for h in range(GROUP)], axis=1)

    for group in range(HEADS // GROUP):
        columns = slice(group * wide, (group + 1) * wide)
        all_queries, all_keys, all_values = (
            contract(normed_ref[...], w_qkv_ref[:, pl.ds(i * width + group * wide, wide)], ((1,), (0,))).astype(
                jnp.bfloat16
            )
            for i in range(3)
        )
        mixed_grad = contract(cot_ref[...], w_out_ref[columns, :], ((1,), (1,))).astype(jnp.bfloat16)
        for clip in range(n_clips):
            here = slice(clip * rows, (clip + 1) * rows)
            queries = all_queries[here]
            keys = stacked(all_keys[here])
            values = stacked(all_values[here])
            upstream = mixed_grad[here]
            scores = contract(keys, queries, ((1,), (1,))).reshape(GROUP, rows, rows)
            scores = jnp.where(same, scores, LOWEST)
            highest = jnp.max(scores, axis=1, keepdims=True)
            expo = jnp.exp2((scores - highest) * (scaling * LOG2E))
            full = expo * (1.0 / jnp.sum(expo, axis=1, keepdims=True))
            low = full.astype(jnp.bfloat16)
            dots = contract(values, upstream * jnp.bfloat16(scaling), ((1,), (1,)))
            dots = dots.reshape(GROUP, rows, rows)
            score_grad = full * (dots - jnp.sum(full * dots, axis=1, keepdims=True))
            score_grad = score_grad.astype(jnp.bfloat16)
            mixed = contract(low.reshape(GROUP * rows, rows), values, ((0,), (0,)))
            mixed_ref[here, columns] = mixed.astype(jnp.bfloat16)
            dq = contract(score_grad.reshape(GROUP * rows, rows), keys, ((0,), (0,)))
            dq_ref[here, columns] = dq.astype(jnp.bfloat16)
            dk = contract(side_by_side(score_grad), stacked(queries), ((1,), (0,)))
            dk_ref[here, columns] = dk.astype(jnp.bfloat16)
            dv = contract(side_by_side(low), stacked(upstream), ((1,), (0,)))
            dv_ref[here, columns] = dv.astype(jnp.bfloat16)

    grads = jnp.concatenate([dq_ref[...], dk_ref[...], dv_ref[...]], axis=1)
    total = contract(grads, w_qkv_ref[...], ((1,), (1,)))
    unit, inverse = statistics(raw.astype(jnp.float32))
    grad = inverse * (
        total
        - jnp.mean(total, axis=-1, keepdims=True)
        - unit * jnp.mean(total * unit, axis=-1, keepdims=True)
    )
    dx = (cot_ref[...].astype(jnp.float32) + grad).astype(jnp.bfloat16)
    for k in range(n_pieces):
        if before:
            dx_refs[k][:at] = before[k][...]
        for clip in range(n_clips):
            start = clip * rows + k * span
            dx_refs[k][at + clip] = dx[start : start + span]


def sublayer(pieces, at, n_clips, w_qkv, w_out, n_positions, before):
    _, _, span, width = pieces[0].shape
    rows = n_clips * len(pieces) * span
    flat = jax.ShapeDtypeStruct((rows, width), jnp.bfloat16)
    dx = jax.ShapeDtypeStruct((at + n_clips, span, width), jnp.bfloat16)
    operands = (*pieces, w_qkv, w_out, *before)
    return pl.pallas_call(
        functools.partial(sublayer_kernel, at, n_clips, n_positions, len(pieces), len(before)),
        out_shape=[flat] * 6 + [dx] * len(pieces),
        in_specs=[pl.BlockSpec(memory_space=pltpu.VMEM)] * len(operands),
        out_specs=[pl.BlockSpec(memory_space=pltpu.VMEM)] * (6 + len(pieces)),
        compiler_params=pltpu.CompilerParams(vmem_limit_bytes=32 * MIB),
        cost_estimate=pl.CostEstimate(
            flops=2 * rows * width * (7 * width + 24 * 128),
            bytes_accessed=16 * rows * width + 8 * width * width,
            transcendentals=rows * 128 * HEADS,
        ),
    )(*operands)


def swap(block, axis, size, distance):
    return lax.ppermute(block, axis, [(i, i ^ distance) for i in range(size)])


def after(values, done):
    values, _ = lax.optimization_barrier((values, done))
    return values


def inbound(near, far, n_tm):
    half = n_tm // 2
    near = [near[0]] + [swap(near[k], "tm", n_tm, k) for k in range(1, half)]
    arrived = []
    for blocks in far:
        gates = arrived[-1] if arrived else [near[2]] + [None] * (half - 1)
        blocks = [block if gate is None else after(block, gate) for block, gate in zip(blocks, gates)]
        done = {i: swap(blocks[i], "tm", n_tm, half + i) for i in reversed(range(half))}
        arrived.append([done[i] for i in range(half)])
    return near, arrived


def shards(n_clip_devices, n_tm, clips, w_qkv, w_out, cotangent):
    n_clips, _, n_patches, width = clips.shape
    n_positions = n_patches // n_tm
    n_x, n_z = n_clip_devices // CORES, n_tm // N_Y
    joined = n_positions % 16 != 0
    ids = jnp.stack([lax.axis_index("clip"), lax.axis_index("tm")]).astype(jnp.int32)

    near, far = inbound(*pick(ids, clips, cotangent, n_tm, CHUNKS), n_tm)
    depth = n_clips // CHUNKS
    factors, dx = [], []
    for chunk in range(CHUNKS):
        at = chunk * depth
        pieces = near + far[chunk]
        if joined:
            pieces = [p[:, at : at + depth] for p in near] + far[chunk]
            pieces = [jnp.stack(pieces, axis=2).reshape(2, depth, -1, width)]
        out = sublayer(pieces, at, depth, w_qkv, w_out, n_positions, dx)
        factors.append(out[:6])
        dx = list(out[6:])
    normed, cot, mixed, dq, dk, dv = zip(*factors)
    if joined:
        cut = dx[0].reshape(n_clips, n_tm, n_positions, width)
        dx = [cut[:, k] for k in range(n_tm)]

    cut = int(4 * width * FIRST) - 2 * width
    first_parts = ([normed], [dq, dk, dv]), ((0, 0, width), (0, 0, width), (0, 0, cut))
    second_parts = ([normed, mixed], [dv, cot]), ((0, cut, width - cut), (1, 0, width))
    sent_first = products(ids, 1, n_x, n_z, *first_parts[0], first_parts[1])
    first = swap(sent_first, "clip", n_clip_devices, 1)
    sent_second = products(ids, 1, n_x, n_z, *after(second_parts[0], sent_first), second_parts[1])
    second = swap(sent_second, "clip", n_clip_devices, 1)
    own_first = products(ids, 0, n_x, n_z, *after(first_parts[0], sent_second), first_parts[1])
    sent, own_first = halve(ids, (own_first, first), 0, 0, CORES)
    first = swap(sent, "clip", n_clip_devices, CORES)
    own_second = products(ids, 0, n_x, n_z, *after(second_parts[0], own_first), second_parts[1])
    sent, own_second = halve(ids, (own_second, second), 2, 1, 1)
    second = swap(sent, "tm", n_tm, 1)
    dx = after(dx, sent_second)
    late = (1, 3)
    back = {}
    for k in reversed([k for k in range(1, n_tm) if k not in late]):
        block = after(dx[k], back[k + 3]) if k + 3 in back else dx[k]
        back[k] = swap(block, "tm", n_tm, k)
    first, second = after((first, second), [back[k] for k in range(n_tm - 3, n_tm)])
    sent, own_first = halve(ids, (own_first, first), 1, 1, 1)
    first = swap(sent, "tm", n_tm, 1)
    sent, own_second = halve(ids, (own_second, second), 0, 0, CORES)
    second = swap(sent, "clip", n_clip_devices, CORES)
    first, second = after((first, second), back)
    if n_z == 4:
        *sent, near_kept, far_kept = cross(ids, (own_first, first), (own_second, second))
        far_came = swap(sent[1], "tm", n_tm, 2 * N_Y)
        near_came = swap(sent[0], "tm", n_tm, N_Y)
        near_last = swap(pass_on(near_kept, near_came), "tm", n_tm, 2 * N_Y)
        far_last = swap(pass_on(far_kept, far_came), "tm", n_tm, N_Y)
        grad_qkv, grad_out = gather((near_kept, near_came, near_last), (far_kept, far_came, far_last))
    else:
        total, *sent = join(ids, (own_first, first), (own_second, second), n_z)
        others = [swap(sent[j - 1], "tm", n_tm, j * N_Y) for j in reversed(range(1, n_z))]
        grad_qkv, grad_out = finish((total, *others))
    back[0] = dx[0]
    for k in late:
        back[k] = swap(after(dx[k], sent), "tm", n_tm, k)
    grad_clips = place(ids, [back[k] for k in range(n_tm)]).reshape(clips.shape)
    return (grad_clips, grad_qkv, grad_out)


def solution(mesh):
    return jax.shard_map(
        functools.partial(shards, mesh.shape["clip"], mesh.shape["tm"]),
        mesh=mesh,
        in_specs=(P("clip", "tm", None, None), P(), P(), P("clip", "tm", None, None)),
        out_specs=(P("clip", "tm", None, None), P(("clip", "tm"), None), P(("clip", "tm"), None)),
        check_vma=False,
    )
```

```python
import functools
import itertools

import jax
import jax.numpy as jnp
from jax import lax
from jax.experimental import pallas as pl
from jax.experimental.pallas import tpu as pltpu
from jax.sharding import PartitionSpec as P

HEADS = 16
GROUP = 4
FIRST = 9 / 16
CHUNKS = 2
CORES = 2
N_Y = 2
EPSILON = 1e-06
LOWEST = -1e30
LOG2E = 1.4426950408889634
MIB = 1024 * 1024


def contract(left, right, dims):
    return lax.dot_general(left, right, (dims, ((), ())), preferred_element_type=jnp.float32)


def statistics(rows32):
    mean = jnp.mean(rows32, axis=-1, keepdims=True)
    centred = rows32 - mean
    inverse = lax.rsqrt(jnp.mean(centred * centred, axis=-1, keepdims=True) + EPSILON)
    return centred * inverse, inverse


def pick_kernel(n_slots, n_chunks, ids_ref, x_ref, cot_ref, *out_refs):
    half = n_slots // 2
    depth = x_ref.shape[0] // n_chunks
    for i, ref in enumerate(out_refs):
        far = i - half
        here = slice(None) if far < 0 else pl.ds(far // half * depth, depth)
        slot = ids_ref[1] ^ (i if far < 0 else half + far % half)
        ref[0] = x_ref[here, slot]
        ref[1] = cot_ref[here, slot]


def pick(ids, clips, cotangent, n_slots, n_chunks):
    n_clips, _, n_patches, width = clips.shape
    cut = (n_clips, n_slots, n_patches // n_slots, width)
    half = n_slots // 2

    def piece(count):
        return jax.ShapeDtypeStruct((2, count) + cut[2:], clips.dtype)

    out = pl.pallas_call(
        functools.partial(pick_kernel, n_slots, n_chunks),
        out_shape=[piece(n_clips)] * half + [piece(n_clips // n_chunks)] * (half * n_chunks),
        in_specs=[pl.BlockSpec(memory_space=pltpu.SMEM)]
        + [pl.BlockSpec(memory_space=pltpu.VMEM)] * 2,
        out_specs=[pl.BlockSpec(memory_space=pltpu.VMEM)] * (half * (1 + n_chunks)),
        compiler_params=pltpu.CompilerParams(vmem_limit_bytes=12 * MIB),
    )(ids, clips.reshape(cut), cotangent.reshape(cut))
    far = [out[half + chunk * half :][:half] for chunk in range(n_chunks)]
    return out[:half], far


def fetch_kernel(w_ref, out_ref, sem):
    copy = pltpu.make_async_copy(w_ref, out_ref, sem)
    copy.start()
    copy.wait()


def fetch(weights):
    return pl.pallas_call(
        fetch_kernel,
        out_shape=jax.ShapeDtypeStruct(weights.shape, weights.dtype),
        in_specs=[pl.BlockSpec(memory_space=pltpu.HBM)],
        out_specs=pl.BlockSpec(memory_space=pltpu.VMEM),
        scratch_shapes=[pltpu.SemaphoreType.DMA],
        compiler_params=pltpu.CompilerParams(vmem_limit_bytes=42 * MIB),
    )(weights)


def place_kernel(ids_ref, *refs):
    for slot, ref in enumerate(refs[:-1]):
        refs[-1][:, ids_ref[1] ^ slot] = ref[...]


def place(ids, blocks):
    n_clips, n_positions, width = blocks[0].shape
    return pl.pallas_call(
        place_kernel,
        out_shape=jax.ShapeDtypeStruct((n_clips, len(blocks), n_positions, width), blocks[0].dtype),
        in_specs=[pl.BlockSpec(memory_space=pltpu.SMEM)]
        + [pl.BlockSpec(memory_space=pltpu.VMEM)] * len(blocks),
        out_specs=pl.BlockSpec(memory_space=pltpu.VMEM),
        compiler_params=pltpu.CompilerParams(vmem_limit_bytes=8 * MIB),
    )(ids, *blocks)


def product_kernel(n_x, flip, n_chunks, spans, ids_ref, *refs):
    lefts, rights, out_ref = refs[: -1 - len(spans) * n_chunks], refs[-1 - len(spans) * n_chunks : -1], refs[-1]
    width = lefts[0].shape[1]
    rest = width // (CORES * n_x)
    core = lax.rem(ids_ref[0], CORES) ^ flip
    starts = [pl.multiple_of((CORES * x + core) * rest, rest) for x in range(n_x)]
    turned = []
    for i in range(0, len(lefts), n_chunks):
        parts = [[left[:, pl.ds(start, rest)] for start in starts] for left in lefts[i : i + n_chunks]]
        turned.append(jnp.concatenate([jnp.concatenate(p, axis=1) for p in parts], axis=0).T)
    at = 0
    for i, (which, start, size) in enumerate(spans):
        right = [ref[:, pl.ds(start, size)] for ref in rights[i * n_chunks : (i + 1) * n_chunks]]
        product = contract(turned[which], jnp.concatenate(right, axis=0), ((1,), (0,)))
        out_ref[:, :, :, :, pl.ds(at, size)] = product.reshape(out_ref.shape[:4] + (size,)).astype(jnp.bfloat16)
        at += size


def products(ids, flip, n_x, n_z, lefts, rights, spans):
    n_chunks = len(rights[0])
    rows, width = rights[0][0].shape
    rest = width // (CORES * n_x * n_z * N_Y)
    columns = sum(size for _, _, size in spans)
    operands = [a for factor in lefts + rights for a in factor]
    return pl.pallas_call(
        functools.partial(product_kernel, n_x, flip, n_chunks, spans),
        out_shape=jax.ShapeDtypeStruct((n_x, n_z, N_Y, rest, columns), jnp.bfloat16),
        in_specs=[pl.BlockSpec(memory_space=pltpu.SMEM)]
        + [pl.BlockSpec(memory_space=pltpu.VMEM)] * len(operands),
        out_specs=pl.BlockSpec(memory_space=pltpu.VMEM),
        compiler_params=pltpu.CompilerParams(vmem_limit_bytes=24 * MIB),
        cost_estimate=pl.CostEstimate(
            flops=n_chunks * rows * width * columns // 4,
            bytes_accessed=n_chunks * rows * width,
            transcendentals=0,
        ),
    )(ids, *operands)


def summed(refs, index):
    total = refs[0][index].astype(jnp.float32)
    for ref in refs[1:]:
        total += ref[index].astype(jnp.float32)
    return total


def halve_kernel(dim, axis, stride, ids_ref, *refs):
    addends, sent_ref, kept_ref = refs[:-2], refs[-2], refs[-1]
    me = lax.rem(lax.div(ids_ref[axis], stride), 2)
    for index in itertools.product(*(range(n) for n in sent_ref.shape[:-2])):
        sent_ref[index] = summed(addends, index[:dim] + (me ^ 1,) + index[dim:]).astype(jnp.bfloat16)
    for index in itertools.product(*(range(n) for n in sent_ref.shape[:-2])):
        kept_ref[index] = summed(addends, index[:dim] + (me,) + index[dim:])


def halve(ids, addends, dim, axis, stride):
    shape = addends[0].shape[:dim] + addends[0].shape[dim + 1 :]
    return pl.pallas_call(
        functools.partial(halve_kernel, dim, axis, stride),
        out_shape=[jax.ShapeDtypeStruct(shape, jnp.bfloat16), jax.ShapeDtypeStruct(shape, jnp.float32)],
        in_specs=[pl.BlockSpec(memory_space=pltpu.SMEM)]
        + [pl.BlockSpec(memory_space=pltpu.VMEM)] * len(addends),
        out_specs=[pl.BlockSpec(memory_space=pltpu.VMEM)] * 2,
        compiler_params=pltpu.CompilerParams(vmem_limit_bytes=16 * MIB),
    )(ids, *addends)


def join_kernel(n_z, n_first, ids_ref, *refs):
    addends, outs = refs[:-n_z], refs[-n_z:]
    me = lax.div(ids_ref[1], N_Y)
    cut = addends[0].shape[-1]
    for j in [*range(1, n_z), 0]:
        outs[j][:, :cut] = summed(addends[:n_first], (me ^ j,)).astype(outs[j].dtype)
        outs[j][:, cut:] = summed(addends[n_first:], (me ^ j,)).astype(outs[j].dtype)


def join(ids, first, second, n_z):
    shape = (first[0].shape[1], first[0].shape[2] + second[0].shape[2])
    own = jax.ShapeDtypeStruct(shape, jnp.float32)
    other = jax.ShapeDtypeStruct(shape, jnp.bfloat16)
    return pl.pallas_call(
        functools.partial(join_kernel, n_z, len(first)),
        out_shape=[own] + [other] * (n_z - 1),
        in_specs=[pl.BlockSpec(memory_space=pltpu.SMEM)]
        + [pl.BlockSpec(memory_space=pltpu.VMEM)] * (len(first) + len(second)),
        out_specs=[pl.BlockSpec(memory_space=pltpu.VMEM)] * n_z,
        compiler_params=pltpu.CompilerParams(vmem_limit_bytes=12 * MIB),
    )(ids, *first, *second)


def finish_kernel(*refs):
    addends, (grad_qkv_ref, grad_out_ref) = refs[:-2], refs[-2:]
    wide = grad_qkv_ref.shape[1]
    everything = slice(None)
    grad_qkv_ref[...] = summed(addends, (everything, pl.ds(0, wide)))
    grad_out_ref[...] = summed(addends, (everything, pl.ds(wide, grad_out_ref.shape[1])))


def finish(addends):
    rows, columns = addends[0].shape
    return pl.pallas_call(
        finish_kernel,
        out_shape=[
            jax.ShapeDtypeStruct((rows, columns // 4 * 3), jnp.float32),
            jax.ShapeDtypeStruct((rows, columns // 4), jnp.float32),
        ],
        in_specs=[pl.BlockSpec(memory_space=pltpu.VMEM)] * len(addends),
        out_specs=[pl.BlockSpec(memory_space=pltpu.VMEM)] * 2,
        compiler_params=pltpu.CompilerParams(vmem_limit_bytes=8 * MIB),
    )(*addends)


def sublayer_kernel(at, n_clips, n_positions, n_pieces, n_before, *refs):
    pieces, refs = refs[:n_pieces], refs[n_pieces:]
    w_qkv_ref, w_out_ref = refs[:2]
    before, refs = refs[2 : 2 + n_before], refs[2 + n_before :]
    normed_ref, cot_ref, mixed_ref, dq_ref, dk_ref, dv_ref = refs[:6]
    dx_refs = refs[6:]
    rows = normed_ref.shape[0] // n_clips
    span = rows // n_pieces
    width = w_out_ref.shape[0]
    wide = width // HEADS * GROUP
    depth = wide // GROUP
    scaling = depth**-0.5

    def piece(k, which, clip):
        return pieces[k][which, clip if pieces[k].shape[1] == n_clips else at + clip]

    raw = jnp.concatenate([piece(k, 0, clip) for clip in range(n_clips) for k in range(n_pieces)], axis=0)
    unit, _ = statistics(raw.astype(jnp.float32))
    normed_ref[...] = unit.astype(jnp.bfloat16)
    for clip in range(n_clips):
        for k in range(n_pieces):
            cot_ref[pl.ds(clip * rows + k * span, span)] = piece(k, 1, clip)

    lane_head = lax.broadcasted_iota(jnp.int32, (rows, wide), 1) // depth
    head_masks = [(lane_head == h).astype(jnp.float32).astype(jnp.bfloat16) for h in range(GROUP)]
    key_pos = lax.broadcasted_iota(jnp.int32, (rows, rows), 0) % n_positions
    query_pos = lax.broadcasted_iota(jnp.int32, (rows, rows), 1) % n_positions
    same = (key_pos == query_pos)[None]

    def stacked(block):
        return jnp.concatenate([block * mask for mask in head_masks], axis=0)

    def side_by_side(blocks):
        return jnp.concatenate([blocks[h] for h in range(GROUP)], axis=1)

    for group in range(HEADS // GROUP):
        columns = slice(group * wide, (group + 1) * wide)
        all_queries, all_keys, all_values = (
            contract(normed_ref[...], w_qkv_ref[:, pl.ds(i * width + group * wide, wide)], ((1,), (0,))).astype(
                jnp.bfloat16
            )
            for i in range(3)
        )
        mixed_grad = contract(cot_ref[...], w_out_ref[columns, :], ((1,), (1,))).astype(jnp.bfloat16)
        for clip in range(n_clips):
            here = slice(clip * rows, (clip + 1) * rows)
            queries = all_queries[here]
            keys = stacked(all_keys[here])
            values = stacked(all_values[here])
            upstream = mixed_grad[here]
            scores = contract(keys, queries, ((1,), (1,))).reshape(GROUP, rows, rows)
            scores = jnp.where(same, scores, LOWEST)
            highest = jnp.max(scores, axis=1, keepdims=True)
            expo = jnp.exp2((scores - highest) * (scaling * LOG2E))
            full = expo * (1.0 / jnp.sum(expo, axis=1, keepdims=True))
            low = full.astype(jnp.bfloat16)
            dots = contract(values, upstream * jnp.bfloat16(scaling), ((1,), (1,)))
            dots = dots.reshape(GROUP, rows, rows)
            score_grad = full * (dots - jnp.sum(full * dots, axis=1, keepdims=True))
            score_grad = score_grad.astype(jnp.bfloat16)
            mixed = contract(low.reshape(GROUP * rows, rows), values, ((0,), (0,)))
            mixed_ref[here, columns] = mixed.astype(jnp.bfloat16)
            dq = contract(score_grad.reshape(GROUP * rows, rows), keys, ((0,), (0,)))
            dq_ref[here, columns] = dq.astype(jnp.bfloat16)
            dk = contract(side_by_side(score_grad), stacked(queries), ((1,), (0,)))
            dk_ref[here, columns] = dk.astype(jnp.bfloat16)
            dv = contract(side_by_side(low), stacked(upstream), ((1,), (0,)))
            dv_ref[here, columns] = dv.astype(jnp.bfloat16)

    grads = jnp.concatenate([dq_ref[...], dk_ref[...], dv_ref[...]], axis=1)
    total = contract(grads, w_qkv_ref[...], ((1,), (1,)))
    unit, inverse = statistics(raw.astype(jnp.float32))
    grad = inverse * (
        total
        - jnp.mean(total, axis=-1, keepdims=True)
        - unit * jnp.mean(total * unit, axis=-1, keepdims=True)
    )
    dx = (cot_ref[...].astype(jnp.float32) + grad).astype(jnp.bfloat16)
    for k in range(n_pieces):
        if before:
            dx_refs[k][:at] = before[k][...]
        for clip in range(n_clips):
            start = clip * rows + k * span
            dx_refs[k][at + clip] = dx[start : start + span]


def sublayer(pieces, at, n_clips, w_qkv, w_out, n_positions, before):
    _, _, span, width = pieces[0].shape
    rows = n_clips * len(pieces) * span
    flat = jax.ShapeDtypeStruct((rows, width), jnp.bfloat16)
    dx = jax.ShapeDtypeStruct((at + n_clips, span, width), jnp.bfloat16)
    operands = (*pieces, w_qkv, w_out, *before)
    return pl.pallas_call(
        functools.partial(sublayer_kernel, at, n_clips, n_positions, len(pieces), len(before)),
        out_shape=[flat] * 6 + [dx] * len(pieces),
        in_specs=[pl.BlockSpec(memory_space=pltpu.VMEM)] * len(operands),
        out_specs=[pl.BlockSpec(memory_space=pltpu.VMEM)] * (6 + len(pieces)),
        compiler_params=pltpu.CompilerParams(vmem_limit_bytes=32 * MIB),
        cost_estimate=pl.CostEstimate(
            flops=2 * rows * width * (7 * width + 24 * 128),
            bytes_accessed=16 * rows * width + 8 * width * width,
            transcendentals=rows * 128 * HEADS,
        ),
    )(*operands)


def swap(block, axis, size, distance):
    return lax.ppermute(block, axis, [(i, i ^ distance) for i in range(size)])


def after(values, done):
    values, _ = lax.optimization_barrier((values, done))
    return values


def inbound(near, far, ready, n_tm):
    half = n_tm // 2
    order, gates = list(range(1, n_tm)), {}
    if half == 4:
        order, gates = [3, 2, 5, 7, 1, 4, 6], {7: 5}
    near = list(near)
    blocks = near + list(far[0])
    for k in order:
        block = after(blocks[k], blocks[gates[k]]) if k in gates else blocks[k]
        blocks[k] = swap(block, "tm", n_tm, k)
    near, arrived = blocks[:half], [blocks[half:]]
    extra = {0: [ready], 3: [near[-1]]}
    for chunk in far[1:]:
        done = list(chunk)
        for i in (0, *reversed(range(1, half))):
            gate = (arrived[-1][i], extra.get(i, [near[1]]))
            done[i] = swap(after(chunk[i], gate), "tm", n_tm, half + i)
        arrived.append(done)
    return near, arrived


def shards(n_clip_devices, n_tm, clips, w_qkv, w_out, cotangent):
    n_clips, _, n_patches, width = clips.shape
    n_positions = n_patches // n_tm
    n_x, n_z = n_clip_devices // CORES, n_tm // N_Y
    joined = n_positions % 16 != 0
    ids = jnp.stack([lax.axis_index("clip"), lax.axis_index("tm")]).astype(jnp.int32)

    near, far = pick(ids, clips, cotangent, n_tm, CHUNKS)
    w_qkv = fetch(w_qkv)
    near, far = inbound(near, far, w_qkv, n_tm)
    depth = n_clips // CHUNKS
    factors, dx = [], []
    for chunk in range(CHUNKS):
        at = chunk * depth
        pieces = near + far[chunk]
        if joined:
            pieces = [p[:, at : at + depth] for p in near] + far[chunk]
            pieces = [jnp.stack(pieces, axis=2).reshape(2, depth, -1, width)]
        out = sublayer(pieces, at, depth, w_qkv, w_out, n_positions, dx)
        factors.append(out[:6])
        dx = list(out[6:])
    normed, cot, mixed, dq, dk, dv = zip(*factors)
    if joined:
        cut = dx[0].reshape(n_clips, n_tm, n_positions, width)
        dx = [cut[:, k] for k in range(n_tm)]

    cut = int(4 * width * FIRST) - 2 * width
    first_parts = ([normed], [dq, dk, dv]), ((0, 0, width), (0, 0, width), (0, 0, cut))
    second_parts = ([normed, mixed], [dv, cot]), ((0, cut, width - cut), (1, 0, width))
    sent_first = products(ids, 1, n_x, n_z, *first_parts[0], first_parts[1])
    first = swap(sent_first, "clip", n_clip_devices, 1)
    sent_second = products(ids, 1, n_x, n_z, *after(second_parts[0], sent_first), second_parts[1])
    second = swap(sent_second, "clip", n_clip_devices, 1)
    own_first = products(ids, 0, n_x, n_z, *after(first_parts[0], sent_second), first_parts[1])
    sent, own_first = halve(ids, (own_first, first), 0, 0, CORES)
    first = swap(sent, "clip", n_clip_devices, CORES)
    own_second = products(ids, 0, n_x, n_z, *after(second_parts[0], own_first), second_parts[1])
    sent, own_second = halve(ids, (own_second, second), 2, 1, 1)
    second = swap(sent, "tm", n_tm, 1)
    dx = after(dx, sent_second)
    late = (1, 3)
    back = {}
    for k in reversed([k for k in range(1, n_tm) if k not in late]):
        block = after(dx[k], back[k + 3]) if k + 3 in back else dx[k]
        back[k] = swap(block, "tm", n_tm, k)
    first, second = after((first, second), [back[k] for k in range(n_tm - 3, n_tm)])
    sent, own_first = halve(ids, (own_first, first), 1, 1, 1)
    first = swap(sent, "tm", n_tm, 1)
    sent, own_second = halve(ids, (own_second, second), 0, 0, CORES)
    second = swap(sent, "clip", n_clip_devices, CORES)
    first, second = after((first, second), back)
    total, *sent = join(ids, (own_first, first), (own_second, second), n_z)
    others = [swap(sent[j - 1], "tm", n_tm, j * N_Y) for j in reversed(range(1, n_z))]
    back[0] = dx[0]
    for k in late:
        back[k] = swap(after(dx[k], sent), "tm", n_tm, k)
    grad_clips = place(ids, [back[k] for k in range(n_tm)]).reshape(clips.shape)
    grad_qkv, grad_out = finish((total, *others))
    return (grad_clips, grad_qkv, grad_out)


def solution(mesh):
    return jax.shard_map(
        functools.partial(shards, mesh.shape["clip"], mesh.shape["tm"]),
        mesh=mesh,
        in_specs=(P("clip", "tm", None, None), P(), P(), P("clip", "tm", None, None)),
        out_specs=(P("clip", "tm", None, None), P(("clip", "tm"), None), P(("clip", "tm"), None)),
        check_vma=False,
    )
```

```python
import functools
import itertools

import jax
import jax.numpy as jnp
from jax import lax
from jax.experimental import pallas as pl
from jax.experimental.pallas import tpu as pltpu
from jax.sharding import PartitionSpec as P

HEADS = 16
GROUP = 4
FIRST = 9 / 16
CHUNKS = 2
CORES = 2
N_Y = 2
EPSILON = 1e-06
LOWEST = -1e30
LOG2E = 1.4426950408889634
MIB = 1024 * 1024


def contract(left, right, dims):
    return lax.dot_general(left, right, (dims, ((), ())), preferred_element_type=jnp.float32)


def statistics(rows32):
    mean = jnp.mean(rows32, axis=-1, keepdims=True)
    centred = rows32 - mean
    inverse = lax.rsqrt(jnp.mean(centred * centred, axis=-1, keepdims=True) + EPSILON)
    return centred * inverse, inverse


def pick_kernel(n_slots, n_chunks, ids_ref, x_ref, cot_ref, *out_refs):
    half = n_slots // 2
    depth = x_ref.shape[0] // n_chunks
    for i, ref in enumerate(out_refs):
        far = i - half
        here = slice(None) if far < 0 else pl.ds(far // half * depth, depth)
        slot = ids_ref[1] ^ (i if far < 0 else half + far % half)
        ref[0] = x_ref[here, slot]
        ref[1] = cot_ref[here, slot]


def pick(ids, clips, cotangent, n_slots, n_chunks):
    n_clips, _, n_patches, width = clips.shape
    cut = (n_clips, n_slots, n_patches // n_slots, width)
    half = n_slots // 2

    def piece(count):
        return jax.ShapeDtypeStruct((2, count) + cut[2:], clips.dtype)

    out = pl.pallas_call(
        functools.partial(pick_kernel, n_slots, n_chunks),
        out_shape=[piece(n_clips)] * half + [piece(n_clips // n_chunks)] * (half * n_chunks),
        in_specs=[pl.BlockSpec(memory_space=pltpu.SMEM)]
        + [pl.BlockSpec(memory_space=pltpu.VMEM)] * 2,
        out_specs=[pl.BlockSpec(memory_space=pltpu.VMEM)] * (half * (1 + n_chunks)),
        compiler_params=pltpu.CompilerParams(vmem_limit_bytes=12 * MIB),
    )(ids, clips.reshape(cut), cotangent.reshape(cut))
    far = [out[half + chunk * half :][:half] for chunk in range(n_chunks)]
    return out[:half], far


def fetch_kernel(w_ref, out_ref, sem):
    copy = pltpu.make_async_copy(w_ref, out_ref, sem)
    copy.start()
    copy.wait()


def fetch(weights):
    return pl.pallas_call(
        fetch_kernel,
        out_shape=jax.ShapeDtypeStruct(weights.shape, weights.dtype),
        in_specs=[pl.BlockSpec(memory_space=pltpu.HBM)],
        out_specs=pl.BlockSpec(memory_space=pltpu.VMEM),
        scratch_shapes=[pltpu.SemaphoreType.DMA],
        compiler_params=pltpu.CompilerParams(vmem_limit_bytes=42 * MIB),
    )(weights)


def place_kernel(ids_ref, *refs):
    for slot, ref in enumerate(refs[:-1]):
        refs[-1][:, ids_ref[1] ^ slot] = ref[...]


def place(ids, blocks):
    n_clips, n_positions, width = blocks[0].shape
    return pl.pallas_call(
        place_kernel,
        out_shape=jax.ShapeDtypeStruct((n_clips, len(blocks), n_positions, width), blocks[0].dtype),
        in_specs=[pl.BlockSpec(memory_space=pltpu.SMEM)]
        + [pl.BlockSpec(memory_space=pltpu.VMEM)] * len(blocks),
        out_specs=pl.BlockSpec(memory_space=pltpu.VMEM),
        compiler_params=pltpu.CompilerParams(vmem_limit_bytes=8 * MIB),
    )(ids, *blocks)


def product_kernel(n_x, flip, n_chunks, spans, ids_ref, *refs):
    lefts, rights, out_ref = refs[: -1 - len(spans) * n_chunks], refs[-1 - len(spans) * n_chunks : -1], refs[-1]
    width = lefts[0].shape[1]
    rest = width // (CORES * n_x)
    core = lax.rem(ids_ref[0], CORES) ^ flip
    starts = [pl.multiple_of((CORES * x + core) * rest, rest) for x in range(n_x)]
    turned = []
    for i in range(0, len(lefts), n_chunks):
        parts = [[left[:, pl.ds(start, rest)] for start in starts] for left in lefts[i : i + n_chunks]]
        turned.append(jnp.concatenate([jnp.concatenate(p, axis=1) for p in parts], axis=0).T)
    at = 0
    for i, (which, start, size) in enumerate(spans):
        right = [ref[:, pl.ds(start, size)] for ref in rights[i * n_chunks : (i + 1) * n_chunks]]
        product = contract(turned[which], jnp.concatenate(right, axis=0), ((1,), (0,)))
        out_ref[:, :, :, :, pl.ds(at, size)] = product.reshape(out_ref.shape[:4] + (size,)).astype(jnp.bfloat16)
        at += size


def products(ids, flip, n_x, n_z, lefts, rights, spans):
    n_chunks = len(rights[0])
    rows, width = rights[0][0].shape
    rest = width // (CORES * n_x * n_z * N_Y)
    columns = sum(size for _, _, size in spans)
    operands = [a for factor in lefts + rights for a in factor]
    return pl.pallas_call(
        functools.partial(product_kernel, n_x, flip, n_chunks, spans),
        out_shape=jax.ShapeDtypeStruct((n_x, n_z, N_Y, rest, columns), jnp.bfloat16),
        in_specs=[pl.BlockSpec(memory_space=pltpu.SMEM)]
        + [pl.BlockSpec(memory_space=pltpu.VMEM)] * len(operands),
        out_specs=pl.BlockSpec(memory_space=pltpu.VMEM),
        compiler_params=pltpu.CompilerParams(vmem_limit_bytes=24 * MIB),
        cost_estimate=pl.CostEstimate(
            flops=n_chunks * rows * width * columns // 4,
            bytes_accessed=n_chunks * rows * width,
            transcendentals=0,
        ),
    )(ids, *operands)


def summed(refs, index):
    total = refs[0][index].astype(jnp.float32)
    for ref in refs[1:]:
        total += ref[index].astype(jnp.float32)
    return total


def halve_kernel(dim, axis, stride, ids_ref, *refs):
    addends, sent_ref, kept_ref = refs[:-2], refs[-2], refs[-1]
    me = lax.rem(lax.div(ids_ref[axis], stride), 2)
    for index in itertools.product(*(range(n) for n in sent_ref.shape[:-2])):
        sent_ref[index] = summed(addends, index[:dim] + (me ^ 1,) + index[dim:]).astype(jnp.bfloat16)
    for index in itertools.product(*(range(n) for n in sent_ref.shape[:-2])):
        kept_ref[index] = summed(addends, index[:dim] + (me,) + index[dim:])


def halve(ids, addends, dim, axis, stride):
    shape = addends[0].shape[:dim] + addends[0].shape[dim + 1 :]
    return pl.pallas_call(
        functools.partial(halve_kernel, dim, axis, stride),
        out_shape=[jax.ShapeDtypeStruct(shape, jnp.bfloat16), jax.ShapeDtypeStruct(shape, jnp.float32)],
        in_specs=[pl.BlockSpec(memory_space=pltpu.SMEM)]
        + [pl.BlockSpec(memory_space=pltpu.VMEM)] * len(addends),
        out_specs=[pl.BlockSpec(memory_space=pltpu.VMEM)] * 2,
        compiler_params=pltpu.CompilerParams(vmem_limit_bytes=16 * MIB),
    )(ids, *addends)


def join_kernel(n_z, n_first, ids_ref, *refs):
    addends, outs = refs[:-n_z], refs[-n_z:]
    me = lax.div(ids_ref[1], N_Y)
    cut = addends[0].shape[-1]
    for j in [*range(1, n_z), 0]:
        outs[j][:, :cut] = summed(addends[:n_first], (me ^ j,)).astype(outs[j].dtype)
        outs[j][:, cut:] = summed(addends[n_first:], (me ^ j,)).astype(outs[j].dtype)


def join(ids, first, second, n_z):
    shape = (first[0].shape[1], first[0].shape[2] + second[0].shape[2])
    own = jax.ShapeDtypeStruct(shape, jnp.float32)
    other = jax.ShapeDtypeStruct(shape, jnp.bfloat16)
    return pl.pallas_call(
        functools.partial(join_kernel, n_z, len(first)),
        out_shape=[own] + [other] * (n_z - 1),
        in_specs=[pl.BlockSpec(memory_space=pltpu.SMEM)]
        + [pl.BlockSpec(memory_space=pltpu.VMEM)] * (len(first) + len(second)),
        out_specs=[pl.BlockSpec(memory_space=pltpu.VMEM)] * n_z,
        compiler_params=pltpu.CompilerParams(vmem_limit_bytes=12 * MIB),
    )(ids, *first, *second)


def finish_kernel(*refs):
    addends, (grad_qkv_ref, grad_out_ref) = refs[:-2], refs[-2:]
    wide = grad_qkv_ref.shape[1]
    everything = slice(None)
    grad_qkv_ref[...] = summed(addends, (everything, pl.ds(0, wide)))
    grad_out_ref[...] = summed(addends, (everything, pl.ds(wide, grad_out_ref.shape[1])))


def finish(addends):
    rows, columns = addends[0].shape
    return pl.pallas_call(
        finish_kernel,
        out_shape=[
            jax.ShapeDtypeStruct((rows, columns // 4 * 3), jnp.float32),
            jax.ShapeDtypeStruct((rows, columns // 4), jnp.float32),
        ],
        in_specs=[pl.BlockSpec(memory_space=pltpu.VMEM)] * len(addends),
        out_specs=[pl.BlockSpec(memory_space=pltpu.VMEM)] * 2,
        compiler_params=pltpu.CompilerParams(vmem_limit_bytes=8 * MIB),
    )(*addends)


def raw_rows(pieces, at, n_clips):
    parts = []
    for clip in range(n_clips):
        parts += [p[0, clip if p.shape[1] == n_clips else at + clip] for p in pieces]
    return jnp.concatenate(parts, axis=0).astype(jnp.float32)


def sublayer_kernel(at, n_clips, n_positions, n_pieces, *refs):
    pieces, refs = refs[:n_pieces], refs[n_pieces:]
    w_qkv_ref, w_out_ref = refs[:2]
    normed_ref, cot_ref, mixed_ref, dq_ref, dk_ref, dv_ref = refs[2:]
    rows = normed_ref.shape[0] // n_clips
    span = rows // n_pieces
    width = w_out_ref.shape[0]
    wide = width // HEADS * GROUP
    depth = wide // GROUP
    scaling = depth**-0.5

    unit, _ = statistics(raw_rows(pieces, at, n_clips))
    normed_ref[...] = unit.astype(jnp.bfloat16)
    for clip in range(n_clips):
        for k, piece in enumerate(pieces):
            source = clip if piece.shape[1] == n_clips else at + clip
            cot_ref[pl.ds(clip * rows + k * span, span)] = piece[1, source]

    lane_head = lax.broadcasted_iota(jnp.int32, (rows, wide), 1) // depth
    head_masks = [(lane_head == h).astype(jnp.float32).astype(jnp.bfloat16) for h in range(GROUP)]
    key_pos = lax.broadcasted_iota(jnp.int32, (rows, rows), 0) % n_positions
    query_pos = lax.broadcasted_iota(jnp.int32, (rows, rows), 1) % n_positions
    same = (key_pos == query_pos)[None]

    def stacked(block):
        return jnp.concatenate([block * mask for mask in head_masks], axis=0)

    def side_by_side(blocks):
        return jnp.concatenate([blocks[h] for h in range(GROUP)], axis=1)

    for group in range(HEADS // GROUP):
        columns = slice(group * wide, (group + 1) * wide)
        all_queries, all_keys, all_values = (
            contract(normed_ref[...], w_qkv_ref[:, pl.ds(i * width + group * wide, wide)], ((1,), (0,))).astype(
                jnp.bfloat16
            )
            for i in range(3)
        )
        mixed_grad = contract(cot_ref[...], w_out_ref[columns, :], ((1,), (1,))).astype(jnp.bfloat16)
        for clip in range(n_clips):
            here = slice(clip * rows, (clip + 1) * rows)
            queries = all_queries[here]
            keys = stacked(all_keys[here])
            values = stacked(all_values[here])
            upstream = mixed_grad[here]
            scores = contract(keys, queries, ((1,), (1,))).reshape(GROUP, rows, rows)
            scores = jnp.where(same, scores, LOWEST)
            highest = jnp.max(scores, axis=1, keepdims=True)
            expo = jnp.exp2((scores - highest) * (scaling * LOG2E))
            full = expo * (1.0 / jnp.sum(expo, axis=1, keepdims=True))
            low = full.astype(jnp.bfloat16)
            dots = contract(values, upstream * jnp.bfloat16(scaling), ((1,), (1,)))
            dots = dots.reshape(GROUP, rows, rows)
            score_grad = full * (dots - jnp.sum(full * dots, axis=1, keepdims=True))
            score_grad = score_grad.astype(jnp.bfloat16)
            mixed = contract(low.reshape(GROUP * rows, rows), values, ((0,), (0,)))
            mixed_ref[here, columns] = mixed.astype(jnp.bfloat16)
            dq = contract(score_grad.reshape(GROUP * rows, rows), keys, ((0,), (0,)))
            dq_ref[here, columns] = dq.astype(jnp.bfloat16)
            dk = contract(side_by_side(score_grad), stacked(queries), ((1,), (0,)))
            dk_ref[here, columns] = dk.astype(jnp.bfloat16)
            dv = contract(side_by_side(low), stacked(upstream), ((1,), (0,)))
            dv_ref[here, columns] = dv.astype(jnp.bfloat16)


def sublayer(pieces, at, n_clips, w_qkv, w_out, n_positions):
    _, _, span, width = pieces[0].shape
    rows = n_clips * len(pieces) * span
    flat = jax.ShapeDtypeStruct((rows, width), jnp.bfloat16)
    operands = (*pieces, w_qkv, w_out)
    return pl.pallas_call(
        functools.partial(sublayer_kernel, at, n_clips, n_positions, len(pieces)),
        out_shape=[flat] * 6,
        in_specs=[pl.BlockSpec(memory_space=pltpu.VMEM)] * len(operands),
        out_specs=[pl.BlockSpec(memory_space=pltpu.VMEM)] * 6,
        compiler_params=pltpu.CompilerParams(vmem_limit_bytes=30 * MIB),
        cost_estimate=pl.CostEstimate(
            flops=2 * rows * width * (4 * width + 24 * 128),
            bytes_accessed=16 * rows * width + 8 * width * width,
            transcendentals=rows * 128 * HEADS,
        ),
    )(*operands)


def input_kernel(at, n_clips, n_pieces, n_before, *refs):
    pieces, refs = refs[:n_pieces], refs[n_pieces:]
    w_qkv_ref, cot_ref, dq_ref, dk_ref, dv_ref = refs[:5]
    before, dx_refs = refs[5 : 5 + n_before], refs[5 + n_before :]
    rows = cot_ref.shape[0] // n_clips
    span = rows // n_pieces
    grads = jnp.concatenate([dq_ref[...], dk_ref[...], dv_ref[...]], axis=1)
    total = contract(grads, w_qkv_ref[...], ((1,), (1,)))
    unit, inverse = statistics(raw_rows(pieces, at, n_clips))
    grad = inverse * (
        total
        - jnp.mean(total, axis=-1, keepdims=True)
        - unit * jnp.mean(total * unit, axis=-1, keepdims=True)
    )
    dx = (cot_ref[...].astype(jnp.float32) + grad).astype(jnp.bfloat16)
    for k in range(n_pieces):
        if before:
            dx_refs[k][:at] = before[k][...]
        for clip in range(n_clips):
            start = clip * rows + k * span
            dx_refs[k][at + clip] = dx[start : start + span]


def input_gradient(pieces, at, n_clips, w_qkv, cot, dq, dk, dv, before):
    _, _, span, width = pieces[0].shape
    dx = jax.ShapeDtypeStruct((at + n_clips, span, width), jnp.bfloat16)
    operands = (*pieces, w_qkv, cot, dq, dk, dv, *before)
    return pl.pallas_call(
        functools.partial(input_kernel, at, n_clips, len(pieces), len(before)),
        out_shape=[dx] * len(pieces),
        in_specs=[pl.BlockSpec(memory_space=pltpu.VMEM)] * len(operands),
        out_specs=[pl.BlockSpec(memory_space=pltpu.VMEM)] * len(pieces),
        compiler_params=pltpu.CompilerParams(vmem_limit_bytes=24 * MIB),
        cost_estimate=pl.CostEstimate(
            flops=6 * cot.shape[0] * width * width,
            bytes_accessed=8 * cot.shape[0] * width + 6 * width * width,
            transcendentals=0,
        ),
    )(*operands)


def swap(block, axis, size, distance):
    return lax.ppermute(block, axis, [(i, i ^ distance) for i in range(size)])


def after(values, done):
    values, _ = lax.optimization_barrier((values, done))
    return values


def inbound(near, far, ready, n_tm):
    half = n_tm // 2
    order, gates = list(range(1, n_tm)), {}
    if half == 4:
        order, gates = [3, 2, 5, 7, 1, 4, 6], {7: 5}
    near = list(near)
    blocks = near + list(far[0])
    for k in order:
        block = after(blocks[k], blocks[gates[k]]) if k in gates else blocks[k]
        blocks[k] = swap(block, "tm", n_tm, k)
    near, arrived = blocks[:half], [blocks[half:]]
    extra = {0: [ready], 3: [near[-1]]}
    for chunk in far[1:]:
        done = list(chunk)
        for i in (0, *reversed(range(1, half))):
            gate = (arrived[-1][i], extra.get(i, [near[1]]))
            done[i] = swap(after(chunk[i], gate), "tm", n_tm, half + i)
        arrived.append(done)
    return near, arrived


def shards(n_clip_devices, n_tm, clips, w_qkv, w_out, cotangent):
    n_clips, _, n_patches, width = clips.shape
    n_positions = n_patches // n_tm
    n_x, n_z = n_clip_devices // CORES, n_tm // N_Y
    joined = n_positions % 16 != 0
    ids = jnp.stack([lax.axis_index("clip"), lax.axis_index("tm")]).astype(jnp.int32)

    near, far = pick(ids, clips, cotangent, n_tm, CHUNKS)
    w_qkv = fetch(w_qkv)
    near, far = inbound(near, far, w_qkv, n_tm)
    depth = n_clips // CHUNKS
    factors, dx = [], []
    for chunk in range(CHUNKS):
        at = chunk * depth
        pieces = near + far[chunk]
        if joined:
            pieces = [p[:, at : at + depth] for p in near] + far[chunk]
            pieces = [jnp.stack(pieces, axis=2).reshape(2, depth, -1, width)]
        factors.append(sublayer(after(pieces, dx), at, depth, w_qkv, w_out, n_positions))
        later = (pieces, [w_qkv, *(factors[-1][i] for i in (1, 3, 4, 5))])
        if chunk < CHUNKS - 1:
            dx = input_gradient(pieces, at, depth, *later[1], dx)
    normed, cot, mixed, dq, dk, dv = zip(*factors)
    cut = int(4 * width * FIRST) - 2 * width
    first_parts = ([normed], [dq, dk, dv]), ((0, 0, width), (0, 0, width), (0, 0, cut))
    second_parts = ([normed, mixed], [dv, cot]), ((0, cut, width - cut), (1, 0, width))
    sent_first = products(ids, 1, n_x, n_z, *first_parts[0], first_parts[1])
    first = swap(sent_first, "clip", n_clip_devices, 1)
    sent_second = products(ids, 1, n_x, n_z, *after(second_parts[0], sent_first), second_parts[1])
    second = swap(sent_second, "clip", n_clip_devices, 1)
    own_first = products(ids, 0, n_x, n_z, *after(first_parts[0], sent_second), first_parts[1])
    sent, own_first = halve(ids, (own_first, first), 0, 0, CORES)
    first = swap(sent, "clip", n_clip_devices, CORES)
    own_second = products(ids, 0, n_x, n_z, *after(second_parts[0], own_first), second_parts[1])
    sent, own_second = halve(ids, (own_second, second), 2, 1, 1)
    second = swap(sent, "tm", n_tm, 1)
    pieces, operands = after(later, sent)
    dx = input_gradient(pieces, n_clips - depth, depth, *operands, dx)
    if joined:
        cut = dx[0].reshape(n_clips, n_tm, n_positions, width)
        dx = [cut[:, k] for k in range(n_tm)]
    late = (1, 3)
    back = {}
    for k in reversed([k for k in range(1, n_tm) if k not in late]):
        block = after(dx[k], back[k + 3]) if k + 3 in back else dx[k]
        back[k] = swap(block, "tm", n_tm, k)
    first, second = after((first, second), [back[k] for k in range(n_tm - 3, n_tm)])
    sent, own_first = halve(ids, (own_first, first), 1, 1, 1)
    first = swap(sent, "tm", n_tm, 1)
    sent, own_second = halve(ids, (own_second, second), 0, 0, CORES)
    second = swap(sent, "clip", n_clip_devices, CORES)
    first, second = after((first, second), back)
    total, *sent = join(ids, (own_first, first), (own_second, second), n_z)
    others = [swap(sent[j - 1], "tm", n_tm, j * N_Y) for j in reversed(range(1, n_z))]
    back[0] = dx[0]
    for k in late:
        back[k] = swap(after(dx[k], sent), "tm", n_tm, k)
    grad_clips = place(ids, [back[k] for k in range(n_tm)]).reshape(clips.shape)
    grad_qkv, grad_out = finish((total, *others))
    return (grad_clips, grad_qkv, grad_out)


def solution(mesh):
    return jax.shard_map(
        functools.partial(shards, mesh.shape["clip"], mesh.shape["tm"]),
        mesh=mesh,
        in_specs=(P("clip", "tm", None, None), P(), P(), P("clip", "tm", None, None)),
        out_specs=(P("clip", "tm", None, None), P(("clip", "tm"), None), P(("clip", "tm"), None)),
        check_vma=False,
    )
```

```python
import functools
import itertools

import jax
import jax.numpy as jnp
from jax import lax
from jax.experimental import pallas as pl
from jax.experimental.pallas import tpu as pltpu
from jax.sharding import PartitionSpec as P

HEADS = 16
GROUP = 4
FIRST = 9 / 16
CHUNKS = 2
CORES = 2
N_Y = 2
EPSILON = 1e-06
LOWEST = -1e30
LOG2E = 1.4426950408889634
MIB = 1024 * 1024


def contract(left, right, dims):
    return lax.dot_general(left, right, (dims, ((), ())), preferred_element_type=jnp.float32)


def statistics(rows32):
    mean = jnp.mean(rows32, axis=-1, keepdims=True)
    centred = rows32 - mean
    inverse = lax.rsqrt(jnp.mean(centred * centred, axis=-1, keepdims=True) + EPSILON)
    return centred * inverse, inverse


def pick_kernel(n_slots, n_chunks, ids_ref, x_ref, cot_ref, *out_refs):
    half = n_slots // 2
    depth = x_ref.shape[0] // n_chunks
    for i, ref in enumerate(out_refs):
        far = i - half
        here = slice(None) if far < 0 else pl.ds(far // half * depth, depth)
        slot = ids_ref[1] ^ (i if far < 0 else half + far % half)
        ref[0] = x_ref[here, slot]
        ref[1] = cot_ref[here, slot]


def pick(ids, clips, cotangent, n_slots, n_chunks):
    n_clips, _, n_patches, width = clips.shape
    cut = (n_clips, n_slots, n_patches // n_slots, width)
    half = n_slots // 2

    def piece(count):
        return jax.ShapeDtypeStruct((2, count) + cut[2:], clips.dtype)

    out = pl.pallas_call(
        functools.partial(pick_kernel, n_slots, n_chunks),
        out_shape=[piece(n_clips)] * half + [piece(n_clips // n_chunks)] * (half * n_chunks),
        in_specs=[pl.BlockSpec(memory_space=pltpu.SMEM)]
        + [pl.BlockSpec(memory_space=pltpu.VMEM)] * 2,
        out_specs=[pl.BlockSpec(memory_space=pltpu.VMEM)] * (half * (1 + n_chunks)),
        compiler_params=pltpu.CompilerParams(vmem_limit_bytes=12 * MIB),
    )(ids, clips.reshape(cut), cotangent.reshape(cut))
    far = [out[half + chunk * half :][:half] for chunk in range(n_chunks)]
    return out[:half], far


def fetch_kernel(w_ref, out_ref, sem):
    copy = pltpu.make_async_copy(w_ref, out_ref, sem)
    copy.start()
    copy.wait()


def fetch(weights):
    return pl.pallas_call(
        fetch_kernel,
        out_shape=jax.ShapeDtypeStruct(weights.shape, weights.dtype),
        in_specs=[pl.BlockSpec(memory_space=pltpu.HBM)],
        out_specs=pl.BlockSpec(memory_space=pltpu.VMEM),
        scratch_shapes=[pltpu.SemaphoreType.DMA],
        compiler_params=pltpu.CompilerParams(vmem_limit_bytes=42 * MIB),
    )(weights)


def place_kernel(ids_ref, *refs):
    for slot, ref in enumerate(refs[:-1]):
        refs[-1][:, ids_ref[1] ^ slot] = ref[...]


def place(ids, blocks):
    n_clips, n_positions, width = blocks[0].shape
    return pl.pallas_call(
        place_kernel,
        out_shape=jax.ShapeDtypeStruct((n_clips, len(blocks), n_positions, width), blocks[0].dtype),
        in_specs=[pl.BlockSpec(memory_space=pltpu.SMEM)]
        + [pl.BlockSpec(memory_space=pltpu.VMEM)] * len(blocks),
        out_specs=pl.BlockSpec(memory_space=pltpu.VMEM),
        compiler_params=pltpu.CompilerParams(vmem_limit_bytes=8 * MIB),
    )(ids, *blocks)


def product_kernel(n_x, flip, n_chunks, spans, ids_ref, *refs):
    lefts, rights, out_ref = refs[: -1 - len(spans) * n_chunks], refs[-1 - len(spans) * n_chunks : -1], refs[-1]
    width = lefts[0].shape[1]
    rest = width // (CORES * n_x)
    core = lax.rem(ids_ref[0], CORES) ^ flip
    starts = [pl.multiple_of((CORES * x + core) * rest, rest) for x in range(n_x)]
    turned = []
    for i in range(0, len(lefts), n_chunks):
        parts = [[left[:, pl.ds(start, rest)] for start in starts] for left in lefts[i : i + n_chunks]]
        turned.append(jnp.concatenate([jnp.concatenate(p, axis=1) for p in parts], axis=0).T)
    at = 0
    for i, (which, start, size) in enumerate(spans):
        right = [ref[:, pl.ds(start, size)] for ref in rights[i * n_chunks : (i + 1) * n_chunks]]
        product = contract(turned[which], jnp.concatenate(right, axis=0), ((1,), (0,)))
        out_ref[:, :, :, :, pl.ds(at, size)] = product.reshape(out_ref.shape[:4] + (size,)).astype(jnp.bfloat16)
        at += size


def products(ids, flip, n_x, n_z, lefts, rights, spans):
    n_chunks = len(rights[0])
    rows, width = rights[0][0].shape
    rest = width // (CORES * n_x * n_z * N_Y)
    columns = sum(size for _, _, size in spans)
    operands = [a for factor in lefts + rights for a in factor]
    return pl.pallas_call(
        functools.partial(product_kernel, n_x, flip, n_chunks, spans),
        out_shape=jax.ShapeDtypeStruct((n_x, n_z, N_Y, rest, columns), jnp.bfloat16),
        in_specs=[pl.BlockSpec(memory_space=pltpu.SMEM)]
        + [pl.BlockSpec(memory_space=pltpu.VMEM)] * len(operands),
        out_specs=pl.BlockSpec(memory_space=pltpu.VMEM),
        compiler_params=pltpu.CompilerParams(vmem_limit_bytes=24 * MIB),
        cost_estimate=pl.CostEstimate(
            flops=n_chunks * rows * width * columns // 4,
            bytes_accessed=n_chunks * rows * width,
            transcendentals=0,
        ),
    )(ids, *operands)


def summed(refs, index):
    total = refs[0][index].astype(jnp.float32)
    for ref in refs[1:]:
        total += ref[index].astype(jnp.float32)
    return total


def halve_kernel(dim, axis, stride, ids_ref, *refs):
    addends, sent_ref, kept_ref = refs[:-2], refs[-2], refs[-1]
    me = lax.rem(lax.div(ids_ref[axis], stride), 2)
    for index in itertools.product(*(range(n) for n in sent_ref.shape[:-2])):
        sent_ref[index] = summed(addends, index[:dim] + (me ^ 1,) + index[dim:]).astype(jnp.bfloat16)
    for index in itertools.product(*(range(n) for n in sent_ref.shape[:-2])):
        kept_ref[index] = summed(addends, index[:dim] + (me,) + index[dim:])


def halve(ids, addends, dim, axis, stride):
    shape = addends[0].shape[:dim] + addends[0].shape[dim + 1 :]
    return pl.pallas_call(
        functools.partial(halve_kernel, dim, axis, stride),
        out_shape=[jax.ShapeDtypeStruct(shape, jnp.bfloat16), jax.ShapeDtypeStruct(shape, jnp.float32)],
        in_specs=[pl.BlockSpec(memory_space=pltpu.SMEM)]
        + [pl.BlockSpec(memory_space=pltpu.VMEM)] * len(addends),
        out_specs=[pl.BlockSpec(memory_space=pltpu.VMEM)] * 2,
        compiler_params=pltpu.CompilerParams(vmem_limit_bytes=16 * MIB),
    )(ids, *addends)


def join_kernel(n_z, n_first, ids_ref, *refs):
    addends, outs = refs[:-n_z], refs[-n_z:]
    me = lax.div(ids_ref[1], N_Y)
    cut = addends[0].shape[-1]
    for j in [*range(1, n_z), 0]:
        outs[j][:, :cut] = summed(addends[:n_first], (me ^ j,)).astype(outs[j].dtype)
        outs[j][:, cut:] = summed(addends[n_first:], (me ^ j,)).astype(outs[j].dtype)


def join(ids, first, second, n_z):
    shape = (first[0].shape[1], first[0].shape[2] + second[0].shape[2])
    own = jax.ShapeDtypeStruct(shape, jnp.float32)
    other = jax.ShapeDtypeStruct(shape, jnp.bfloat16)
    return pl.pallas_call(
        functools.partial(join_kernel, n_z, len(first)),
        out_shape=[own] + [other] * (n_z - 1),
        in_specs=[pl.BlockSpec(memory_space=pltpu.SMEM)]
        + [pl.BlockSpec(memory_space=pltpu.VMEM)] * (len(first) + len(second)),
        out_specs=[pl.BlockSpec(memory_space=pltpu.VMEM)] * n_z,
        compiler_params=pltpu.CompilerParams(vmem_limit_bytes=12 * MIB),
    )(ids, *first, *second)


def finish_kernel(*refs):
    addends, (grad_qkv_ref, grad_out_ref) = refs[:-2], refs[-2:]
    wide = grad_qkv_ref.shape[1]
    everything = slice(None)
    grad_qkv_ref[...] = summed(addends, (everything, pl.ds(0, wide)))
    grad_out_ref[...] = summed(addends, (everything, pl.ds(wide, grad_out_ref.shape[1])))


def finish(addends):
    rows, columns = addends[0].shape
    return pl.pallas_call(
        finish_kernel,
        out_shape=[
            jax.ShapeDtypeStruct((rows, columns // 4 * 3), jnp.float32),
            jax.ShapeDtypeStruct((rows, columns // 4), jnp.float32),
        ],
        in_specs=[pl.BlockSpec(memory_space=pltpu.VMEM)] * len(addends),
        out_specs=[pl.BlockSpec(memory_space=pltpu.VMEM)] * 2,
        compiler_params=pltpu.CompilerParams(vmem_limit_bytes=8 * MIB),
    )(*addends)


def raw_rows(pieces, at, n_clips):
    parts = []
    for clip in range(n_clips):
        parts += [p[0, clip if p.shape[1] == n_clips else at + clip] for p in pieces]
    return jnp.concatenate(parts, axis=0).astype(jnp.float32)


def sublayer_kernel(at, n_clips, n_positions, n_pieces, *refs):
    pieces, refs = refs[:n_pieces], refs[n_pieces:]
    w_qkv_ref, w_out_ref = refs[:2]
    normed_ref, cot_ref, mixed_ref, dq_ref, dk_ref, dv_ref = refs[2:]
    rows = normed_ref.shape[0] // n_clips
    span = rows // n_pieces
    width = w_out_ref.shape[0]
    wide = width // HEADS * GROUP
    depth = wide // GROUP
    scaling = depth**-0.5

    unit, _ = statistics(raw_rows(pieces, at, n_clips))
    normed_ref[...] = unit.astype(jnp.bfloat16)
    for clip in range(n_clips):
        for k, piece in enumerate(pieces):
            source = clip if piece.shape[1] == n_clips else at + clip
            cot_ref[pl.ds(clip * rows + k * span, span)] = piece[1, source]

    lane_head = lax.broadcasted_iota(jnp.int32, (rows, wide), 1) // depth
    head_masks = [(lane_head == h).astype(jnp.float32).astype(jnp.bfloat16) for h in range(GROUP)]
    key_pos = lax.broadcasted_iota(jnp.int32, (rows, rows), 0) % n_positions
    query_pos = lax.broadcasted_iota(jnp.int32, (rows, rows), 1) % n_positions
    same = (key_pos == query_pos)[None]

    def stacked(block):
        return jnp.concatenate([block * mask for mask in head_masks], axis=0)

    def side_by_side(blocks):
        return jnp.concatenate([blocks[h] for h in range(GROUP)], axis=1)

    for group in range(HEADS // GROUP):
        columns = slice(group * wide, (group + 1) * wide)
        all_queries, all_keys, all_values = (
            contract(normed_ref[...], w_qkv_ref[:, pl.ds(i * width + group * wide, wide)], ((1,), (0,))).astype(
                jnp.bfloat16
            )
            for i in range(3)
        )
        mixed_grad = contract(cot_ref[...], w_out_ref[columns, :], ((1,), (1,))).astype(jnp.bfloat16)
        for clip in range(n_clips):
            here = slice(clip * rows, (clip + 1) * rows)
            queries = all_queries[here]
            keys = stacked(all_keys[here])
            values = stacked(all_values[here])
            upstream = mixed_grad[here]
            scores = contract(keys, queries, ((1,), (1,))).reshape(GROUP, rows, rows)
            scores = jnp.where(same, scores, LOWEST)
            highest = jnp.max(scores, axis=1, keepdims=True)
            expo = jnp.exp2((scores - highest) * (scaling * LOG2E))
            full = expo * (1.0 / jnp.sum(expo, axis=1, keepdims=True))
            low = full.astype(jnp.bfloat16)
            dots = contract(values, upstream * jnp.bfloat16(scaling), ((1,), (1,)))
            dots = dots.reshape(GROUP, rows, rows)
            score_grad = full * (dots - jnp.sum(full * dots, axis=1, keepdims=True))
            score_grad = score_grad.astype(jnp.bfloat16)
            mixed = contract(low.reshape(GROUP * rows, rows), values, ((0,), (0,)))
            mixed_ref[here, columns] = mixed.astype(jnp.bfloat16)
            dq = contract(score_grad.reshape(GROUP * rows, rows), keys, ((0,), (0,)))
            dq_ref[here, columns] = dq.astype(jnp.bfloat16)
            dk = contract(side_by_side(score_grad), stacked(queries), ((1,), (0,)))
            dk_ref[here, columns] = dk.astype(jnp.bfloat16)
            dv = contract(side_by_side(low), stacked(upstream), ((1,), (0,)))
            dv_ref[here, columns] = dv.astype(jnp.bfloat16)


def sublayer(pieces, at, n_clips, w_qkv, w_out, n_positions):
    _, _, span, width = pieces[0].shape
    rows = n_clips * len(pieces) * span
    flat = jax.ShapeDtypeStruct((rows, width), jnp.bfloat16)
    operands = (*pieces, w_qkv, w_out)
    return pl.pallas_call(
        functools.partial(sublayer_kernel, at, n_clips, n_positions, len(pieces)),
        out_shape=[flat] * 6,
        in_specs=[pl.BlockSpec(memory_space=pltpu.VMEM)] * len(operands),
        out_specs=[pl.BlockSpec(memory_space=pltpu.VMEM)] * 6,
        compiler_params=pltpu.CompilerParams(vmem_limit_bytes=30 * MIB),
        cost_estimate=pl.CostEstimate(
            flops=2 * rows * width * (4 * width + 24 * 128),
            bytes_accessed=16 * rows * width + 8 * width * width,
            transcendentals=rows * 128 * HEADS,
        ),
    )(*operands)


def input_kernel(at, n_clips, n_pieces, n_before, *refs):
    pieces, refs = refs[:n_pieces], refs[n_pieces:]
    w_qkv_ref, cot_ref, dq_ref, dk_ref, dv_ref = refs[:5]
    before, dx_refs = refs[5 : 5 + n_before], refs[5 + n_before :]
    rows = cot_ref.shape[0] // n_clips
    span = rows // n_pieces
    grads = jnp.concatenate([dq_ref[...], dk_ref[...], dv_ref[...]], axis=1)
    total = contract(grads, w_qkv_ref[...], ((1,), (1,)))
    unit, inverse = statistics(raw_rows(pieces, at, n_clips))
    grad = inverse * (
        total
        - jnp.mean(total, axis=-1, keepdims=True)
        - unit * jnp.mean(total * unit, axis=-1, keepdims=True)
    )
    dx = (cot_ref[...].astype(jnp.float32) + grad).astype(jnp.bfloat16)
    for k in range(n_pieces):
        if before:
            dx_refs[k][:at] = before[k][...]
        for clip in range(n_clips):
            start = clip * rows + k * span
            dx_refs[k][at + clip] = dx[start : start + span]


def input_gradient(pieces, at, n_clips, w_qkv, cot, dq, dk, dv, before):
    _, _, span, width = pieces[0].shape
    dx = jax.ShapeDtypeStruct((at + n_clips, span, width), jnp.bfloat16)
    operands = (*pieces, w_qkv, cot, dq, dk, dv, *before)
    return pl.pallas_call(
        functools.partial(input_kernel, at, n_clips, len(pieces), len(before)),
        out_shape=[dx] * len(pieces),
        in_specs=[pl.BlockSpec(memory_space=pltpu.VMEM)] * len(operands),
        out_specs=[pl.BlockSpec(memory_space=pltpu.VMEM)] * len(pieces),
        compiler_params=pltpu.CompilerParams(vmem_limit_bytes=24 * MIB),
        cost_estimate=pl.CostEstimate(
            flops=6 * cot.shape[0] * width * width,
            bytes_accessed=8 * cot.shape[0] * width + 6 * width * width,
            transcendentals=0,
        ),
    )(*operands)


def swap(block, axis, size, distance):
    return lax.ppermute(block, axis, [(i, i ^ distance) for i in range(size)])


def after(values, done):
    values, _ = lax.optimization_barrier((values, done))
    return values


def inbound(near, far, ready, n_tm):
    half = n_tm // 2
    order, gates = list(range(1, n_tm)), {}
    if half == 4:
        order, gates = [3, 2, 5, 7, 1, 4, 6], {7: 5}
    near = list(near)
    blocks = near + list(far[0])
    for k in order:
        block = after(blocks[k], blocks[gates[k]]) if k in gates else blocks[k]
        blocks[k] = swap(block, "tm", n_tm, k)
    near, arrived = blocks[:half], [blocks[half:]]
    extra = {0: [ready], 3: [near[-1]]}
    for chunk in far[1:]:
        done = list(chunk)
        for i in (0, *reversed(range(1, half))):
            gate = (arrived[-1][i], extra.get(i, [near[1]]))
            done[i] = swap(after(chunk[i], gate), "tm", n_tm, half + i)
        arrived.append(done)
    return near, arrived


def shards(n_clip_devices, n_tm, clips, w_qkv, w_out, cotangent):
    n_clips, _, n_patches, width = clips.shape
    n_positions = n_patches // n_tm
    n_x, n_z = n_clip_devices // CORES, n_tm // N_Y
    joined = n_positions % 16 != 0
    ids = jnp.stack([lax.axis_index("clip"), lax.axis_index("tm")]).astype(jnp.int32)

    near, far = pick(ids, clips, cotangent, n_tm, CHUNKS)
    w_qkv = fetch(w_qkv)
    near, far = inbound(near, far, w_qkv, n_tm)
    depth = n_clips // CHUNKS
    factors, dx = [], []
    for chunk in range(CHUNKS):
        at = chunk * depth
        pieces = near + far[chunk]
        if joined:
            pieces = [p[:, at : at + depth] for p in near] + far[chunk]
            pieces = [jnp.stack(pieces, axis=2).reshape(2, depth, -1, width)]
        factors.append(sublayer(after(pieces, dx), at, depth, w_qkv, w_out, n_positions))
        later = (pieces, [w_qkv, *(factors[-1][i] for i in (1, 3, 4, 5))])
        if chunk < CHUNKS - 1:
            dx = input_gradient(pieces, at, depth, *later[1], dx)
    normed, cot, mixed, dq, dk, dv = zip(*factors)
    cut = int(4 * width * FIRST) - 2 * width
    first_parts = ([normed], [dq, dk, dv]), ((0, 0, width), (0, 0, width), (0, 0, cut))
    second_parts = ([normed, mixed], [dv, cot]), ((0, cut, width - cut), (1, 0, width))
    sent_first = products(ids, 1, n_x, n_z, *first_parts[0], first_parts[1])
    first = swap(sent_first, "clip", n_clip_devices, 1)
    sent_second = products(ids, 1, n_x, n_z, *after(second_parts[0], sent_first), second_parts[1])
    second = swap(sent_second, "clip", n_clip_devices, 1)
    own_first = products(ids, 0, n_x, n_z, *after(first_parts[0], sent_second), first_parts[1])
    sent, own_first = halve(ids, (own_first, first), 0, 0, CORES)
    first = swap(sent, "clip", n_clip_devices, CORES)
    own_second = products(ids, 0, n_x, n_z, *after(second_parts[0], own_first), second_parts[1])
    sent, own_second = halve(ids, (own_second, second), 2, 1, 1)
    second = swap(sent, "tm", n_tm, 1)
    pieces, operands = after(later, sent)
    dx = input_gradient(pieces, n_clips - depth, depth, *operands, dx)
    if joined:
        cut = dx[0].reshape(n_clips, n_tm, n_positions, width)
        dx = [cut[:, k] for k in range(n_tm)]
    late = (1, 3)
    back = {}
    for k in reversed([k for k in range(1, n_tm) if k not in late]):
        block = after(dx[k], back[k + 3]) if k + 3 in back else dx[k]
        back[k] = swap(block, "tm", n_tm, k)
    first, second = after((first, second), [back[k] for k in range(n_tm - 3, n_tm)])
    sent, own_first = halve(ids, (own_first, first), 1, 1, 1)
    first = swap(sent, "tm", n_tm, 1)
    sent, own_second = halve(ids, (own_second, second), 0, 0, CORES)
    second = swap(sent, "clip", n_clip_devices, CORES)
    first, second = after((first, second), back)
    total, *sent = join(ids, (own_first, first), (own_second, second), n_z)
    back[0] = dx[0]
    for k in late:
        back[k] = swap(after(dx[k], sent), "tm", n_tm, k)
    sent[0] = after(sent[0], back[1])
    others = [swap(sent[j - 1], "tm", n_tm, j * N_Y) for j in reversed(range(1, n_z))]
    grad_clips = place(ids, [back[k] for k in range(n_tm)]).reshape(clips.shape)
    grad_qkv, grad_out = finish((total, *others))
    return (grad_clips, grad_qkv, grad_out)


def solution(mesh):
    return jax.shard_map(
        functools.partial(shards, mesh.shape["clip"], mesh.shape["tm"]),
        mesh=mesh,
        in_specs=(P("clip", "tm", None, None), P(), P(), P("clip", "tm", None, None)),
        out_specs=(P("clip", "tm", None, None), P(("clip", "tm"), None), P(("clip", "tm"), None)),
        check_vma=False,
    )
```
